32 devices in a mesh: seq: 8 (over z, core), fsdp: 4 (over y, x).
Axes of the slice: x: 2, y: 2, z: 4, core: 2. Of those that a mesh axis runs over, the one named last changes fastest.
Arguments:
- inputs: bfloat16 [2, 2048, 2048], P(None, ('seq', 'fsdp')), may hold values from -6 to 6
- segments: int32 [2, 2048], replicated, may hold values from 0 to 1, as said below
- norm1_gain: float32 [2048], replicated, may hold values from 0.5 to 1.5
- norm1_bias: float32 [2048], replicated, may hold values from -1.75 to 1.75
- qkv_weight: bfloat16 [2048, 6144], P('fsdp'), may hold values from -0.125 to 0.125
- qkv_bias: float32 [6144], replicated, may hold values from -0.625 to 0.625
- out_weight: bfloat16 [2048, 2048], P('fsdp'), may hold values from -1 to 1
- norm2_gain: float32 [2048], replicated, may hold values from 0.5 to 1.5
- norm2_bias: float32 [2048], replicated, may hold values from -1.75 to 1.75
- gate_up_weight: bfloat16 [2048, 11264], P('fsdp'), may hold values from -0.125 to 0.125
- down_weight: bfloat16 [5632, 2048], P('fsdp'), may hold values from -0.078125 to 0.078125
- cotangent: bfloat16 [2, 2048, 2048], P(None, ('seq', 'fsdp')), may hold values from -6 to 6
Outputs:
- result: float32 [2, 2048, 2048], P(None, ('seq', 'fsdp'))
- inputs_grad: float32 [2, 2048, 2048], P(None, ('seq', 'fsdp'))
- norm1_gain_grad: float32 [2048], replicated
- norm1_bias_grad: float32 [2048], replicated
- qkv_weight_grad: float32 [2048, 6144], P('fsdp')
- qkv_bias_grad: float32 [6144], replicated
- out_weight_grad: float32 [2048, 2048], P('fsdp')
- norm2_gain_grad: float32 [2048], replicated
- norm2_bias_grad: float32 [2048], replicated
- gate_up_weight_grad: float32 [2048, 11264], P('fsdp')
- down_weight_grad: float32 [5632, 2048], P('fsdp')
The draws below stay inside these ranges and needn't reach their ends.
Inputs may be any that keep to these rules, and one draw needn't show every extreme that they name: `segments`: along each row the id is 0 and may change to 1 once, never back. One row, drawn from the seed, is all 0; in every other row the change comes at a position from 512 to 1536.
All inputs are finite; a program needn't handle non-finite values.
Results may differ from the reference program's by a relative error of at most 0.02.
Values may be sent and summed in bfloat16 or wider, within the bound.
No kernel may reach another device: no remote copies, remote signals or barrier semaphores. Data moves between devices by JAX's collectives and lax.ppermute only.
A program may use at most 640 MiB of HBM per device.

```python
from functools import partial
import jax
import jax.numpy as jnp
from jax import lax

D = 2048
HD = 64
ROT = 16
FF = 5632
ROWS = 2
ROW_LEN = 2048


def draw_segments(key, part):
    key = jax.random.fold_in(key, 7)
    whole_key, split_key = jax.random.split(key)
    whole_row = jax.random.randint(whole_key, (), 0, ROWS)
    split_at = jax.random.randint(split_key, (ROWS, 1), ROW_LEN // 4, ROW_LEN - ROW_LEN // 4 + 1)
    places = jnp.arange(ROW_LEN, dtype=jnp.int32)[None, :]
    row_ids = jnp.arange(ROWS, dtype=jnp.int32)[:, None]
    return ((places >= split_at) & (row_ids != whole_row)).astype(jnp.int32)


def block_scale(rng, dims, shards, smallest, top_value):
    factor_of = 1.0
    for position, blocks in shards:
        steps = jax.random.uniform(jax.random.fold_in(jax.random.fold_in(rng, 6), position), (blocks,), jnp.float32, smallest / len(shards), top_value / len(shards))
        factor_of = factor_of * jnp.repeat(jnp.exp(steps), dims[position] // blocks).reshape((-1,) + (1,) * (len(dims) - 1 - position))
    return factor_of


def gaussian(rng, dims, spread, reach, shards=(), held_as=jnp.bfloat16):
    entries = jax.random.normal(rng, dims, jnp.float32) * spread
    if len(shards) > 0:
        entries = block_scale(rng, dims, shards, -0.22, 0.18) * entries
    return jnp.clip(entries, min=-reach, max=reach).astype(held_as)


def setup_inputs(seed: int = 0) -> dict:
    splits = jax.random.split(jax.random.key(seed), 13)
    inputs = gaussian(splits[0], (ROWS, ROW_LEN, D), 1.0, 6.0, ((1, 32),))
    segments = draw_segments(jax.random.fold_in(splits[12], 71), 0)
    norm1_gain = jnp.clip(1.0 + 0.1 * jax.random.normal(splits[2], (D,), jnp.float32), 0.5, 1.5)
    norm1_bias = gaussian(splits[3], (D,), 0.3, 1.75, (), jnp.float32)
    qkv_weight = gaussian(splits[4], (D, 3 * D), D ** -0.5, 0.125, ((0, 4),))
    qkv_bias = gaussian(splits[5], (3 * D,), 0.1, 0.625, (), jnp.float32)
    out_weight = gaussian(splits[6], (D, D), (max(1, D * 32 // ROW_LEN)) ** -0.5, 1.0, ((0, 4),))
    norm2_gain = jnp.clip(1.0 + 0.1 * jax.random.normal(splits[7], (D,), jnp.float32), 0.5, 1.5)
    norm2_bias = gaussian(splits[8], (D,), 0.3, 1.75, (), jnp.float32)
    gate_up_weight = gaussian(splits[9], (D, 2 * FF), D ** -0.5, 0.125, ((0, 4),))
    down_weight = gaussian(splits[10], (FF, D), FF ** -0.5, 0.078125, ((0, 4),))
    cotangent = gaussian(splits[11], (ROWS, ROW_LEN, D), 1.0, 6.0, ((1, 32),))
    return {"inputs": inputs, "segments": segments, "norm1_gain": norm1_gain, "norm1_bias": norm1_bias, "qkv_weight": qkv_weight, "qkv_bias": qkv_bias, "out_weight": out_weight, "norm2_gain": norm2_gain, "norm2_bias": norm2_bias, "gate_up_weight": gate_up_weight, "down_weight": down_weight, "cotangent": cotangent}


EPSILON = 1e-05
MASKED = -1e+30
HIGH = lax.Precision.HIGHEST

@jax.custom_vjp
def low(v):
    return lax.optimization_barrier(v.astype(jnp.bfloat16)).astype(jnp.float32)

@jax.custom_vjp
def low_back(v):
    return v

def low_keep(v):
    return (low(v), None)

def low_pass(kept, grad):
    return (grad,)

def back_keep(v):
    return (v, None)

def back_low(kept, grad):
    return (low(grad),)
low.defvjp(low_keep, low_pass)
low_back.defvjp(back_keep, back_low)

def product(left, right_side):
    return jnp.dot(left, right_side, precision=HIGH, preferred_element_type=jnp.float32)

def layer_norm(values, norm_gain, offset):
    average = lax.optimization_barrier(jnp.mean(values, axis=-1, keepdims=True))
    centred = values - average
    variance = lax.optimization_barrier(jnp.mean(centred * centred, axis=-1, keepdims=True))
    return centred * lax.rsqrt(variance + EPSILON) * norm_gain + offset

def rotate(values, positions):
    half_rot = ROT // 2
    exponent = jnp.arange(half_rot, dtype=jnp.float32) * (2.0 / ROT)
    inverse = jnp.power(jnp.float32(10000.0), -exponent)
    angles = positions.astype(jnp.float32)[:, None] * inverse[None, :]
    cosine = jnp.cos(angles)[:, None, :]
    sine = jnp.sin(angles)[:, None, :]
    first = values[:, :, :half_rot]
    second = values[:, :, half_rot:ROT]
    return jnp.concatenate([first * cosine - second * sine, second * cosine + first * sine, values[:, :, ROT:]], axis=2)

def row_attention(row_items):
    queries, keys_all, values_all, segment_row = row_items
    row_len = queries.shape[0]
    span = min(256, row_len)
    scale_factor = HD ** (-0.5)
    key_pos = jnp.arange(row_len, dtype=jnp.int32)

    def attend_block(first_row):
        block_query = lax.dynamic_slice_in_dim(queries, first_row, span, 0)
        query_pos = first_row + jnp.arange(span, dtype=jnp.int32)
        query_seg = lax.dynamic_slice_in_dim(segment_row, first_row, span, 0)
        scores = low_back(jnp.einsum('qhd,khd->hqk', block_query, keys_all, precision=HIGH) * scale_factor)
        allowed = (query_seg[:, None] == segment_row[None, :]) & (key_pos[None, :] <= query_pos[:, None])
        scores = jnp.where(allowed[None], scores, MASKED)
        probs = low(jax.nn.softmax(scores, axis=-1))
        return jnp.einsum('hqk,khd->qhd', probs, values_all, precision=HIGH)
    starts = jnp.arange(row_len // span, dtype=jnp.int32) * span
    blocks = lax.map(jax.checkpoint(attend_block), starts)
    return blocks.reshape(row_len, queries.shape[1], queries.shape[2])

def forward(segments, inputs, norm1_gain, norm1_bias, qkv_weight, qkv_bias, out_weight, norm2_gain, norm2_bias, gate_up_weight, down_weight):
    row_count, row_len, features = inputs.shape
    head_count = features // HD
    token_count = row_count * row_len
    flat = inputs.reshape(token_count, features)
    normed_in = low(layer_norm(flat, norm1_gain, norm1_bias))
    mixed = low_back(product(normed_in, qkv_weight) + qkv_bias)
    positions = jnp.tile(jnp.arange(row_len, dtype=jnp.int32), row_count)
    turned = rotate(mixed[:, :2 * features].reshape(token_count, 2 * head_count, HD), positions)
    turned = low_back(low(turned))
    queries = turned[:, :head_count].reshape(row_count, row_len, head_count, HD)
    keys_all = turned[:, head_count:].reshape(row_count, row_len, head_count, HD)
    values_all = low_back(low(mixed[:, 2 * features:])).reshape(row_count, row_len, head_count, HD)
    attended = lax.map(row_attention, (queries, keys_all, values_all, segments))
    attended = low_back(low(attended.reshape(token_count, features)))
    middle = flat + low_back(product(attended, out_weight))
    normed_mid = low(layer_norm(middle, norm2_gain, norm2_bias))
    gate_up = low_back(product(normed_mid, gate_up_weight))
    ff_width = gate_up.shape[1] // 2
    act_value = low(jax.nn.silu(gate_up[:, :ff_width]) * gate_up[:, ff_width:])
    result = middle + product(act_value, down_weight)
    return result.reshape(row_count, row_len, features)

def reference(inputs, segments, norm1_gain, norm1_bias, qkv_weight, qkv_bias, out_weight, norm2_gain, norm2_bias, gate_up_weight, down_weight, cotangent):
    primals = (inputs.astype(jnp.float32), norm1_gain.astype(jnp.float32), norm1_bias.astype(jnp.float32), qkv_weight.astype(jnp.float32), qkv_bias.astype(jnp.float32), out_weight.astype(jnp.float32), norm2_gain.astype(jnp.float32), norm2_bias.astype(jnp.float32), gate_up_weight.astype(jnp.float32), down_weight.astype(jnp.float32))
    result, pullback = jax.vjp(partial(forward, segments), *primals)
    grads = pullback(cotangent.astype(jnp.float32))
    return (result, grads[0], grads[1], grads[2], grads[3], grads[4], grads[5], grads[6], grads[7], grads[8], grads[9])
```

```python
import jax
import jax.numpy as jnp
from jax import lax
from jax.experimental import pallas as pl
from jax.experimental.pallas import tpu as pltpu
from jax.sharding import PartitionSpec as P

HD = 64
ROT = 16


EPSILON = 1e-05
MASKED = -1e30


def layer_norm(values, norm_gain, offset):
    average = jnp.mean(values, axis=-1, keepdims=True)
    centred = values - average
    variance = jnp.mean(centred * centred, axis=-1, keepdims=True)
    return centred * lax.rsqrt(variance + EPSILON) * norm_gain + offset


def rotate(values, positions):
    half_rot = ROT // 2
    exponent = jnp.arange(half_rot, dtype=jnp.float32) * (2.0 / ROT)
    inverse = jnp.power(jnp.float32(10000.0), -exponent)
    angles = positions.astype(jnp.float32)[:, None] * inverse[None, :]
    cosine = jnp.cos(angles)[:, None, :]
    sine = jnp.sin(angles)[:, None, :]
    first = values[:, :, :half_rot]
    second = values[:, :, half_rot:ROT]
    return jnp.concatenate(
        [first * cosine - second * sine, second * cosine + first * sine, values[:, :, ROT:]], axis=2
    )


def fold_rows(left, shard):
    return jnp.dot(
        left, lax.all_gather(shard, "fsdp", axis=0, tiled=True), preferred_element_type=jnp.float32
    )


def map_back(grad_rows, shard):
    return lax.dot_general(
        grad_rows,
        lax.all_gather(shard, "fsdp", axis=0, tiled=True),
        (((1,), (1,)), ((), ())),
        preferred_element_type=jnp.float32,
    )


def grad_joint(left, right_side):
    seq_count = lax.axis_size("seq")
    fsdp_count = lax.axis_size("fsdp")
    token_count, total_rows = left.shape
    share = total_rows // (seq_count * fsdp_count)
    permuted = (
        left.reshape(token_count, fsdp_count, seq_count, share)
        .transpose(0, 2, 1, 3)
        .reshape(token_count, total_rows)
    )
    return lax.psum_scatter(
        lax.dot_general(
            permuted, right_side, (((0,), (0,)), ((), ())), preferred_element_type=jnp.float32
        ),
        ("seq", "fsdp"),
        scatter_dimension=0,
        tiled=True,
    )


def general_plan(
    inputs,
    segments,
    norm1_gain,
    norm1_bias,
    qkv_weight,
    qkv_bias,
    out_weight,
    norm2_gain,
    norm2_bias,
    gate_up_weight,
    down_weight,
    cotangent,
):
    row_count, local_len, features = inputs.shape
    fsdp_count = lax.axis_size("fsdp")
    fsdp_rank = lax.axis_index("fsdp")
    block_rank = lax.axis_index("seq") * fsdp_count + fsdp_rank
    token_count = row_count * local_len
    head_count = features // HD
    ff_width = gate_up_weight.shape[1] // 2
    scale_factor = HD ** (-0.5)
    flat = inputs.reshape(token_count, features).astype(jnp.float32)
    local_pos = block_rank * local_len + jnp.arange(local_len, dtype=jnp.int32)
    positions = jnp.tile(local_pos, row_count)
    weight_set = (qkv_weight, out_weight, gate_up_weight, down_weight)

    def forward_product(left, slot_index):
        return fold_rows(left, weight_set[slot_index])

    def backward_product(grad_rows, slot_index):
        return map_back(grad_rows, weight_set[slot_index])

    normed_in, norm1_back = jax.vjp(layer_norm, flat, norm1_gain, norm1_bias)
    in_low = normed_in.astype(jnp.bfloat16)
    mixed = forward_product(in_low, 0) + qkv_bias
    turn_input = mixed[:, : 2 * features].reshape(token_count, 2 * head_count, HD)
    turned, turn_back = jax.vjp(lambda values: rotate(values, positions), turn_input)
    turned_low = turned.astype(jnp.bfloat16)
    queries = turned_low[:, :head_count].reshape(row_count, local_len, features)
    keys_loc = turned_low[:, head_count:].reshape(row_count, local_len, features)
    values_loc = (
        mixed[:, 2 * features :].astype(jnp.bfloat16).reshape(row_count, local_len, features)
    )
    head_query, head_key, head_value = (
        lax.all_to_all(queries, "seq", split_axis=2, concat_axis=1, tiled=True),
        lax.all_to_all(keys_loc, "seq", split_axis=2, concat_axis=1, tiled=True),
        lax.all_to_all(values_loc, "seq", split_axis=2, concat_axis=1, tiled=True),
    )
    all_keys, all_values = (
        lax.all_gather(head_key, "fsdp", axis=1, tiled=True),
        lax.all_gather(head_value, "fsdp", axis=1, tiled=True),
    )
    query_len = head_query.shape[1]
    key_len = all_keys.shape[1]
    head_width = head_query.shape[2]
    local_heads = head_width // HD
    query_four = head_query.reshape(row_count, query_len, local_heads, HD)
    keys_four = all_keys.reshape(row_count, key_len, local_heads, HD)
    values_four = all_values.reshape(row_count, key_len, local_heads, HD)
    query_index = jnp.arange(query_len, dtype=jnp.int32)
    query_pos = (
        query_index // local_len * fsdp_count + fsdp_rank
    ) * local_len + query_index % local_len
    key_index = jnp.arange(key_len, dtype=jnp.int32)
    key_pos = (
        key_index % query_len // local_len * fsdp_count + key_index // query_len
    ) * local_len + key_index % local_len
    query_seg = jnp.take(segments, query_pos, axis=1)
    key_seg = jnp.take(segments, key_pos, axis=1)
    span = min(512, key_len)
    block_count = key_len // span

    def block_inputs(block_index):
        first_row = block_index * span
        block_keys = lax.dynamic_slice_in_dim(keys_four, first_row, span, 1)
        block_values = lax.dynamic_slice_in_dim(values_four, first_row, span, 1)
        block_pos = lax.dynamic_slice_in_dim(key_pos, first_row, span, 0)
        block_seg = lax.dynamic_slice_in_dim(key_seg, first_row, span, 1)
        allowed = (query_seg[:, :, None] == block_seg[:, None, :]) & (
            block_pos[None, None, :] <= query_pos[None, :, None]
        )
        scores = (
            jnp.einsum(
                "rqhd,rkhd->rhqk", query_four, block_keys, preferred_element_type=jnp.float32
            )
            * scale_factor
        )
        return (first_row, block_keys, block_values, allowed[:, None], scores)

    def forward_block(carry, block_index):
        row_top, running, weighted = carry
        first_row, block_keys, block_values, allowed, scores = block_inputs(block_index)
        new_top = jnp.maximum(row_top, jnp.max(jnp.where(allowed, scores, MASKED), axis=-1))
        probs = jnp.where(allowed, jnp.exp(scores - new_top[..., None]), 0.0)
        factor = jnp.exp(row_top - new_top)
        running = running * factor + jnp.sum(probs, axis=-1)
        weighted = weighted * factor[..., None] + jnp.einsum(
            "rhqk,rkhd->rhqd",
            probs.astype(jnp.bfloat16),
            block_values,
            preferred_element_type=jnp.float32,
        )
        return ((new_top, running, weighted), None)

    start_top = jnp.full((row_count, local_heads, query_len), MASKED, jnp.float32)
    start_total = jnp.zeros((row_count, local_heads, query_len), jnp.float32)
    start_weighted = jnp.zeros((row_count, local_heads, query_len, HD), jnp.float32)
    (row_top, running, weighted), _ = lax.scan(
        forward_block, (start_top, start_total, start_weighted), jnp.arange(block_count)
    )
    log_total = row_top + jnp.log(running)
    attended_heads = (
        (weighted / running[..., None])
        .transpose(0, 2, 1, 3)
        .reshape(row_count, query_len, head_width)
        .astype(jnp.bfloat16)
    )
    attended_loc = lax.all_to_all(attended_heads, "seq", split_axis=1, concat_axis=2, tiled=True)
    att_flat = attended_loc.reshape(token_count, features)
    middle = flat + forward_product(att_flat, 1)
    normed_mid, norm2_back = jax.vjp(layer_norm, middle, norm2_gain, norm2_bias)
    mid_low = normed_mid.astype(jnp.bfloat16)
    gate_up = forward_product(mid_low, 2)
    act_value, silu_back = jax.vjp(
        lambda gate_part, up_part: jax.nn.silu(gate_part) * up_part,
        gate_up[:, :ff_width],
        gate_up[:, ff_width:],
    )
    act_low = act_value.astype(jnp.bfloat16)
    result = middle + forward_product(act_low, 3)
    d_out = cotangent.reshape(token_count, features)
    d_act = backward_product(d_out, 3)
    d_gate, d_up = silu_back(d_act)
    d_gate_up = jnp.concatenate([d_gate, d_up], axis=1).astype(jnp.bfloat16)
    d_mid_norm = backward_product(d_gate_up, 2)
    d_middle_part, d_gain_two, d_bias_two = norm2_back(d_mid_norm)
    d_middle = d_out.astype(jnp.float32) + d_middle_part
    d_branch = d_middle.astype(jnp.bfloat16)
    d_attended = (
        backward_product(d_branch, 1).astype(jnp.bfloat16).reshape(row_count, local_len, features)
    )
    d_heads = lax.all_to_all(d_attended, "seq", split_axis=2, concat_axis=1, tiled=True)
    d_heads_four = d_heads.reshape(row_count, query_len, local_heads, HD)
    attended_four = attended_heads.reshape(row_count, query_len, local_heads, HD)
    delta = jnp.einsum(
        "rqhd,rqhd->rhq", d_heads_four.astype(jnp.float32), attended_four.astype(jnp.float32)
    )

    def backward_block(carry, block_index):
        d_query, d_keys_all, d_values_all = carry
        first_row, block_keys, block_values, allowed, scores = block_inputs(block_index)
        probs = jnp.where(allowed, jnp.exp(scores - log_total[..., None]), 0.0)
        d_block_values = jnp.einsum(
            "rhqk,rqhd->rkhd",
            probs.astype(jnp.bfloat16),
            d_heads_four,
            preferred_element_type=jnp.float32,
        )
        d_probs = jnp.einsum(
            "rqhd,rkhd->rhqk", d_heads_four, block_values, preferred_element_type=jnp.float32
        )
        d_scores = (probs * (d_probs - delta[..., None])).astype(jnp.bfloat16)
        d_query = (
            d_query
            + jnp.einsum(
                "rhqk,rkhd->rqhd", d_scores, block_keys, preferred_element_type=jnp.float32
            )
            * scale_factor
        )
        d_block_keys = (
            jnp.einsum("rhqk,rqhd->rkhd", d_scores, query_four, preferred_element_type=jnp.float32)
            * scale_factor
        )
        d_keys_all = lax.dynamic_update_slice_in_dim(d_keys_all, d_block_keys, first_row, 1)
        d_values_all = lax.dynamic_update_slice_in_dim(d_values_all, d_block_values, first_row, 1)
        return ((d_query, d_keys_all, d_values_all), None)

    zero_query = jnp.zeros((row_count, query_len, local_heads, HD), jnp.float32)
    zero_keys = jnp.zeros((row_count, key_len, local_heads, HD), jnp.float32)
    (d_query, d_keys_all, d_values_all), _ = lax.scan(
        backward_block, (zero_query, zero_keys, zero_keys), jnp.arange(block_count)
    )
    d_keys_sum, d_values_sum = (
        lax.psum_scatter(
            d_keys_all.reshape(row_count, key_len, head_width).astype(jnp.bfloat16),
            "fsdp",
            scatter_dimension=1,
            tiled=True,
        ).astype(jnp.float32),
        lax.psum_scatter(
            d_values_all.reshape(row_count, key_len, head_width).astype(jnp.bfloat16),
            "fsdp",
            scatter_dimension=1,
            tiled=True,
        ).astype(jnp.float32),
    )
    d_query_low = d_query.reshape(row_count, query_len, head_width).astype(jnp.bfloat16)
    dq_back, dk_back, dv_back = (
        lax.all_to_all(d_query_low, "seq", split_axis=1, concat_axis=2, tiled=True),
        lax.all_to_all(
            d_keys_sum.astype(jnp.bfloat16), "seq", split_axis=1, concat_axis=2, tiled=True
        ),
        lax.all_to_all(
            d_values_sum.astype(jnp.bfloat16), "seq", split_axis=1, concat_axis=2, tiled=True
        ),
    )
    d_turned = jnp.concatenate(
        [
            dq_back.reshape(token_count, head_count, HD),
            dk_back.reshape(token_count, head_count, HD),
        ],
        axis=1,
    ).astype(jnp.float32)
    (d_turn_input,) = turn_back(d_turned)
    d_mixed = jnp.concatenate(
        [
            d_turn_input.reshape(token_count, 2 * features),
            dv_back.reshape(token_count, features).astype(jnp.float32),
        ],
        axis=1,
    ).astype(jnp.bfloat16)
    d_qkv_bias = jnp.sum(d_mixed.astype(jnp.float32), axis=0)
    d_norm_in = backward_product(d_mixed, 0)
    d_flat_part, d_gain_one, d_bias_one = norm1_back(d_norm_in)
    d_inputs = d_middle + d_flat_part
    first_grad = grad_joint(in_low, d_mixed)
    second_grad = grad_joint(att_flat, d_branch)
    third_grad = grad_joint(mid_low, d_gate_up)
    fourth_grad = grad_joint(act_low, d_out)
    qkv_grad, out_grad, gate_up_grad, down_grad = (
        lax.all_gather(first_grad.astype(jnp.bfloat16), "seq", axis=0, tiled=True).astype(
            first_grad.dtype
        ),
        lax.all_gather(second_grad.astype(jnp.bfloat16), "seq", axis=0, tiled=True).astype(
            second_grad.dtype
        ),
        lax.all_gather(third_grad.astype(jnp.bfloat16), "seq", axis=0, tiled=True).astype(
            third_grad.dtype
        ),
        lax.all_gather(fourth_grad.astype(jnp.bfloat16), "seq", axis=0, tiled=True).astype(
            fourth_grad.dtype
        ),
    )
    gain_one, bias_one, bias_qkv, gain_two, bias_two = lax.psum(
        (d_gain_one, d_bias_one, d_qkv_bias, d_gain_two, d_bias_two), ("seq", "fsdp")
    )
    return (
        result.reshape(row_count, local_len, features),
        d_inputs.reshape(row_count, local_len, features),
        gain_one,
        bias_one,
        qkv_grad,
        bias_qkv,
        out_grad,
        gain_two,
        bias_two,
        gate_up_grad,
        down_grad,
    )


BLOCK = 512
BF = jnp.bfloat16
F32 = jnp.float32


def swap(value, mask):
    return lax.ppermute(value, ("seq", "fsdp"), [(i, i ^ mask) for i in range(32)])


def shift(value, steps):
    return lax.ppermute(value, ("seq", "fsdp"), [(i, (i + 8 * steps) % 32) for i in range(32)])


def pick(stacked, index):
    return lax.dynamic_index_in_dim(stacked, index, 0, keepdims=False)


def unswap(pieces, rank):
    stacked = jnp.stack(pieces) if isinstance(pieces, (list, tuple)) else pieces
    return jnp.stack([pick(stacked, j ^ rank) for j in range(stacked.shape[0])])


def gather_quad(value):
    half = value.shape[0] // 2
    by_x = swap(value, 1)
    by_y = swap(value, 2)
    low_part = swap(by_x[:half], 2)
    high_part = swap(by_y[half:], 1)
    return jnp.concatenate([value, by_x, by_y, low_part, high_part], axis=0)


def gather_plane(value):
    quad = gather_quad(value)
    return quad, swap(quad, 4)


def sum_quad(blocks):
    return (
        blocks[0].astype(F32)
        + swap(blocks[1].astype(BF), 1).astype(F32)
        + swap(blocks[2].astype(BF), 2).astype(F32)
        + swap(blocks[3].astype(BF), 3).astype(F32)
    )


def sum_plane(near, far):
    arrived = swap(far.astype(BF), 4).astype(F32)
    total = near.astype(F32) + arrived
    return sum_quad([total[m] for m in range(4)])


def sum_all(value):
    for mask in (4, 1, 2, 8, 16):
        value = value + swap(value, mask)
    return value


def dot(left, right):
    return jnp.dot(left, right, preferred_element_type=F32)


def dot_rows(left, right):
    return lax.dot_general(left, right, (((1,), (1,)), ((), ())), preferred_element_type=F32)


def dot_cols(left, right):
    return lax.dot_general(left, right, (((0,), (0,)), ((), ())), preferred_element_type=F32)


def turn_tables(row_len):
    half_rot = ROT // 2
    lane = jnp.arange(2 * HD, dtype=jnp.int32) % HD
    exponent = (lane % half_rot).astype(F32) * (2.0 / ROT)
    inverse = jnp.power(jnp.float32(10000.0), -exponent)
    angles = jnp.arange(row_len, dtype=jnp.int32).astype(F32)[:, None] * inverse[None, :]
    cosine = jnp.where(lane < ROT, jnp.cos(angles), 1.0)
    sine = jnp.sin(angles)
    ahead = jnp.where(lane < half_rot, -sine, 0.0)
    behind = jnp.where((lane >= half_rot) & (lane < ROT), sine, 0.0)
    return cosine, ahead, behind


def attend_kernel(
    place_ref, split_ref, mixed_ref, cos_ref, ahead_ref, behind_ref,
    q_ref, k_ref, v_ref, o_ref, log_ref, kz, vz,
):
    local_len = mixed_ref.shape[2]
    row_len = q_ref.shape[0]
    low = lax.broadcasted_iota(jnp.int32, (local_len, 2 * HD), 1) < HD

    def prepare(i, carry):
        rows = pl.ds(pl.multiple_of(i * local_len, local_len), local_len)
        source = place_ref[i]
        cosine, ahead, behind = cos_ref[rows], ahead_ref[rows], behind_ref[rows]

        def turn(x):
            return (
                x * cosine
                + pltpu.roll(x, 2 * HD - ROT // 2, 1) * ahead
                + pltpu.roll(x, ROT // 2, 1) * behind
            )

        first = mixed_ref[source, 0]
        second = mixed_ref[source, 1]
        turned0 = turn(first[:, : 2 * HD])
        turned1 = turn(second[:, : 2 * HD])
        q = jnp.where(low, turned0, pltpu.roll(turned1, HD, 1))
        k = jnp.where(low, pltpu.roll(turned0, HD, 1), turned1)
        v = jnp.where(low, first[:, 2 * HD :], second[:, 2 * HD :])
        q_ref[rows] = (q * HD**-0.5).astype(BF)
        k_ref[rows] = k.astype(BF)
        v_ref[rows] = v.astype(BF)
        kz[0, rows] = jnp.where(low, k, 0.0).astype(BF)
        kz[1, rows] = jnp.where(low, 0.0, k).astype(BF)
        vz[0, rows] = jnp.where(low, v, 0.0).astype(BF)
        vz[1, rows] = jnp.where(low, 0.0, v).astype(BF)
        return carry

    lax.fori_loop(0, row_len // local_len, prepare, 0)
    t_in = lax.broadcasted_iota(jnp.int32, (BLOCK, 1), 0)
    u_in = lax.broadcasted_iota(jnp.int32, (1, BLOCK), 1)
    low_q = lax.broadcasted_iota(jnp.int32, (BLOCK, 2 * HD), 1) < HD

    def query_block(qb, carry):
        rows = pl.ds(pl.multiple_of(qb * BLOCK, BLOCK), BLOCK)
        q = q_ref[rows]
        t = t_in + qb * BLOCK
        outs, logs = [], []
        for row in range(2):
            split = split_ref[row]
            start = jnp.where(t >= split, split, 0)

            def step(kb, state, diagonal, row=row, start=start):
                top, total, acc = state
                keys = pl.ds(pl.multiple_of(kb * BLOCK, BLOCK), BLOCK)
                u = u_in + kb * BLOCK
                scores = dot_rows(q, kz[row, keys])
                allowed = u >= start
                if diagonal:
                    allowed = allowed & (u <= t)
                scores = jnp.where(allowed, scores, MASKED)
                new_top = jnp.maximum(top, jnp.max(scores, axis=1, keepdims=True))
                probs = jnp.exp(scores - new_top)
                factor = jnp.exp(top - new_top)
                total = total * factor + jnp.sum(probs, axis=1, keepdims=True)
                acc = acc * factor + dot(probs.astype(BF), vz[row, keys])
                return new_top, total, acc

            state = (
                jnp.full((BLOCK, 1), MASKED, F32),
                jnp.zeros((BLOCK, 1), F32),
                jnp.zeros((BLOCK, 2 * HD), F32),
            )
            first_kb = jnp.where(qb * BLOCK >= split, split // BLOCK, 0)
            state = lax.fori_loop(
                first_kb, qb, lambda kb, state, step=step: step(kb, state, False), state
            )
            top, total, acc = step(qb, state, True)
            outs.append(acc / total)
            logs.append(top + jnp.log(total))
        o_ref[rows] = (outs[0] + outs[1]).astype(BF)
        log_ref[rows] = jnp.where(low_q, logs[0], logs[1])
        return carry

    lax.fori_loop(0, row_len // BLOCK, query_block, 0)


def attend(place, split, mixed, tables):
    row_len = tables[0].shape[0]
    packed = jax.ShapeDtypeStruct((row_len, 2 * HD), BF)
    smem = pl.BlockSpec(memory_space=pltpu.SMEM)
    vmem = pl.BlockSpec(memory_space=pltpu.VMEM)
    pairs = 2 * row_len * row_len // 2
    return pl.pallas_call(
        attend_kernel,
        out_shape=(packed, packed, packed, packed, jax.ShapeDtypeStruct((row_len, 2 * HD), F32)),
        in_specs=[smem, smem, vmem, vmem, vmem, vmem],
        out_specs=(vmem,) * 5,
        scratch_shapes=[pltpu.VMEM((2, row_len, 2 * HD), BF), pltpu.VMEM((2, row_len, 2 * HD), BF)],
        compiler_params=pltpu.CompilerParams(vmem_limit_bytes=48 * 2**20),
        cost_estimate=pl.CostEstimate(
            flops=16 * pairs * HD, bytes_accessed=12 * 2**20, transcendentals=pairs
        ),
        name="attend",
    )(place, split, mixed, *tables)


def attend_back_kernel(
    place_ref, split_ref, q_ref, k_ref, v_ref, kt_ref, o_ref, do_ref, log_ref,
    cos_ref, ahead_ref, behind_ref,
    dmix_ref, dpos_ref, kz, vz, qz, dz, ktz, delta, dq_t, dk, dv,
):
    row_len = q_ref.shape[0]
    local_len = dmix_ref.shape[2]
    low = lax.broadcasted_iota(jnp.int32, (BLOCK, 2 * HD), 1) < HD
    low_t = lax.broadcasted_iota(jnp.int32, (2 * HD, BLOCK), 0) < HD
    lane = lax.broadcasted_iota(jnp.int32, (8, 2 * HD), 1)
    ones = [jnp.where(lane < HD, 1.0, 0.0).astype(BF), jnp.where(lane < HD, 0.0, 1.0).astype(BF)]

    def prepare(b, carry):
        rows = pl.ds(pl.multiple_of(b * BLOCK, BLOCK), BLOCK)
        zero = jnp.zeros((BLOCK, 2 * HD), F32)
        for ref, out in ((k_ref, kz), (v_ref, vz), (q_ref, qz), (do_ref, dz)):
            value = ref[rows].astype(F32)
            out[0, rows] = jnp.where(low, value, zero).astype(BF)
            out[1, rows] = jnp.where(low, zero, value).astype(BF)
        value = kt_ref[:, rows].astype(F32)
        ktz[0, :, rows] = jnp.where(low_t, value, 0.0).astype(BF)
        ktz[1, :, rows] = jnp.where(low_t, 0.0, value).astype(BF)
        product = do_ref[rows].astype(F32) * o_ref[rows].astype(F32)
        coarse = product.astype(BF)
        fine = (product - coarse.astype(F32)).astype(BF)
        for row in range(2):
            delta[row, :, rows] = dot_rows(ones[row], coarse) + dot_rows(ones[row], fine)
        dq_t[:, rows] = jnp.zeros((2 * HD, BLOCK), F32)
        return carry

    lax.fori_loop(0, row_len // BLOCK, prepare, 0)
    u_in = lax.broadcasted_iota(jnp.int32, (BLOCK, 1), 0)
    t_in = lax.broadcasted_iota(jnp.int32, (1, BLOCK), 1)

    def key_block(kb, carry):
        keys = pl.ds(pl.multiple_of(kb * BLOCK, BLOCK), BLOCK)
        u = u_in + kb * BLOCK
        sums_k, sums_v = [], []
        for row in range(2):
            split = split_ref[row]
            k_row = kz[row, keys]
            v_row = vz[row, keys]
            kt_row = ktz[row, :, keys]

            def step(qb, state, row=row, split=split, k_row=k_row, v_row=v_row, kt_row=kt_row):
                d_keys, d_values = state
                rows = pl.ds(pl.multiple_of(qb * BLOCK, BLOCK), BLOCK)
                t = t_in + qb * BLOCK
                start = jnp.where(t >= split, split, 0)
                allowed = (u >= start) & (u <= t)
                scores = dot_rows(k_row, q_ref[rows])
                probs = jnp.where(allowed, jnp.exp(scores - log_ref[pl.ds(row, 1), rows]), 0.0)
                d_probs = dot_rows(v_row, do_ref[rows])
                d_scores = (probs * (d_probs - delta[row, pl.ds(0, 1), rows])).astype(BF)
                d_values = d_values + dot(probs.astype(BF), dz[row, rows])
                d_keys = d_keys + dot(d_scores, qz[row, rows])
                dq_t[:, rows] += dot(kt_row, d_scores)
                return d_keys, d_values

            zero = jnp.zeros((BLOCK, 2 * HD), F32)
            last = jnp.where(
                (kb + 1) * BLOCK <= split, (split + BLOCK - 1) // BLOCK, row_len // BLOCK
            )
            d_keys, d_values = lax.fori_loop(kb, last, step, (zero, zero))
            sums_k.append(d_keys)
            sums_v.append(d_values)
        dk[keys] = sums_k[0] + sums_k[1]
        dv[keys] = sums_v[0] + sums_v[1]
        return carry

    lax.fori_loop(0, row_len // BLOCK, key_block, 0)
    low_l = lax.broadcasted_iota(jnp.int32, (local_len, 2 * HD), 1) < HD
    per = 2 * HD // local_len

    def finish(b, carry):
        both = pl.ds(pl.multiple_of(b * 2 * HD, 2 * HD), 2 * HD)
        dq = dq_t[:, both].T * HD**-0.5
        for part in range(per):
            i = b * per + part
            rows = pl.ds(pl.multiple_of(i * local_len, local_len), local_len)
            target = place_ref[i]
            cosine, ahead, behind = cos_ref[rows], ahead_ref[rows], behind_ref[rows]

            def turn(x, cosine=cosine, ahead=ahead, behind=behind):
                return (
                    x * cosine
                    - pltpu.roll(x, 2 * HD - ROT // 2, 1) * ahead
                    - pltpu.roll(x, ROT // 2, 1) * behind
                )

            q_part = turn(dq[part * local_len : (part + 1) * local_len])
            k_part = turn(dk[rows])
            v_part = dv[rows]
            first = jnp.where(low_l, q_part, pltpu.roll(k_part, HD, 1)).astype(BF)
            second = jnp.where(low_l, pltpu.roll(q_part, HD, 1), k_part).astype(BF)
            dpos_ref[rows, : 2 * HD] = first
            dpos_ref[rows, 2 * HD : 4 * HD] = second
            dpos_ref[rows, 4 * HD :] = v_part.astype(BF)
            dmix_ref[target, 0, :, : 2 * HD] = first
            dmix_ref[target, 1, :, : 2 * HD] = second
            dmix_ref[target, 0, :, 2 * HD :] = jnp.where(low_l, v_part, 0.0).astype(BF)
            dmix_ref[target, 1, :, 2 * HD :] = jnp.where(
                low_l, pltpu.roll(v_part, HD, 1), 0.0
            ).astype(BF)
        return carry

    lax.fori_loop(0, row_len // (2 * HD), finish, 0)


def attend_back(place, split, q, k, v, k_t, out, d_out, logs, tables, local_len):
    row_len = q.shape[0]
    smem = pl.BlockSpec(memory_space=pltpu.SMEM)
    vmem = pl.BlockSpec(memory_space=pltpu.VMEM)
    masked = pltpu.VMEM((2, row_len, 2 * HD), BF)
    whole = pltpu.VMEM((row_len, 2 * HD), F32)
    pairs = 2 * row_len * row_len // 2
    return pl.pallas_call(
        attend_back_kernel,
        out_shape=(
            jax.ShapeDtypeStruct((row_len // local_len, 2, local_len, 4 * HD), BF),
            jax.ShapeDtypeStruct((row_len, 6 * HD), BF),
        ),
        in_specs=[smem, smem] + [vmem] * 10,
        out_specs=(vmem, vmem),
        scratch_shapes=[
            masked, masked, masked, masked,
            pltpu.VMEM((2, 2 * HD, row_len), BF),
            pltpu.VMEM((2, 8, row_len), F32),
            pltpu.VMEM((2 * HD, row_len), F32),
            whole, whole,
        ],
        compiler_params=pltpu.CompilerParams(vmem_limit_bytes=48 * 2**20),
        cost_estimate=pl.CostEstimate(
            flops=40 * pairs * HD, bytes_accessed=12 * 2**20, transcendentals=pairs
        ),
        name="attend_back",
    )(place, split, q, k, v, k_t, out, d_out, logs, *tables)


def hidden_layer(mid, d_result, gate_up_pad, down_pad):
    width = down_pad.shape[0]
    gate_up = dot(mid, gate_up_pad)
    gate, up = gate_up[:, :width], gate_up[:, width:]
    sig = jax.nn.sigmoid(gate)
    silu = gate * sig
    act = (silu * up).astype(BF)
    d_act = dot_rows(d_result, down_pad)
    d_gate = d_act * up * (sig + silu * (1.0 - sig))
    d_gate_up = jnp.concatenate([d_gate.astype(BF), (d_act * silu).astype(BF)], axis=1)
    return act, d_gate_up


def plane_plan(
    inputs,
    segments,
    norm1_gain,
    norm1_bias,
    qkv_weight,
    qkv_bias,
    out_weight,
    norm2_gain,
    norm2_bias,
    gate_up_weight,
    down_weight,
    cotangent,
):
    row_count, local_len, features = inputs.shape
    row_len = segments.shape[1]
    tokens = row_count * local_len
    seq = lax.axis_index("seq")
    rank = lax.axis_index("fsdp")
    core = seq % 2
    plane = seq // 2
    own = core * 4 + rank
    shard = features // 4
    hidden = gate_up_weight.shape[1] // 2
    share = hidden // 8
    padded = -(-share // 128) * 128
    tables = turn_tables(row_len)
    split = jnp.sum((segments == 0).astype(jnp.int32), axis=1)
    canon = jnp.arange(32, dtype=jnp.int32)
    place = ((plane - canon // 8) % 4) * 8 + ((canon % 8) ^ own)

    def head_columns(m):
        first = ((rank ^ m) * 8 + seq) * HD
        parts = [
            lax.dynamic_slice_in_dim(qkv_weight, first + part * features, HD, 1) for part in (0, 1, 2)
        ]
        return jnp.concatenate(parts + parts[2:], axis=1)

    head_weight = unswap(
        [head_columns(0)] + [swap(head_columns(m), m) for m in (1, 2, 3)], rank
    ).reshape(features, 4 * HD)
    head_first = (rank * 8 + seq) * HD
    bias_parts = [
        lax.dynamic_slice_in_dim(qkv_bias, head_first + part * features, HD, 0) for part in (0, 1, 2)
    ]
    head_bias = jnp.concatenate(bias_parts + bias_parts[2:])

    flat = inputs.reshape(tokens, features).astype(F32)
    normed_in, norm1_back = jax.vjp(layer_norm, flat, norm1_gain, norm1_bias)
    chunk = normed_in.astype(BF)
    in_halves = []
    for k in range(4):
        in_halves += list(gather_plane(chunk))
        if k < 3:
            chunk = shift(chunk, 1)
    mixed = jnp.concatenate([dot(half, head_weight) + head_bias for half in in_halves], axis=0)
    q, k, v, out_heads, logs = attend(
        place, split, mixed.reshape(row_len // local_len, row_count, local_len, 4 * HD), tables
    )

    span = row_len // 8
    sent = [lax.dynamic_slice_in_dim(out_heads, (seq ^ m) * span, span, 0) for m in range(8)]
    arrived = [sent[0]] + [swap(sent[m], m * 4) for m in range(1, 8)]
    att = (
        unswap(arrived, seq)
        .reshape(8, span, row_count, HD)
        .transpose(2, 1, 0, 3)
        .reshape(row_count, 4, local_len, shard)
    )
    branch = dot(att.reshape(row_count * span, shard), out_weight).reshape(
        row_count, 4, local_len, features
    )
    branch = branch.transpose(1, 0, 2, 3)
    middle = flat + sum_quad([pick(branch, rank ^ m).reshape(tokens, features) for m in range(4)])
    normed_mid, norm2_back = jax.vjp(layer_norm, middle, norm2_gain, norm2_bias)
    mid_low = normed_mid.astype(BF)
    mid_near, mid_far = gather_plane(mid_low)

    def hidden_columns(m):
        first = (rank ^ m) * 2 * share + core * share
        return jnp.concatenate(
            [
                lax.dynamic_slice_in_dim(gate_up_weight, first, share, 1),
                lax.dynamic_slice_in_dim(gate_up_weight, first + hidden, share, 1),
            ],
            axis=1,
        )

    gate_up_cols = unswap(
        [hidden_columns(0)] + [swap(hidden_columns(m), m) for m in (1, 2, 3)], rank
    ).reshape(features, 2, share)
    gate_up_pad = jnp.pad(gate_up_cols, ((0, 0), (0, 0), (0, padded - share))).reshape(
        features, 2 * padded
    )
    down_pad = jnp.pad(
        lax.dynamic_slice_in_dim(down_weight, core * share, share, 0),
        ((0, padded - share), (0, 0)),
    )
    d_out = cotangent.reshape(tokens, features)
    out_near, out_far = gather_plane(d_out)

    act_far, d_gu_far = hidden_layer(mid_far, out_far, gate_up_pad, down_pad)
    act_near, d_gu_near = hidden_layer(mid_near, out_near, gate_up_pad, down_pad)
    blocks = (4, tokens, features)
    d_norm_mid = sum_plane(
        dot_rows(d_gu_near, gate_up_pad).reshape(blocks),
        dot_rows(d_gu_far, gate_up_pad).reshape(blocks),
    )
    d_middle_part, d_gain_two, d_bias_two = norm2_back(d_norm_mid)
    d_middle = d_out.astype(F32) + d_middle_part
    d_branch = gather_quad(d_middle.astype(BF))
    result = middle + sum_plane(
        dot(act_near, down_pad).reshape(blocks), dot(act_far, down_pad).reshape(blocks)
    )

    d_att = dot_rows(d_branch, out_weight).astype(BF)
    d_att = unswap(d_att.reshape(4, row_count, local_len, 8, HD), rank)
    d_att = d_att.transpose(3, 0, 2, 1, 4).reshape(8, span, row_count * HD)
    sent = [pick(d_att, seq ^ m) for m in range(8)]
    arrived = [sent[0]] + [swap(sent[m], m * 4) for m in range(1, 8)]
    d_heads = unswap(arrived, seq).reshape(row_len, row_count * HD)
    log_rows = jnp.stack([logs[:, 0], logs[:, HD]])
    d_mixed, d_packed = attend_back(
        place, split, q, k, v, k.T, out_heads, d_heads, log_rows, tables, local_len
    )

    reach = row_len // 4
    sent = [lax.dynamic_slice_in_dim(d_packed, (plane + s) % 4 * reach, reach, 0) for s in range(4)]
    arrived = jnp.stack([sent[0]] + [shift(sent[s], s) for s in (1, 2, 3)])
    weights = [head_weight]
    for _ in range(3):
        weights.append(shift(weights[-1], 1))
    weights = jnp.stack(weights)
    near_weight = jnp.concatenate(
        [
            weights[:, :, : 2 * HD].transpose(1, 0, 2).reshape(features, 8 * HD),
            weights[:, :, 2 * HD : 3 * HD].transpose(1, 0, 2).reshape(features, 4 * HD),
        ],
        axis=1,
    )
    tiles = arrived.reshape(4, reach, 3, 2 * HD)
    lines = []
    for row in range(2):
        lines.append(
            jnp.concatenate(
                [
                    tiles[:, :, row].transpose(1, 0, 2).reshape(reach, 8 * HD),
                    tiles[:, :, 2, row * HD : (row + 1) * HD].transpose(1, 0, 2).reshape(reach, 4 * HD),
                ],
                axis=1,
            )
        )
    d_in = dot_rows(jnp.concatenate(lines, axis=0), near_weight)
    d_in = d_in.reshape(row_count, 8, local_len, features).transpose(1, 0, 2, 3)
    near = jnp.stack([pick(d_in, own ^ m).reshape(tokens, features) for m in range(4)])
    far = jnp.stack([pick(d_in, own ^ (m + 4)).reshape(tokens, features) for m in range(4)])
    d_norm_in = sum_plane(near, far)
    d_flat_part, d_gain_one, d_bias_one = norm1_back(d_norm_in)
    d_inputs = d_middle + d_flat_part

    d_mixed = d_mixed.reshape(row_len * row_count, 4 * HD)
    head_grad = dot_cols(jnp.concatenate(in_halves, axis=0), d_mixed)[:, : 3 * HD].astype(BF)
    head_grad = head_grad.reshape(4, shard, 3 * HD)
    head_rows = unswap(
        [pick(head_grad, rank)] + [swap(pick(head_grad, rank ^ m), m) for m in (1, 2, 3)], rank
    )
    qkv_grad = lax.all_gather(head_rows, "seq", axis=0)
    qkv_grad = (
        qkv_grad.reshape(8, 4, shard, 3, HD).transpose(2, 3, 1, 0, 4).reshape(shard, 3 * features)
    ).astype(F32)
    bias_sum = jnp.sum(d_mixed.astype(F32), axis=0)
    bias_own = jnp.zeros((3 * features,), F32)
    for part in range(3):
        bias_own = lax.dynamic_update_slice_in_dim(
            bias_own, bias_sum[part * HD : (part + 1) * HD], head_first + part * features, 0
        )

    att_order = jnp.stack([pick(att.transpose(1, 0, 2, 3), rank ^ m) for m in range(4)])
    out_part = dot_cols(att_order.reshape(4 * tokens, shard), d_branch).astype(BF)
    out_part = lax.psum_scatter(out_part, "seq", scatter_dimension=0, tiled=True)
    out_grad = lax.all_gather(out_part, "seq", axis=0, tiled=True).astype(F32)

    def gather_rest(value):
        pieces = [shift(value, 1)]
        for _ in range(2):
            pieces.append(shift(pieces[-1], 1))
        return gather_plane(jnp.concatenate(pieces, axis=0))

    mid_rest = gather_rest(mid_low)
    out_rest = gather_rest(d_out)
    rest = [hidden_layer(m, o, gate_up_pad, down_pad) for m, o in zip(mid_rest, out_rest)]
    mid_all = jnp.concatenate([mid_near, mid_far, *mid_rest], axis=0)
    out_all = jnp.concatenate([out_near, out_far, *out_rest], axis=0)
    act_all = jnp.concatenate([act_near, act_far, rest[0][0], rest[1][0]], axis=0)
    d_gu_all = jnp.concatenate([d_gu_near, d_gu_far, rest[0][1], rest[1][1]], axis=0)
    down_own = dot_cols(act_all, out_all)[:share].astype(BF)
    down_other = swap(down_own, 4)
    down_pair = jnp.stack([down_own, down_other])
    down_grad = jnp.concatenate([pick(down_pair, core), pick(down_pair, 1 - core)], axis=0).astype(F32)
    gate_up_own = dot_cols(mid_all, d_gu_all).reshape(features, 2, padded)[:, :, :share].astype(BF)
    gate_up_own = gate_up_own.reshape(4, shard, 2 * share)
    gate_up_rows = unswap(
        [pick(gate_up_own, rank)] + [swap(pick(gate_up_own, rank ^ m), m) for m in (1, 2, 3)], rank
    )
    gate_up_pair = jnp.stack([gate_up_rows, swap(gate_up_rows, 4)])
    gate_up_pair = jnp.stack([pick(gate_up_pair, core), pick(gate_up_pair, 1 - core)])
    gate_up_grad = (
        gate_up_pair.reshape(2, 4, shard, 2, share)
        .transpose(2, 3, 1, 0, 4)
        .reshape(shard, 2 * hidden)
        .astype(F32)
    )
    sums = sum_all(jnp.concatenate([d_gain_one, d_bias_one, bias_own, d_gain_two, d_bias_two]))
    return (
        result.reshape(row_count, local_len, features),
        d_inputs.reshape(row_count, local_len, features),
        sums[:features],
        sums[features : 2 * features],
        qkv_grad,
        sums[2 * features : 5 * features],
        out_grad,
        sums[5 * features : 6 * features],
        sums[6 * features :],
        gate_up_grad,
        down_grad,
    )


def solution(mesh):
    placed = (
        P(None, ("seq", "fsdp"), None),
        P(),
        P(),
        P(),
        P("fsdp", None),
        P(),
        P("fsdp", None),
        P(),
        P(),
        P("fsdp", None),
        P("fsdp", None),
        P(None, ("seq", "fsdp"), None),
    )
    plan = plane_plan if (mesh.shape["seq"], mesh.shape["fsdp"]) == (8, 4) else general_plan
    return jax.shard_map(
        plan,
        mesh=mesh,
        in_specs=placed,
        out_specs=(
            P(None, ("seq", "fsdp"), None),
            P(None, ("seq", "fsdp"), None),
            P(),
            P(),
            P("fsdp", None),
            P(),
            P("fsdp", None),
            P(),
            P(),
            P("fsdp", None),
            P("fsdp", None),
        ),
        check_vma=False,
    )
```

```python
import functools

import jax
import jax.numpy as jnp
from jax import lax
from jax.experimental import pallas as pl
from jax.experimental.pallas import tpu as pltpu
from jax.sharding import PartitionSpec as P

HD = 64
ROT = 16


EPSILON = 1e-05
MASKED = -1e30


def layer_norm(values, norm_gain, offset):
    average = jnp.mean(values, axis=-1, keepdims=True)
    centred = values - average
    variance = jnp.mean(centred * centred, axis=-1, keepdims=True)
    return centred * lax.rsqrt(variance + EPSILON) * norm_gain + offset


def rotate(values, positions):
    half_rot = ROT // 2
    exponent = jnp.arange(half_rot, dtype=jnp.float32) * (2.0 / ROT)
    inverse = jnp.power(jnp.float32(10000.0), -exponent)
    angles = positions.astype(jnp.float32)[:, None] * inverse[None, :]
    cosine = jnp.cos(angles)[:, None, :]
    sine = jnp.sin(angles)[:, None, :]
    first = values[:, :, :half_rot]
    second = values[:, :, half_rot:ROT]
    return jnp.concatenate(
        [first * cosine - second * sine, second * cosine + first * sine, values[:, :, ROT:]], axis=2
    )


def fold_rows(left, shard):
    return jnp.dot(
        left, lax.all_gather(shard, "fsdp", axis=0, tiled=True), preferred_element_type=jnp.float32
    )


def map_back(grad_rows, shard):
    return lax.dot_general(
        grad_rows,
        lax.all_gather(shard, "fsdp", axis=0, tiled=True),
        (((1,), (1,)), ((), ())),
        preferred_element_type=jnp.float32,
    )


def grad_joint(left, right_side):
    seq_count = lax.axis_size("seq")
    fsdp_count = lax.axis_size("fsdp")
    token_count, total_rows = left.shape
    share = total_rows // (seq_count * fsdp_count)
    permuted = (
        left.reshape(token_count, fsdp_count, seq_count, share)
        .transpose(0, 2, 1, 3)
        .reshape(token_count, total_rows)
    )
    return lax.psum_scatter(
        lax.dot_general(
            permuted, right_side, (((0,), (0,)), ((), ())), preferred_element_type=jnp.float32
        ),
        ("seq", "fsdp"),
        scatter_dimension=0,
        tiled=True,
    )


def general_plan(
    inputs,
    segments,
    norm1_gain,
    norm1_bias,
    qkv_weight,
    qkv_bias,
    out_weight,
    norm2_gain,
    norm2_bias,
    gate_up_weight,
    down_weight,
    cotangent,
):
    row_count, local_len, features = inputs.shape
    fsdp_count = lax.axis_size("fsdp")
    fsdp_rank = lax.axis_index("fsdp")
    block_rank = lax.axis_index("seq") * fsdp_count + fsdp_rank
    token_count = row_count * local_len
    head_count = features // HD
    ff_width = gate_up_weight.shape[1] // 2
    scale_factor = HD ** (-0.5)
    flat = inputs.reshape(token_count, features).astype(jnp.float32)
    local_pos = block_rank * local_len + jnp.arange(local_len, dtype=jnp.int32)
    positions = jnp.tile(local_pos, row_count)
    weight_set = (qkv_weight, out_weight, gate_up_weight, down_weight)

    def forward_product(left, slot_index):
        return fold_rows(left, weight_set[slot_index])

    def backward_product(grad_rows, slot_index):
        return map_back(grad_rows, weight_set[slot_index])

    normed_in, norm1_back = jax.vjp(layer_norm, flat, norm1_gain, norm1_bias)
    in_low = normed_in.astype(jnp.bfloat16)
    mixed = forward_product(in_low, 0) + qkv_bias
    turn_input = mixed[:, : 2 * features].reshape(token_count, 2 * head_count, HD)
    turned, turn_back = jax.vjp(lambda values: rotate(values, positions), turn_input)
    turned_low = turned.astype(jnp.bfloat16)
    queries = turned_low[:, :head_count].reshape(row_count, local_len, features)
    keys_loc = turned_low[:, head_count:].reshape(row_count, local_len, features)
    values_loc = (
        mixed[:, 2 * features :].astype(jnp.bfloat16).reshape(row_count, local_len, features)
    )
    head_query, head_key, head_value = (
        lax.all_to_all(queries, "seq", split_axis=2, concat_axis=1, tiled=True),
        lax.all_to_all(keys_loc, "seq", split_axis=2, concat_axis=1, tiled=True),
        lax.all_to_all(values_loc, "seq", split_axis=2, concat_axis=1, tiled=True),
    )
    all_keys, all_values = (
        lax.all_gather(head_key, "fsdp", axis=1, tiled=True),
        lax.all_gather(head_value, "fsdp", axis=1, tiled=True),
    )
    query_len = head_query.shape[1]
    key_len = all_keys.shape[1]
    head_width = head_query.shape[2]
    local_heads = head_width // HD
    query_four = head_query.reshape(row_count, query_len, local_heads, HD)
    keys_four = all_keys.reshape(row_count, key_len, local_heads, HD)
    values_four = all_values.reshape(row_count, key_len, local_heads, HD)
    query_index = jnp.arange(query_len, dtype=jnp.int32)
    query_pos = (
        query_index // local_len * fsdp_count + fsdp_rank
    ) * local_len + query_index % local_len
    key_index = jnp.arange(key_len, dtype=jnp.int32)
    key_pos = (
        key_index % query_len // local_len * fsdp_count + key_index // query_len
    ) * local_len + key_index % local_len
    query_seg = jnp.take(segments, query_pos, axis=1)
    key_seg = jnp.take(segments, key_pos, axis=1)
    span = min(512, key_len)
    block_count = key_len // span

    def block_inputs(block_index):
        first_row = block_index * span
        block_keys = lax.dynamic_slice_in_dim(keys_four, first_row, span, 1)
        block_values = lax.dynamic_slice_in_dim(values_four, first_row, span, 1)
        block_pos = lax.dynamic_slice_in_dim(key_pos, first_row, span, 0)
        block_seg = lax.dynamic_slice_in_dim(key_seg, first_row, span, 1)
        allowed = (query_seg[:, :, None] == block_seg[:, None, :]) & (
            block_pos[None, None, :] <= query_pos[None, :, None]
        )
        scores = (
            jnp.einsum(
                "rqhd,rkhd->rhqk", query_four, block_keys, preferred_element_type=jnp.float32
            )
            * scale_factor
        )
        return (first_row, block_keys, block_values, allowed[:, None], scores)

    def forward_block(carry, block_index):
        row_top, running, weighted = carry
        first_row, block_keys, block_values, allowed, scores = block_inputs(block_index)
        new_top = jnp.maximum(row_top, jnp.max(jnp.where(allowed, scores, MASKED), axis=-1))
        probs = jnp.where(allowed, jnp.exp(scores - new_top[..., None]), 0.0)
        factor = jnp.exp(row_top - new_top)
        running = running * factor + jnp.sum(probs, axis=-1)
        weighted = weighted * factor[..., None] + jnp.einsum(
            "rhqk,rkhd->rhqd",
            probs.astype(jnp.bfloat16),
            block_values,
            preferred_element_type=jnp.float32,
        )
        return ((new_top, running, weighted), None)

    start_top = jnp.full((row_count, local_heads, query_len), MASKED, jnp.float32)
    start_total = jnp.zeros((row_count, local_heads, query_len), jnp.float32)
    start_weighted = jnp.zeros((row_count, local_heads, query_len, HD), jnp.float32)
    (row_top, running, weighted), _ = lax.scan(
        forward_block, (start_top, start_total, start_weighted), jnp.arange(block_count)
    )
    log_total = row_top + jnp.log(running)
    attended_heads = (
        (weighted / running[..., None])
        .transpose(0, 2, 1, 3)
        .reshape(row_count, query_len, head_width)
        .astype(jnp.bfloat16)
    )
    attended_loc = lax.all_to_all(attended_heads, "seq", split_axis=1, concat_axis=2, tiled=True)
    att_flat = attended_loc.reshape(token_count, features)
    middle = flat + forward_product(att_flat, 1)
    normed_mid, norm2_back = jax.vjp(layer_norm, middle, norm2_gain, norm2_bias)
    mid_low = normed_mid.astype(jnp.bfloat16)
    gate_up = forward_product(mid_low, 2)
    act_value, silu_back = jax.vjp(
        lambda gate_part, up_part: jax.nn.silu(gate_part) * up_part,
        gate_up[:, :ff_width],
        gate_up[:, ff_width:],
    )
    act_low = act_value.astype(jnp.bfloat16)
    result = middle + forward_product(act_low, 3)
    d_out = cotangent.reshape(token_count, features)
    d_act = backward_product(d_out, 3)
    d_gate, d_up = silu_back(d_act)
    d_gate_up = jnp.concatenate([d_gate, d_up], axis=1).astype(jnp.bfloat16)
    d_mid_norm = backward_product(d_gate_up, 2)
    d_middle_part, d_gain_two, d_bias_two = norm2_back(d_mid_norm)
    d_middle = d_out.astype(jnp.float32) + d_middle_part
    d_branch = d_middle.astype(jnp.bfloat16)
    d_attended = (
        backward_product(d_branch, 1).astype(jnp.bfloat16).reshape(row_count, local_len, features)
    )
    d_heads = lax.all_to_all(d_attended, "seq", split_axis=2, concat_axis=1, tiled=True)
    d_heads_four = d_heads.reshape(row_count, query_len, local_heads, HD)
    attended_four = attended_heads.reshape(row_count, query_len, local_heads, HD)
    delta = jnp.einsum(
        "rqhd,rqhd->rhq", d_heads_four.astype(jnp.float32), attended_four.astype(jnp.float32)
    )

    def backward_block(carry, block_index):
        d_query, d_keys_all, d_values_all = carry
        first_row, block_keys, block_values, allowed, scores = block_inputs(block_index)
        probs = jnp.where(allowed, jnp.exp(scores - log_total[..., None]), 0.0)
        d_block_values = jnp.einsum(
            "rhqk,rqhd->rkhd",
            probs.astype(jnp.bfloat16),
            d_heads_four,
            preferred_element_type=jnp.float32,
        )
        d_probs = jnp.einsum(
            "rqhd,rkhd->rhqk", d_heads_four, block_values, preferred_element_type=jnp.float32
        )
        d_scores = (probs * (d_probs - delta[..., None])).astype(jnp.bfloat16)
        d_query = (
            d_query
            + jnp.einsum(
                "rhqk,rkhd->rqhd", d_scores, block_keys, preferred_element_type=jnp.float32
            )
            * scale_factor
        )
        d_block_keys = (
            jnp.einsum("rhqk,rqhd->rkhd", d_scores, query_four, preferred_element_type=jnp.float32)
            * scale_factor
        )
        d_keys_all = lax.dynamic_update_slice_in_dim(d_keys_all, d_block_keys, first_row, 1)
        d_values_all = lax.dynamic_update_slice_in_dim(d_values_all, d_block_values, first_row, 1)
        return ((d_query, d_keys_all, d_values_all), None)

    zero_query = jnp.zeros((row_count, query_len, local_heads, HD), jnp.float32)
    zero_keys = jnp.zeros((row_count, key_len, local_heads, HD), jnp.float32)
    (d_query, d_keys_all, d_values_all), _ = lax.scan(
        backward_block, (zero_query, zero_keys, zero_keys), jnp.arange(block_count)
    )
    d_keys_sum, d_values_sum = (
        lax.psum_scatter(
            d_keys_all.reshape(row_count, key_len, head_width).astype(jnp.bfloat16),
            "fsdp",
            scatter_dimension=1,
            tiled=True,
        ).astype(jnp.float32),
        lax.psum_scatter(
            d_values_all.reshape(row_count, key_len, head_width).astype(jnp.bfloat16),
            "fsdp",
            scatter_dimension=1,
            tiled=True,
        ).astype(jnp.float32),
    )
    d_query_low = d_query.reshape(row_count, query_len, head_width).astype(jnp.bfloat16)
    dq_back, dk_back, dv_back = (
        lax.all_to_all(d_query_low, "seq", split_axis=1, concat_axis=2, tiled=True),
        lax.all_to_all(
            d_keys_sum.astype(jnp.bfloat16), "seq", split_axis=1, concat_axis=2, tiled=True
        ),
        lax.all_to_all(
            d_values_sum.astype(jnp.bfloat16), "seq", split_axis=1, concat_axis=2, tiled=True
        ),
    )
    d_turned = jnp.concatenate(
        [
            dq_back.reshape(token_count, head_count, HD),
            dk_back.reshape(token_count, head_count, HD),
        ],
        axis=1,
    ).astype(jnp.float32)
    (d_turn_input,) = turn_back(d_turned)
    d_mixed = jnp.concatenate(
        [
            d_turn_input.reshape(token_count, 2 * features),
            dv_back.reshape(token_count, features).astype(jnp.float32),
        ],
        axis=1,
    ).astype(jnp.bfloat16)
    d_qkv_bias = jnp.sum(d_mixed.astype(jnp.float32), axis=0)
    d_norm_in = backward_product(d_mixed, 0)
    d_flat_part, d_gain_one, d_bias_one = norm1_back(d_norm_in)
    d_inputs = d_middle + d_flat_part
    first_grad = grad_joint(in_low, d_mixed)
    second_grad = grad_joint(att_flat, d_branch)
    third_grad = grad_joint(mid_low, d_gate_up)
    fourth_grad = grad_joint(act_low, d_out)
    qkv_grad, out_grad, gate_up_grad, down_grad = (
        lax.all_gather(first_grad.astype(jnp.bfloat16), "seq", axis=0, tiled=True).astype(
            first_grad.dtype
        ),
        lax.all_gather(second_grad.astype(jnp.bfloat16), "seq", axis=0, tiled=True).astype(
            second_grad.dtype
        ),
        lax.all_gather(third_grad.astype(jnp.bfloat16), "seq", axis=0, tiled=True).astype(
            third_grad.dtype
        ),
        lax.all_gather(fourth_grad.astype(jnp.bfloat16), "seq", axis=0, tiled=True).astype(
            fourth_grad.dtype
        ),
    )
    gain_one, bias_one, bias_qkv, gain_two, bias_two = lax.psum(
        (d_gain_one, d_bias_one, d_qkv_bias, d_gain_two, d_bias_two), ("seq", "fsdp")
    )
    return (
        result.reshape(row_count, local_len, features),
        d_inputs.reshape(row_count, local_len, features),
        gain_one,
        bias_one,
        qkv_grad,
        bias_qkv,
        out_grad,
        gain_two,
        bias_two,
        gate_up_grad,
        down_grad,
    )


BLOCK = 512
BF = jnp.bfloat16
F32 = jnp.float32
SMALL = pl.CostEstimate(flops=1000, bytes_accessed=1000, transcendentals=0)


def swap(value, mask):
    return lax.ppermute(value, ("z", "core", "fsdp"), [(i, i ^ mask) for i in range(32)])


def shift(value, steps):
    return lax.ppermute(value, ("z", "core", "fsdp"), [(i, (i + 8 * steps) % 32) for i in range(32)])


def pick(stacked, index):
    return lax.dynamic_index_in_dim(stacked, index, 0, keepdims=False)


def exchange(value, axis="fsdp"):
    return lax.all_to_all(value, axis, split_axis=0, concat_axis=0, tiled=True)


def gather_near(value):
    half = value.shape[0] // 2
    by_x = swap(value, 1)
    by_y = swap(value, 2)
    return [value, by_x, by_y, swap(by_x[:half], 2), swap(by_y[half:], 1)]


def both_cores(near):
    return near + [swap(piece, 4) for piece in near]


def gather_pieces(value):
    return both_cores(gather_near(value))


def sum_quad(terms):
    return terms[0].astype(F32) + sum(swap(terms[m].astype(BF), m).astype(F32) for m in (1, 2, 3))


def sum_plane(near, far):
    arrived = swap(far.astype(BF), 4)
    return sum_quad([near[m].astype(F32) + arrived[m].astype(F32) for m in range(4)])


def dot(left, right):
    return jnp.dot(left, right, preferred_element_type=F32)


def dot_rows(left, right):
    return lax.dot_general(left, right, (((1,), (1,)), ((), ())), preferred_element_type=F32)


def dot_cols(left, right):
    return lax.dot_general(left, right, (((0,), (0,)), ((), ())), preferred_element_type=F32)


def turn_tables(row_len):
    half_rot = ROT // 2
    lane = jnp.arange(2 * HD, dtype=jnp.int32) % HD
    exponent = (lane % half_rot).astype(F32) * (2.0 / ROT)
    inverse = jnp.power(jnp.float32(10000.0), -exponent)
    angles = jnp.arange(row_len, dtype=jnp.int32).astype(F32)[:, None] * inverse[None, :]
    cosine = jnp.where(lane < ROT, jnp.cos(angles), 1.0)
    sine = jnp.sin(angles)
    ahead = jnp.where(lane < half_rot, -sine, 0.0)
    behind = jnp.where((lane >= half_rot) & (lane < ROT), sine, 0.0)
    return cosine, ahead, behind


def attend_kernel(
    split_ref, where_ref, mixed_ref, cos_ref, ahead_ref, behind_ref,
    q_ref, k_ref, v_ref, o_ref, log_ref, mine_ref, theirs_ref, kz, vz,
):
    local_len = mixed_ref.shape[2]
    row_len = q_ref.shape[0]
    low = lax.broadcasted_iota(jnp.int32, (local_len, 2 * HD), 1) < HD

    def prepare(i, carry):
        rows = pl.ds(pl.multiple_of(i * local_len, local_len), local_len)
        cosine, ahead, behind = cos_ref[rows], ahead_ref[rows], behind_ref[rows]

        def turn(x):
            return (
                x * cosine
                + pltpu.roll(x, 2 * HD - ROT // 2, 1) * ahead
                + pltpu.roll(x, ROT // 2, 1) * behind
            )

        first = mixed_ref[i, 0]
        second = mixed_ref[i, 1]
        turned0 = turn(first[:, : 2 * HD])
        turned1 = turn(second[:, : 2 * HD])
        q = jnp.where(low, turned0, pltpu.roll(turned1, HD, 1))
        k = jnp.where(low, pltpu.roll(turned0, HD, 1), turned1)
        v = jnp.where(low, first[:, 2 * HD :], second[:, 2 * HD :])
        q_ref[rows] = (q * HD**-0.5).astype(BF)
        k_ref[rows] = k.astype(BF)
        v_ref[rows] = v.astype(BF)
        kz[0, rows] = jnp.where(low, k, 0.0).astype(BF)
        kz[1, rows] = jnp.where(low, 0.0, k).astype(BF)
        vz[0, rows] = jnp.where(low, v, 0.0).astype(BF)
        vz[1, rows] = jnp.where(low, 0.0, v).astype(BF)
        return carry

    lax.fori_loop(0, row_len // local_len, prepare, 0)
    t_in = lax.broadcasted_iota(jnp.int32, (BLOCK, 1), 0)
    u_in = lax.broadcasted_iota(jnp.int32, (1, BLOCK), 1)
    low_q = lax.broadcasted_iota(jnp.int32, (BLOCK, 2 * HD), 1) < HD

    def query_block(qb, carry):
        rows = pl.ds(pl.multiple_of(qb * BLOCK, BLOCK), BLOCK)
        q = q_ref[rows]
        t = t_in + qb * BLOCK
        outs, logs = [], []
        for row in range(2):
            split = split_ref[row]
            start = jnp.where(t >= split, split, 0)

            def step(kb, state, diagonal, row=row, start=start):
                top, total, acc = state
                keys = pl.ds(pl.multiple_of(kb * BLOCK, BLOCK), BLOCK)
                u = u_in + kb * BLOCK
                scores = dot_rows(q, kz[row, keys])
                allowed = u >= start
                if diagonal:
                    allowed = allowed & (u <= t)
                scores = jnp.where(allowed, scores, MASKED)
                new_top = jnp.maximum(top, jnp.max(scores, axis=1, keepdims=True))
                probs = jnp.exp(scores - new_top)
                factor = jnp.exp(top - new_top)
                total = total * factor + jnp.sum(probs, axis=1, keepdims=True)
                acc = acc * factor + dot(probs.astype(BF), vz[row, keys])
                return new_top, total, acc

            state = (
                jnp.full((BLOCK, 1), MASKED, F32),
                jnp.zeros((BLOCK, 1), F32),
                jnp.zeros((BLOCK, 2 * HD), F32),
            )
            first_kb = jnp.where(qb * BLOCK >= split, split // BLOCK, 0)
            state = lax.fori_loop(
                first_kb, qb, lambda kb, state, step=step: step(kb, state, False), state
            )
            top, total, acc = step(qb, state, True)
            outs.append(acc / total)
            logs.append(top + jnp.log(total))
        o_ref[rows] = (outs[0] + outs[1]).astype(BF)
        log_ref[rows] = jnp.where(low_q, logs[0], logs[1])
        step = lax.rem(qb - where_ref[0] + 4, 4)
        core = where_ref[1] // 4
        half = BLOCK // 2
        for ref, which in ((mine_ref, core), (theirs_ref, 1 - core)):
            ref[step] = o_ref[pl.ds(pl.multiple_of(qb * BLOCK + which * half, half), half)]
        return carry

    lax.fori_loop(0, row_len // BLOCK, query_block, 0)


def attend(split, where, mixed, tables):
    row_len = tables[0].shape[0]
    packed = jax.ShapeDtypeStruct((row_len, 2 * HD), BF)
    smem = pl.BlockSpec(memory_space=pltpu.SMEM)
    vmem = pl.BlockSpec(memory_space=pltpu.VMEM)
    pairs = 2 * row_len * row_len // 2
    return pl.pallas_call(
        attend_kernel,
        out_shape=(packed, packed, packed, packed, jax.ShapeDtypeStruct((row_len, 2 * HD), F32))
        + (jax.ShapeDtypeStruct((4, row_len // 8, 2 * HD), BF),) * 2,
        in_specs=[smem, smem, vmem, vmem, vmem, vmem],
        out_specs=(vmem,) * 7,
        scratch_shapes=[pltpu.VMEM((2, row_len, 2 * HD), BF), pltpu.VMEM((2, row_len, 2 * HD), BF)],
        compiler_params=pltpu.CompilerParams(vmem_limit_bytes=48 * 2**20),
        cost_estimate=SMALL,
        name="attend",
    )(split, where, mixed, *tables)


def attend_back_kernel(
    split_ref, q_ref, k_ref, v_ref, kt_ref, o_ref, do_ref, log_ref,
    cos_ref, ahead_ref, behind_ref,
    dmix_ref, dpos_ref, kz, vz, qz, dz, ktz, delta, dq_t, dk, dv,
):
    row_len = q_ref.shape[0]
    local_len = dmix_ref.shape[2]
    low = lax.broadcasted_iota(jnp.int32, (BLOCK, 2 * HD), 1) < HD
    low_t = lax.broadcasted_iota(jnp.int32, (2 * HD, BLOCK), 0) < HD
    lane = lax.broadcasted_iota(jnp.int32, (8, 2 * HD), 1)
    ones = [jnp.where(lane < HD, 1.0, 0.0).astype(BF), jnp.where(lane < HD, 0.0, 1.0).astype(BF)]

    def prepare(b, carry):
        rows = pl.ds(pl.multiple_of(b * BLOCK, BLOCK), BLOCK)
        zero = jnp.zeros((BLOCK, 2 * HD), F32)
        for ref, out in ((k_ref, kz), (v_ref, vz), (q_ref, qz), (do_ref, dz)):
            value = ref[rows].astype(F32)
            out[0, rows] = jnp.where(low, value, zero).astype(BF)
            out[1, rows] = jnp.where(low, zero, value).astype(BF)
        value = kt_ref[:, rows].astype(F32)
        ktz[0, :, rows] = jnp.where(low_t, value, 0.0).astype(BF)
        ktz[1, :, rows] = jnp.where(low_t, 0.0, value).astype(BF)
        product = do_ref[rows].astype(F32) * o_ref[rows].astype(F32)
        coarse = product.astype(BF)
        fine = (product - coarse.astype(F32)).astype(BF)
        for row in range(2):
            delta[row, :, rows] = dot_rows(ones[row], coarse) + dot_rows(ones[row], fine)
        dq_t[:, rows] = jnp.zeros((2 * HD, BLOCK), F32)
        return carry

    lax.fori_loop(0, row_len // BLOCK, prepare, 0)
    u_in = lax.broadcasted_iota(jnp.int32, (BLOCK, 1), 0)
    t_in = lax.broadcasted_iota(jnp.int32, (1, BLOCK), 1)

    def key_block(kb, carry):
        keys = pl.ds(pl.multiple_of(kb * BLOCK, BLOCK), BLOCK)
        u = u_in + kb * BLOCK
        sums_k, sums_v = [], []
        for row in range(2):
            split = split_ref[row]
            k_row = kz[row, keys]
            v_row = vz[row, keys]
            kt_row = ktz[row, :, keys]

            def step(qb, state, row=row, split=split, k_row=k_row, v_row=v_row, kt_row=kt_row):
                d_keys, d_values = state
                rows = pl.ds(pl.multiple_of(qb * BLOCK, BLOCK), BLOCK)
                t = t_in + qb * BLOCK
                start = jnp.where(t >= split, split, 0)
                allowed = (u >= start) & (u <= t)
                scores = dot_rows(k_row, q_ref[rows])
                probs = jnp.where(allowed, jnp.exp(scores - log_ref[pl.ds(row, 1), rows]), 0.0)
                d_probs = dot_rows(v_row, do_ref[rows])
                d_scores = (probs * (d_probs - delta[row, pl.ds(0, 1), rows])).astype(BF)
                d_values = d_values + dot(probs.astype(BF), dz[row, rows])
                d_keys = d_keys + dot(d_scores, qz[row, rows])
                dq_t[:, rows] += dot(kt_row, d_scores)
                return d_keys, d_values

            zero = jnp.zeros((BLOCK, 2 * HD), F32)
            last = jnp.where(
                (kb + 1) * BLOCK <= split, (split + BLOCK - 1) // BLOCK, row_len // BLOCK
            )
            d_keys, d_values = lax.fori_loop(kb, last, step, (zero, zero))
            sums_k.append(d_keys)
            sums_v.append(d_values)
        dk[keys] = sums_k[0] + sums_k[1]
        dv[keys] = sums_v[0] + sums_v[1]
        return carry

    lax.fori_loop(0, row_len // BLOCK, key_block, 0)
    low_l = lax.broadcasted_iota(jnp.int32, (local_len, 2 * HD), 1) < HD
    per = 2 * HD // local_len


    def finish(b, carry):
        start = pl.multiple_of(b * 2 * HD, 2 * HD)
        dq = dq_t[:, pl.ds(start, 2 * HD)].T * HD**-0.5
        for part in range(per):
            i = b * per + part
            rows = pl.ds(pl.multiple_of(i * local_len, local_len), local_len)
            cosine, ahead, behind = cos_ref[rows], ahead_ref[rows], behind_ref[rows]

            def turn(x, cosine=cosine, ahead=ahead, behind=behind):
                return (
                    x * cosine
                    - pltpu.roll(x, 2 * HD - ROT // 2, 1) * ahead
                    - pltpu.roll(x, ROT // 2, 1) * behind
                )

            q_part = turn(dq[part * local_len : (part + 1) * local_len])
            k_part = turn(dk[rows])
            v_part = dv[rows]
            first = jnp.where(low_l, q_part, pltpu.roll(k_part, HD, 1)).astype(BF)
            second = jnp.where(low_l, pltpu.roll(q_part, HD, 1), k_part).astype(BF)
            dpos_ref[rows, : 2 * HD] = first
            dpos_ref[rows, 2 * HD : 4 * HD] = second
            dpos_ref[rows, 4 * HD :] = v_part.astype(BF)
            dmix_ref[i, 0, :, : 2 * HD] = first
            dmix_ref[i, 1, :, : 2 * HD] = second
            dmix_ref[i, 0, :, 2 * HD :] = jnp.where(low_l, v_part, 0.0).astype(BF)
            dmix_ref[i, 1, :, 2 * HD :] = jnp.where(low_l, pltpu.roll(v_part, HD, 1), 0.0).astype(BF)
        return carry

    lax.fori_loop(0, row_len // (2 * HD), finish, 0)


def attend_back(split, q, k, v, k_t, out, d_out, logs, tables, local_len):
    row_len = q.shape[0]
    smem = pl.BlockSpec(memory_space=pltpu.SMEM)
    vmem = pl.BlockSpec(memory_space=pltpu.VMEM)
    masked = pltpu.VMEM((2, row_len, 2 * HD), BF)
    whole = pltpu.VMEM((row_len, 2 * HD), F32)
    pairs = 2 * row_len * row_len // 2
    return pl.pallas_call(
        attend_back_kernel,
        out_shape=(
            jax.ShapeDtypeStruct((row_len // local_len, 2, local_len, 4 * HD), BF),
        )
        + (jax.ShapeDtypeStruct((row_len, 6 * HD), BF),),
        in_specs=[smem] + [vmem] * 10,
        out_specs=(vmem,) * 2,
        scratch_shapes=[
            masked, masked, masked, masked,
            pltpu.VMEM((2, 2 * HD, row_len), BF),
            pltpu.VMEM((2, 8, row_len), F32),
            pltpu.VMEM((2 * HD, row_len), F32),
            whole, whole,
        ],
        compiler_params=pltpu.CompilerParams(vmem_limit_bytes=48 * 2**20),
        cost_estimate=SMALL,
        name="attend_back",
    )(split, q, k, v, k_t, out, d_out, logs, *tables)


def pick_heads_kernel(where_ref, q_ref, k_ref, v_ref, out_ref):
    wide = 2 * HD
    low = lax.broadcasted_iota(jnp.int32, (q_ref.shape[0], wide), 1) < HD
    for core in (0, 1):

        @pl.when(where_ref[1] // 4 == core)
        def _(core=core):
            def join(left, right):
                if core == 0:
                    return jnp.where(low, left, pltpu.roll(right, HD, 1)).astype(BF)
                return jnp.where(low, pltpu.roll(left, HD, 1), right).astype(BF)

            for z in range(4):
                cols = slice(z * wide, (z + 1) * wide)
                out_ref[:, cols] = join(q_ref[:, cols].astype(F32), k_ref[:, cols].astype(F32))
            for pair in range(2):
                left, right = (
                    v_ref[:, (2 * pair + n) * wide : (2 * pair + n + 1) * wide].astype(F32) for n in (0, 1)
                )
                out_ref[:, (4 + pair) * wide : (5 + pair) * wide] = join(left, right)


def pick_heads(where, weight):
    rows, columns = weight.shape
    wide = columns // 12
    blocks = [
        pl.BlockSpec((rows, wide), lambda chip, where, part=part: (0, part * 4 + chip)) for part in range(3)
    ]
    return pl.pallas_call(
        pick_heads_kernel,
        grid_spec=pltpu.PrefetchScalarGridSpec(
            num_scalar_prefetch=1,
            grid=(4,),
            in_specs=blocks,
            out_specs=pl.BlockSpec((None, rows, 12 * HD), lambda chip, where: (chip, 0, 0)),
        ),
        out_shape=jax.ShapeDtypeStruct((4, rows, 12 * HD), BF),
        compiler_params=pltpu.CompilerParams(vmem_limit_bytes=32 * 2**20),
        cost_estimate=SMALL,
        name="pick_heads",
    )(where, weight, weight, weight)


def small_call(kernel, name, out_shape, where, *arrays, flops=0, scratch=(), limit=32):
    size = sum(x.size * x.dtype.itemsize for x in arrays)
    vmem = pl.BlockSpec(memory_space=pltpu.VMEM)
    return pl.pallas_call(
        kernel,
        out_shape=out_shape,
        in_specs=[pl.BlockSpec(memory_space=pltpu.SMEM)] + [vmem] * len(arrays),
        out_specs=[vmem] * len(out_shape),
        scratch_shapes=scratch,
        compiler_params=pltpu.CompilerParams(vmem_limit_bytes=limit * 2**20),
        cost_estimate=SMALL,
        name=name,
    )(where, *arrays)


def pair_kernel(where_ref, mine_ref, theirs_ref, *outs):
    low = lax.broadcasted_iota(jnp.int32, mine_ref.shape[1:], 1) < HD
    for step, out in enumerate(outs):
        for core, (ref0, ref1) in enumerate(((mine_ref, theirs_ref), (theirs_ref, mine_ref))):

            @pl.when(where_ref[1] // 4 == core)
            def _(ref0=ref0, ref1=ref1):
                even, uneven = ref0[step].astype(F32), ref1[step].astype(F32)
                out[:, : 2 * HD] = jnp.where(low, even, pltpu.roll(uneven, HD, 1)).astype(BF)
                out[:, 2 * HD :] = jnp.where(low, pltpu.roll(even, HD, 1), uneven).astype(BF)


def out_project_kernel(where_ref, a0, a1, a2, a3, weight_ref, att_ref, o0, o1, o2, o3, sum_v):
    plane, rank = where_ref[0], where_ref[1] % 4
    span = a0.shape[0]
    for step, ref in enumerate((a0, a1, a2, a3)):
        lanes = pl.ds(pl.multiple_of(lax.rem(plane - step + 4, 4) * 2 * HD, 2 * HD), 2 * HD)
        for row in range(2):
            att_ref[row * span : (row + 1) * span, lanes] = ref[:, row * 2 * HD : (row + 1) * 2 * HD]
    sum_v[...] = dot(att_ref[...], weight_ref[...])
    part = span // 4
    for m, out in enumerate((o0, o1, o2, o3)):
        for row in range(2):
            rows = pl.ds(pl.multiple_of(row * span + (rank ^ m) * part, part), part)
            out[row * part : (row + 1) * part] = sum_v[rows].astype(out.dtype)


def d_att_kernel(where_ref, p0, p1, p2, p3_low, p3_high, weight_ref, branch_ref, heads_ref):
    rank = where_ref[1] % 4
    span = heads_ref.shape[1]
    part = span // 4
    for m, pieces in enumerate(((p0,), (p1,), (p2,), (p3_low, p3_high))):
        for row in range(2):
            rows = pl.ds(pl.multiple_of(row * span + (rank ^ m) * part, part), part)
            if len(pieces) == 2:
                branch_ref[rows] = pieces[row][...]
            else:
                branch_ref[rows] = pieces[0][row * part : (row + 1) * part]
    d_att = dot_rows(branch_ref[...], weight_ref[...])
    low = lax.broadcasted_iota(jnp.int32, heads_ref.shape[1:], 1) < HD
    for z in range(4):
        lanes = slice(z * 2 * HD, (z + 1) * 2 * HD)
        row0, row1 = d_att[:span, lanes], d_att[span:, lanes]
        heads_ref[2 * z] = jnp.where(low, row0, pltpu.roll(row1, HD, 1)).astype(BF)
        heads_ref[2 * z + 1] = jnp.where(low, pltpu.roll(row0, HD, 1), row1).astype(BF)


def d_in_kernel(where_ref, in_ref, weight_ref, near_ref, far_ref, x_v, d_v):
    core, rank = where_ref[1] // 4, where_ref[1] % 4
    reach, wide = in_ref.shape[1], 2 * HD
    features = weight_ref.shape[0]
    low = lax.broadcasted_iota(jnp.int32, (reach, wide), 1) < HD
    for z in range(4):
        for row in range(2):
            x_v[row * reach : (row + 1) * reach, z * wide : (z + 1) * wide] = in_ref[
                z, :, row * wide : (row + 1) * wide
            ]
    for pair in range(2):
        cols = slice((4 + pair) * wide, (5 + pair) * wide)
        one, two = (in_ref[2 * pair + n, :, 2 * wide :].astype(F32) for n in (0, 1))
        x_v[:reach, cols] = jnp.where(low, one, pltpu.roll(two, HD, 1)).astype(BF)
        x_v[reach:, cols] = jnp.where(low, pltpu.roll(one, HD, 1), two).astype(BF)
    part = reach // 8
    span = d_v.shape[1]

    def columns(n, carry):
        cols = pl.ds(pl.multiple_of(n * span, span), span)
        d_v[...] = dot_rows(x_v[...], weight_ref[cols])
        for ref, which in ((near_ref, core), (far_ref, 1 - core)):
            for m in range(4):
                for row in range(2):
                    first = row * reach + which * 4 * part + (rank ^ m) * part
                    rows = pl.ds(pl.multiple_of(first, part), part)
                    ref[m, row * part : (row + 1) * part, cols] = d_v[rows].astype(BF)
        return carry

    lax.fori_loop(0, features // span, columns, 0)


def hidden_kernel(where_ref, *refs, steps, own):
    n_mid, n_out = (10, 2) if own else (1, 4 * len(steps))
    mids, outs, refs = refs[:n_mid], refs[n_mid : n_mid + n_out], refs[n_mid + n_out :]
    gate_ref, up_ref, down_ref = refs[:3]
    refs = refs[3:] if own else refs[7:]
    alls, refs = refs[:4], refs[4:]
    d_mids, acts, refs = (refs[:2], refs[2:4], refs[4:]) if own else ((), (), refs)
    mid_v, out_v, gate_up_v, down_v, act_v, d_gate_v, d_up_v, sem_in, sem_w, sem_out = refs[:10]
    rows, features = mid_v.shape[1:]
    width, tile = down_v.shape[0], 256
    tiles = width // tile
    plane, mine = where_ref[0], where_ref[1]
    core = mine // 4
    shard = gate_ref.shape[1]
    step = rows // 4
    halves = 2 * len(steps)

    def blocks(h):
        base = lax.rem(plane + 4 - steps[h // 2], 4) * (2 * rows)
        return [
            pl.ds(pl.multiple_of(base + (mine ^ (4 * (h % 2) + m)) * step, step), step) for m in range(4)
        ]

    def loads(h):
        slot = h % 2
        if own:
            pieces, out_pieces = mids[5 * h : 5 * h + 5], outs[h : h + 1]
        else:
            pieces = [mids[0].at[block] for block in blocks(h)]
            out_pieces = outs[2 * h : 2 * h + 2]
        found = []
        for held, sources in ((mid_v, pieces), (out_v, out_pieces)):
            at = 0
            for source in sources:
                size = source.shape[0]
                found.append((source, held.at[slot, pl.ds(at, size)]))
                at += size
        return [pltpu.make_async_copy(x, y, sem_in.at[slot, n]) for n, (x, y) in enumerate(found)]

    def stores(h):
        slot = h % 2
        return [
            pltpu.make_async_copy(
                held.at[slot, pl.ds(m * step, step)], target.at[block], sem_out.at[slot, n, m]
            )
            for n, (held, target) in enumerate(zip((act_v, d_gate_v, d_up_v, out_v), alls))
            for m, block in enumerate(blocks(h))
        ]

    def tile_copies(j):
        cols = pl.ds(j * tile, tile)
        found = [
            (ref.at[m, :, cols], gate_up_v.at[g, pl.ds(m * shard, shard), cols])
            for g, ref in enumerate((gate_ref, up_ref))
            for m in range(4)
        ]
        first = pl.multiple_of(core * (down_ref.shape[0] - width) + j * tile, 128)
        found.append((down_ref.at[pl.ds(first, tile)], down_v.at[cols]))
        return [pltpu.make_async_copy(x, y, sem_w.at[j, n]) for n, (x, y) in enumerate(found)]

    def wait_tile(j):
        for copy in weight_copies[j]:
            copy.wait()
        if j == 0:

            @pl.when(core == 1)
            def _():
                gate_up_v[:, :, : 2 * width - down_ref.shape[0]] = jnp.zeros(
                    (2, features, 2 * width - down_ref.shape[0]), BF
                )

    def compute(slot, cols):
        gate = dot(mid_v[slot], gate_up_v[0, :, cols])
        up = dot(mid_v[slot], gate_up_v[1, :, cols])
        d_act = dot_rows(out_v[slot], down_v[cols])
        sig = 1.0 / (1.0 + jnp.exp(-gate))
        silu = gate * sig
        act_v[slot, :, cols] = (silu * up).astype(BF)
        d_gate_v[slot, :, cols] = (d_act * up * (sig + silu * (1.0 - sig))).astype(BF)
        d_up_v[slot, :, cols] = (d_act * silu).astype(BF)

    weight_copies = [tile_copies(j) for j in range(tiles)]
    for copies in [weight_copies[0], loads(0)] + weight_copies[1:] + [loads(1)]:
        for copy in copies:
            copy.start()
    for h in range(halves):
        slot = h % 2
        for copy in loads(h):
            copy.wait()
        if h == 0:
            for j in range(tiles):
                wait_tile(j)
                compute(0, pl.ds(j * tile, tile))
        else:
            compute(slot, pl.ds(0, tile))
            if h + 1 < halves:
                for copy in stores(h - 1):
                    copy.wait()
                for copy in loads(h + 1):
                    copy.start()

            def part(j, carry, slot=slot):
                compute(slot, pl.ds(pl.multiple_of(j * tile, tile), tile))
                return carry

            lax.fori_loop(1, tiles, part, 0)
        for copy in stores(h):
            copy.start()
    left = []
    if own:
        sum_v = refs[10]
        span = 512
        for i in (1, 0):
            for m in range(4):
                part = pl.ds(m * step, step)
                left.append(
                    pltpu.make_async_copy(act_v.at[i, part], acts[i].at[m], sem_out.at[i, 4, m])
                )
                left[-1].start()

            def term(n, carry, i=i):
                cols = pl.ds(pl.multiple_of(n * span, span), span)
                sum_v[i, :, cols] = (
                    dot_rows(d_gate_v[i], gate_up_v[0, cols]) + dot_rows(d_up_v[i], gate_up_v[1, cols])
                ).astype(BF)
                return carry

            lax.fori_loop(0, features // span, term, 0)
            for m in range(4):
                part = pl.ds(m * step, step)
                left.append(
                    pltpu.make_async_copy(sum_v.at[i, part], d_mids[i].at[m], sem_out.at[i, 5, m])
                )
                left[-1].start()
    for h in (halves - 2, halves - 1):
        left += stores(h)
    for copy in left:
        copy.wait()


def hidden_layer(where, mids, outs, weights, total, steps=(0,), before=None):
    own = before is None
    features = outs[0].shape[1]
    rows, width = total // 8, weights[0].shape[2]
    narrow = jax.ShapeDtypeStruct((total, width), BF)
    wide = jax.ShapeDtypeStruct((total, features), BF)
    term = jax.ShapeDtypeStruct((4, rows // 4, features), BF)
    act = jax.ShapeDtypeStruct((4, rows // 4, width), BF)
    held = pltpu.VMEM((2, rows, features), BF)
    small = pltpu.VMEM((2, rows, width), BF)
    dma = pltpu.SemaphoreType.DMA
    count = len(mids) + len(outs)
    kept = [] if own else list(before)
    hbm = pl.BlockSpec(memory_space=pl.ANY)
    found = pl.pallas_call(
        functools.partial(hidden_kernel, steps=steps, own=own),
        in_specs=[pl.BlockSpec(memory_space=pltpu.SMEM)] + [hbm] * (count + 3 + len(kept)),
        out_specs=[hbm] * (8 if own else 4),
        out_shape=[narrow, narrow, narrow, wide] + ([term, term, act, act] if own else []),
        input_output_aliases={count + 4 + n: n for n in range(len(kept))},
        scratch_shapes=[
            held, held,
            pltpu.VMEM((2, features, width), BF),
            pltpu.VMEM((width, features), BF),
            small, small, small,
            dma((2, 9)), dma((width // 256, 9)), dma((2, 6, 4)),
        ]
        + ([held] if own else []),
        compiler_params=pltpu.CompilerParams(vmem_limit_bytes=48 * 2**20),
        cost_estimate=SMALL,
        name="hidden",
    )(where, *mids, *outs, *weights, *kept)
    return list(found[:4]), list(found[4:])


def weight_grad_kernel(left_ref, right_ref, out_ref):
    out_ref[...] = dot_cols(left_ref[...], right_ref[...]).astype(BF)


def weight_grad(left, right):
    tokens, features = left.shape
    width = right.shape[1]
    step = 256
    return pl.pallas_call(
        weight_grad_kernel,
        grid=(features // step,),
        in_specs=[
            pl.BlockSpec((tokens, step), lambda i: (0, i)),
            pl.BlockSpec((tokens, width), lambda i: (0, 0), pipeline_mode=pl.Buffered(1)),
        ],
        out_specs=pl.BlockSpec((step, width), lambda i: (i, 0)),
        out_shape=jax.ShapeDtypeStruct((features, width), BF),
        compiler_params=pltpu.CompilerParams(vmem_limit_bytes=48 * 2**20),
        cost_estimate=SMALL,
        name="weight_grad",
    )(left, right)


def place_columns_kernel(where_ref, own_ref, other_ref, *rest):
    out_ref = rest[-1]
    wide = own_ref.shape[-1]
    extra = out_ref.shape[-1] - wide

    @pl.when(where_ref[0] == 0)
    def _():
        out_ref[:, :wide] = own_ref[...].astype(F32)
        out_ref[:, wide:] = other_ref[:, wide - extra :].astype(F32)

    @pl.when(where_ref[0] == 1)
    def _():
        out_ref[:, :wide] = other_ref[...].astype(F32)
        out_ref[:, wide:] = own_ref[:, wide - extra :].astype(F32)


def place_columns(core, own, other, before, chip_width, kind):
    chips, rows, wide = own.shape
    cut = rows // 2
    half = pl.BlockSpec((None, cut, wide), lambda chip, b, core: (chip, b, 0))
    return pl.pallas_call(
        place_columns_kernel,
        grid_spec=pltpu.PrefetchScalarGridSpec(
            num_scalar_prefetch=1,
            grid=(chips, rows // cut),
            in_specs=[half, half] + ([] if before is None else [pl.BlockSpec(memory_space=pl.ANY)]),
            out_specs=pl.BlockSpec((cut, chip_width), lambda chip, b, core: (b, kind * chips + chip)),
        ),
        out_shape=jax.ShapeDtypeStruct((rows, 2 * chips * chip_width), F32),
        input_output_aliases={} if before is None else {3: 0},
        compiler_params=pltpu.CompilerParams(vmem_limit_bytes=32 * 2**20),
        cost_estimate=SMALL,
        name="place_columns",
    )(core, own, other, *([] if before is None else [before]))


def place_down_kernel(core_ref, own_ref, other_ref, out_ref, *, lead):
    first = pl.program_id(0) < lead
    mine = first == (core_ref[0] == 0)

    @pl.when(mine)
    def _():
        out_ref[...] = own_ref[...].astype(F32)

    @pl.when(jnp.logical_not(mine))
    def _():
        out_ref[...] = other_ref[...].astype(F32)


def place_down(core, own, other, total):
    width, features = own.shape
    step = 128
    count, lead = total // step, width // step
    skip = 2 * lead - count

    def block(of_core):
        def index(i, core):
            which = core[0] if of_core else 1 - core[0]
            return (jnp.where(which == 0, jnp.minimum(i, lead - 1), jnp.maximum(i - lead + skip, 0)), 0)

        return pl.BlockSpec((step, features), index)

    return pl.pallas_call(
        functools.partial(place_down_kernel, lead=lead),
        grid_spec=pltpu.PrefetchScalarGridSpec(
            num_scalar_prefetch=1,
            grid=(count,),
            in_specs=[block(True), block(False)],
            out_specs=pl.BlockSpec((step, features), lambda i, core: (i, 0)),
        ),
        out_shape=jax.ShapeDtypeStruct((total, features), F32),
        cost_estimate=SMALL,
        name="place_down",
    )(core, own, other)


def place_qkv_kernel(where_ref, own_ref, other_ref, out_ref):
    cut = own_ref.shape[2]
    core = where_ref[0]
    for ref, half in ((own_ref, core), (other_ref, 1 - core)):
        rows = pl.ds(pl.multiple_of(half * cut, cut), cut)
        for z in range(4):
            out_ref[rows, z * 2 * HD : (z + 1) * 2 * HD] = ref[z, 0].astype(F32)


def place_qkv(where, own, other):
    _, _, cut, wide = own.shape
    parts = wide // (2 * HD)
    piece = pl.BlockSpec((4, 1, cut, 2 * HD), lambda part, chip, where: (0, chip, 0, part))
    return pl.pallas_call(
        place_qkv_kernel,
        grid_spec=pltpu.PrefetchScalarGridSpec(
            num_scalar_prefetch=1,
            grid=(parts, 4),
            in_specs=[piece, piece],
            out_specs=pl.BlockSpec((2 * cut, 8 * HD), lambda part, chip, where: (0, part * 4 + chip)),
        ),
        out_shape=jax.ShapeDtypeStruct((2 * cut, parts * 32 * HD), F32),
        cost_estimate=SMALL,
        name="place_qkv",
    )(where, own, other)


def tie(*values):
    return lax.optimization_barrier(values)


def plane_plan(
    inputs,
    segments,
    norm1_gain,
    norm1_bias,
    qkv_weight,
    qkv_bias,
    out_weight,
    norm2_gain,
    norm2_bias,
    gate_up_weight,
    down_weight,
    cotangent,
):
    row_count, local_len, features = inputs.shape
    row_len = segments.shape[1]
    tokens = row_count * local_len
    plane, core, rank = lax.axis_index("z"), lax.axis_index("core"), lax.axis_index("fsdp")
    seq = plane * 2 + core
    own = core * 4 + rank
    shard = features // 4
    hidden = gate_up_weight.shape[1] // 2
    chip_width = hidden // 4
    width = -(-chip_width // 256) * 128
    tables = turn_tables(row_len)
    split = jnp.sum((segments == 0).astype(jnp.int32), axis=1)
    where = jnp.stack([plane, own]).astype(jnp.int32)

    head_all = exchange(pick_heads(where, qkv_weight)).reshape(features, 12 * HD)
    value = lax.dynamic_slice_in_dim(head_all, 8 * HD + plane * HD, HD, 1)
    head_weight = jnp.concatenate(
        [lax.dynamic_slice_in_dim(head_all, plane * 2 * HD, 2 * HD, 1), value, value], axis=1
    )
    head_first = (rank * 8 + seq) * HD
    bias_parts = [
        lax.dynamic_slice_in_dim(qkv_bias, head_first + part * features, HD, 0) for part in (0, 1, 2)
    ]
    head_bias = jnp.concatenate(bias_parts + bias_parts[2:])
    hidden_first = core * (chip_width - width)

    def hidden_columns(kind):
        firsts = [hidden_first + chip * chip_width + kind * hidden for chip in range(4)]
        return jnp.stack([lax.dynamic_slice_in_dim(gate_up_weight, first, width, 1) for first in firsts])

    gate_weight, up_weight = hidden_columns(0), hidden_columns(1)

    flat = inputs.reshape(tokens, features).astype(F32)
    normed_in, norm1_back = jax.vjp(layer_norm, flat, norm1_gain, norm1_bias)
    everywhere = ("z", "core", "fsdp")
    in_all = lax.all_gather(normed_in.astype(BF), everywhere, axis=0, tiled=True)
    d_out = cotangent.reshape(tokens, features)
    out_near = jnp.concatenate(gather_near(d_out), axis=0)
    out_far = swap(out_near, 4)
    in_all, out_near, out_far, gate_weight, up_weight, head_weight, head_all, *tables = tie(
        in_all, out_near, out_far, gate_weight, up_weight, head_weight, head_all, *tables
    )
    lows, highs = [out_near[: 2 * tokens]], [out_near[2 * tokens :]]

    mixed = (dot(in_all, head_weight) + head_bias).reshape(
        row_len // local_len, row_count, local_len, 4 * HD
    )
    q, k, v, out_heads, logs, mine, theirs, gate_weight, low, up_weight = tie(
        *attend(split, where, mixed, tables), exchange(gate_weight), shift(lows[0], 1), up_weight
    )
    lows.append(low)
    span = row_len // 8
    pair = jax.ShapeDtypeStruct((span, 4 * HD), BF)
    pairs = small_call(pair_kernel, "pair", [pair] * 4, where, mine, swap(theirs, 4))
    arrived = [pairs[0]] + [shift(pairs[n], n) for n in (1, 2, 3)]
    square = row_count * span
    block = jax.ShapeDtypeStruct((tokens, features), BF)
    blocks = jax.ShapeDtypeStruct((4, tokens, features), BF)
    att, *branch = small_call(
        out_project_kernel,
        "out_project",
        [jax.ShapeDtypeStruct((square, shard), BF), jax.ShapeDtypeStruct((tokens, features), F32)]
        + [block] * 3,
        where,
        *arrived,
        out_weight,
        scratch=[pltpu.VMEM((square, features), F32)],
    )
    branch_sum, up_weight, high = tie(sum_quad(branch), exchange(up_weight), shift(highs[0], 1))
    highs.append(high)
    hidden_weights = [gate_weight, up_weight, down_weight]
    middle = flat + branch_sum
    normed_mid, norm2_back = jax.vjp(layer_norm, middle, norm2_gain, norm2_bias)
    mid_low = normed_mid.astype(BF)

    mid_pieces = gather_pieces(mid_low)
    *mid_pieces, mid_own, low = tie(*mid_pieces, mid_low, shift(lows[1], 1))
    lows.append(low)
    mid_all = lax.all_gather(mid_own, everywhere, axis=0, tiled=True)
    total = row_count * row_len
    hidden_all, (d_near, d_far, act_near, act_far) = hidden_layer(
        where, mid_pieces, [out_near, out_far], hidden_weights, total
    )
    d_near, d_far, high = tie(d_near, d_far, shift(highs[1], 1))
    highs.append(high)
    d_norm_mid, low = tie(sum_plane(d_near, d_far), shift(lows[2], 1))
    lows.append(low)
    d_middle_part, d_gain_two, d_bias_two = norm2_back(d_norm_mid)
    d_middle = d_out.astype(F32) + d_middle_part

    d_pieces = gather_near(d_middle.astype(BF))
    d_pieces[4], high = tie(d_pieces[4], shift(highs[2], 1))
    highs.append(high)
    d_branch, d_heads = small_call(
        d_att_kernel,
        "d_att",
        [
            jax.ShapeDtypeStruct((square, features), BF),
            jax.ShapeDtypeStruct((8, span, 2 * HD), BF),
        ],
        where,
        *d_pieces,
        out_weight,
    )
    d_heads = exchange(d_heads, ("z", "core")).reshape(row_len, 2 * HD)
    log_rows = jnp.stack([logs[:, 0], logs[:, HD]])
    d_mixed, d_packed = attend_back(
        split, q, k, v, k.T, out_heads, d_heads, log_rows, tables, local_len
    )
    d_packed, d_mixed, mid_all = tie(d_packed, d_mixed, mid_all)

    arrived = exchange(d_packed.reshape(4, row_len // 4, 6 * HD), "z")
    d_mixed = d_mixed.reshape(row_len * row_count, 4 * HD)
    head_grad = dot_cols(in_all, d_mixed)[:, : 3 * HD].astype(BF)
    down = lax.dynamic_slice_in_dim(down_weight, hidden_first, width, 0)
    result_sum = sum_plane(
        dot(act_near.reshape(4 * tokens, width), down).reshape(4, tokens, features),
        dot(act_far.reshape(4 * tokens, width), down).astype(BF).reshape(4, tokens, features),
    )

    def rest(steps, before):
        outs = [
            piece for n in steps for piece in (lows[n], highs[n], swap(lows[n], 4), swap(highs[n], 4))
        ]
        return hidden_layer(where, [mid_all], outs, hidden_weights, total, steps, before)[0]

    hidden_all = rest((1, 2), hidden_all)
    arrived, result_sum, head_grad, att, d_branch, *hidden_all = tie(
        arrived, result_sum, head_grad, att, d_branch, *hidden_all
    )
    result = middle + result_sum
    near, far = small_call(
        d_in_kernel,
        "d_in",
        [blocks] * 2,
        where,
        arrived,
        head_all,
        scratch=[
            pltpu.VMEM((8 * tokens, 12 * HD), BF),
            pltpu.VMEM((8 * tokens, 512), F32),
        ],
        limit=48,
    )
    cut = shard // 2
    head_grad = head_grad.reshape(4, 2, cut, 3 * HD)
    mine = lax.dynamic_index_in_dim(head_grad, core, 1, keepdims=False)
    theirs = swap(lax.dynamic_index_in_dim(head_grad, 1 - core, 1, keepdims=False), 4)
    first, second = jnp.where(core == 0, mine, theirs), jnp.where(core == 0, theirs, mine)
    pairs = jnp.concatenate(
        [half[:, :, p * HD : (p + 1) * HD] for p in range(3) for half in (first, second)], axis=2
    )
    heads = lax.all_gather(exchange(pairs), "z", axis=0)

    out_part = dot_cols(att, d_branch).astype(BF)
    out_part = lax.psum_scatter(out_part, ("z", "core"), scatter_dimension=0, tiled=True)
    out_rows = lax.all_gather(out_part, ("z", "core"), axis=0, tiled=True)

    far, near, *hidden_all = tie(swap(far, 4), near, *hidden_all)
    hidden_all = rest((3,), hidden_all)
    act_all, d_gate_all, d_up_all, out_all = hidden_all
    d_norm_in, d_gate_all = tie(
        sum_quad([near[m].astype(F32) + far[m].astype(F32) for m in range(4)]), d_gate_all
    )
    d_flat_part, d_gain_one, d_bias_one = norm1_back(d_norm_in)
    d_inputs = d_middle + d_flat_part

    bias_sum = jnp.sum(d_mixed.astype(F32), axis=0)
    bias_own = jnp.zeros((3 * features,), F32)
    for part in range(3):
        bias_own = lax.dynamic_update_slice_in_dim(
            bias_own, bias_sum[part * HD : (part + 1) * HD], head_first + part * features, 0
        )
    sums = jnp.concatenate([d_gain_one, d_bias_one, bias_own, d_gain_two, d_bias_two])
    sums = sums + swap(sums, 4)
    sums = sums + sum(swap(sums, m) for m in (1, 2, 3))

    d_gate_grad, sums, d_up_all = tie(
        weight_grad(mid_all, d_gate_all), sums + sum(shift(sums, n) for n in (1, 2, 3)), d_up_all
    )
    by_chip = (4, shard, width)
    gate_parts, d_up_grad, act_all, out_rows, heads = tie(
        exchange(d_gate_grad.reshape(by_chip)),
        weight_grad(mid_all, d_up_all),
        act_all,
        out_rows,
        heads,
    )
    core_index = core.reshape(1).astype(jnp.int32)
    up_parts, down_own, gate_up_grad = tie(
        exchange(d_up_grad.reshape(by_chip)),
        weight_grad(act_all, out_all),
        place_columns(core_index, gate_parts, swap(gate_parts, 4), None, chip_width, 0),
    )
    down_grad = place_down(core_index, down_own, swap(down_own, 4), chip_width)
    qkv_grad = place_qkv(core_index, heads, swap(heads, 4))
    out_grad = out_rows.astype(F32)
    gate_up_grad = place_columns(
        core_index, up_parts, swap(up_parts, 4), gate_up_grad, chip_width, 1
    )
    return (
        result.reshape(row_count, local_len, features),
        d_inputs.reshape(row_count, local_len, features),
        sums[:features],
        sums[features : 2 * features],
        qkv_grad,
        sums[2 * features : 5 * features],
        out_grad,
        sums[5 * features : 6 * features],
        sums[6 * features :],
        gate_up_grad,
        down_grad,
    )


def solution(mesh):
    planes = (mesh.shape["seq"], mesh.shape["fsdp"]) == (8, 4)
    plan = plane_plan if planes else general_plan
    if planes:
        mesh = jax.sharding.Mesh(mesh.devices.reshape(4, 2, 4), ("z", "core", "fsdp"))
    spread = P(None, (*mesh.axis_names,), None)
    placed = (
        spread,
        P(),
        P(),
        P(),
        P("fsdp", None),
        P(),
        P("fsdp", None),
        P(),
        P(),
        P("fsdp", None),
        P("fsdp", None),
        spread,
    )
    return jax.shard_map(
        plan,
        mesh=mesh,
        in_specs=placed,
        out_specs=(
            spread,
            spread,
            P(),
            P(),
            P("fsdp", None),
            P(),
            P("fsdp", None),
            P(),
            P(),
            P("fsdp", None),
            P("fsdp", None),
        ),
        check_vma=False,
    )
```

```python
import functools

import jax
import jax.numpy as jnp
from jax import lax
from jax.experimental import pallas as pl
from jax.experimental.pallas import tpu as pltpu
from jax.sharding import PartitionSpec as P

HD = 64
ROT = 16


EPSILON = 1e-05
MASKED = -1e30


def layer_norm(values, norm_gain, offset):
    average = jnp.mean(values, axis=-1, keepdims=True)
    centred = values - average
    variance = jnp.mean(centred * centred, axis=-1, keepdims=True)
    return centred * lax.rsqrt(variance + EPSILON) * norm_gain + offset


def rotate(values, positions):
    half_rot = ROT // 2
    exponent = jnp.arange(half_rot, dtype=jnp.float32) * (2.0 / ROT)
    inverse = jnp.power(jnp.float32(10000.0), -exponent)
    angles = positions.astype(jnp.float32)[:, None] * inverse[None, :]
    cosine = jnp.cos(angles)[:, None, :]
    sine = jnp.sin(angles)[:, None, :]
    first = values[:, :, :half_rot]
    second = values[:, :, half_rot:ROT]
    return jnp.concatenate(
        [first * cosine - second * sine, second * cosine + first * sine, values[:, :, ROT:]], axis=2
    )


def fold_rows(left, shard):
    return jnp.dot(
        left, lax.all_gather(shard, "fsdp", axis=0, tiled=True), preferred_element_type=jnp.float32
    )


def map_back(grad_rows, shard):
    return lax.dot_general(
        grad_rows,
        lax.all_gather(shard, "fsdp", axis=0, tiled=True),
        (((1,), (1,)), ((), ())),
        preferred_element_type=jnp.float32,
    )


def grad_joint(left, right_side):
    seq_count = lax.axis_size("seq")
    fsdp_count = lax.axis_size("fsdp")
    token_count, total_rows = left.shape
    share = total_rows // (seq_count * fsdp_count)
    permuted = (
        left.reshape(token_count, fsdp_count, seq_count, share)
        .transpose(0, 2, 1, 3)
        .reshape(token_count, total_rows)
    )
    return lax.psum_scatter(
        lax.dot_general(
            permuted, right_side, (((0,), (0,)), ((), ())), preferred_element_type=jnp.float32
        ),
        ("seq", "fsdp"),
        scatter_dimension=0,
        tiled=True,
    )


def general_plan(
    inputs,
    segments,
    norm1_gain,
    norm1_bias,
    qkv_weight,
    qkv_bias,
    out_weight,
    norm2_gain,
    norm2_bias,
    gate_up_weight,
    down_weight,
    cotangent,
):
    row_count, local_len, features = inputs.shape
    fsdp_count = lax.axis_size("fsdp")
    fsdp_rank = lax.axis_index("fsdp")
    block_rank = lax.axis_index("seq") * fsdp_count + fsdp_rank
    token_count = row_count * local_len
    head_count = features // HD
    ff_width = gate_up_weight.shape[1] // 2
    scale_factor = HD ** (-0.5)
    flat = inputs.reshape(token_count, features).astype(jnp.float32)
    local_pos = block_rank * local_len + jnp.arange(local_len, dtype=jnp.int32)
    positions = jnp.tile(local_pos, row_count)
    weight_set = (qkv_weight, out_weight, gate_up_weight, down_weight)

    def forward_product(left, slot_index):
        return fold_rows(left, weight_set[slot_index])

    def backward_product(grad_rows, slot_index):
        return map_back(grad_rows, weight_set[slot_index])

    normed_in, norm1_back = jax.vjp(layer_norm, flat, norm1_gain, norm1_bias)
    in_low = normed_in.astype(jnp.bfloat16)
    mixed = forward_product(in_low, 0) + qkv_bias
    turn_input = mixed[:, : 2 * features].reshape(token_count, 2 * head_count, HD)
    turned, turn_back = jax.vjp(lambda values: rotate(values, positions), turn_input)
    turned_low = turned.astype(jnp.bfloat16)
    queries = turned_low[:, :head_count].reshape(row_count, local_len, features)
    keys_loc = turned_low[:, head_count:].reshape(row_count, local_len, features)
    values_loc = (
        mixed[:, 2 * features :].astype(jnp.bfloat16).reshape(row_count, local_len, features)
    )
    head_query, head_key, head_value = (
        lax.all_to_all(queries, "seq", split_axis=2, concat_axis=1, tiled=True),
        lax.all_to_all(keys_loc, "seq", split_axis=2, concat_axis=1, tiled=True),
        lax.all_to_all(values_loc, "seq", split_axis=2, concat_axis=1, tiled=True),
    )
    all_keys, all_values = (
        lax.all_gather(head_key, "fsdp", axis=1, tiled=True),
        lax.all_gather(head_value, "fsdp", axis=1, tiled=True),
    )
    query_len = head_query.shape[1]
    key_len = all_keys.shape[1]
    head_width = head_query.shape[2]
    local_heads = head_width // HD
    query_four = head_query.reshape(row_count, query_len, local_heads, HD)
    keys_four = all_keys.reshape(row_count, key_len, local_heads, HD)
    values_four = all_values.reshape(row_count, key_len, local_heads, HD)
    query_index = jnp.arange(query_len, dtype=jnp.int32)
    query_pos = (
        query_index // local_len * fsdp_count + fsdp_rank
    ) * local_len + query_index % local_len
    key_index = jnp.arange(key_len, dtype=jnp.int32)
    key_pos = (
        key_index % query_len // local_len * fsdp_count + key_index // query_len
    ) * local_len + key_index % local_len
    query_seg = jnp.take(segments, query_pos, axis=1)
    key_seg = jnp.take(segments, key_pos, axis=1)
    span = min(512, key_len)
    block_count = key_len // span

    def block_inputs(block_index):
        first_row = block_index * span
        block_keys = lax.dynamic_slice_in_dim(keys_four, first_row, span, 1)
        block_values = lax.dynamic_slice_in_dim(values_four, first_row, span, 1)
        block_pos = lax.dynamic_slice_in_dim(key_pos, first_row, span, 0)
        block_seg = lax.dynamic_slice_in_dim(key_seg, first_row, span, 1)
        allowed = (query_seg[:, :, None] == block_seg[:, None, :]) & (
            block_pos[None, None, :] <= query_pos[None, :, None]
        )
        scores = (
            jnp.einsum(
                "rqhd,rkhd->rhqk", query_four, block_keys, preferred_element_type=jnp.float32
            )
            * scale_factor
        )
        return (first_row, block_keys, block_values, allowed[:, None], scores)

    def forward_block(carry, block_index):
        row_top, running, weighted = carry
        first_row, block_keys, block_values, allowed, scores = block_inputs(block_index)
        new_top = jnp.maximum(row_top, jnp.max(jnp.where(allowed, scores, MASKED), axis=-1))
        probs = jnp.where(allowed, jnp.exp(scores - new_top[..., None]), 0.0)
        factor = jnp.exp(row_top - new_top)
        running = running * factor + jnp.sum(probs, axis=-1)
        weighted = weighted * factor[..., None] + jnp.einsum(
            "rhqk,rkhd->rhqd",
            probs.astype(jnp.bfloat16),
            block_values,
            preferred_element_type=jnp.float32,
        )
        return ((new_top, running, weighted), None)

    start_top = jnp.full((row_count, local_heads, query_len), MASKED, jnp.float32)
    start_total = jnp.zeros((row_count, local_heads, query_len), jnp.float32)
    start_weighted = jnp.zeros((row_count, local_heads, query_len, HD), jnp.float32)
    (row_top, running, weighted), _ = lax.scan(
        forward_block, (start_top, start_total, start_weighted), jnp.arange(block_count)
    )
    log_total = row_top + jnp.log(running)
    attended_heads = (
        (weighted / running[..., None])
        .transpose(0, 2, 1, 3)
        .reshape(row_count, query_len, head_width)
        .astype(jnp.bfloat16)
    )
    attended_loc = lax.all_to_all(attended_heads, "seq", split_axis=1, concat_axis=2, tiled=True)
    att_flat = attended_loc.reshape(token_count, features)
    middle = flat + forward_product(att_flat, 1)
    normed_mid, norm2_back = jax.vjp(layer_norm, middle, norm2_gain, norm2_bias)
    mid_low = normed_mid.astype(jnp.bfloat16)
    gate_up = forward_product(mid_low, 2)
    act_value, silu_back = jax.vjp(
        lambda gate_part, up_part: jax.nn.silu(gate_part) * up_part,
        gate_up[:, :ff_width],
        gate_up[:, ff_width:],
    )
    act_low = act_value.astype(jnp.bfloat16)
    result = middle + forward_product(act_low, 3)
    d_out = cotangent.reshape(token_count, features)
    d_act = backward_product(d_out, 3)
    d_gate, d_up = silu_back(d_act)
    d_gate_up = jnp.concatenate([d_gate, d_up], axis=1).astype(jnp.bfloat16)
    d_mid_norm = backward_product(d_gate_up, 2)
    d_middle_part, d_gain_two, d_bias_two = norm2_back(d_mid_norm)
    d_middle = d_out.astype(jnp.float32) + d_middle_part
    d_branch = d_middle.astype(jnp.bfloat16)
    d_attended = (
        backward_product(d_branch, 1).astype(jnp.bfloat16).reshape(row_count, local_len, features)
    )
    d_heads = lax.all_to_all(d_attended, "seq", split_axis=2, concat_axis=1, tiled=True)
    d_heads_four = d_heads.reshape(row_count, query_len, local_heads, HD)
    attended_four = attended_heads.reshape(row_count, query_len, local_heads, HD)
    delta = jnp.einsum(
        "rqhd,rqhd->rhq", d_heads_four.astype(jnp.float32), attended_four.astype(jnp.float32)
    )

    def backward_block(carry, block_index):
        d_query, d_keys_all, d_values_all = carry
        first_row, block_keys, block_values, allowed, scores = block_inputs(block_index)
        probs = jnp.where(allowed, jnp.exp(scores - log_total[..., None]), 0.0)
        d_block_values = jnp.einsum(
            "rhqk,rqhd->rkhd",
            probs.astype(jnp.bfloat16),
            d_heads_four,
            preferred_element_type=jnp.float32,
        )
        d_probs = jnp.einsum(
            "rqhd,rkhd->rhqk", d_heads_four, block_values, preferred_element_type=jnp.float32
        )
        d_scores = (probs * (d_probs - delta[..., None])).astype(jnp.bfloat16)
        d_query = (
            d_query
            + jnp.einsum(
                "rhqk,rkhd->rqhd", d_scores, block_keys, preferred_element_type=jnp.float32
            )
            * scale_factor
        )
        d_block_keys = (
            jnp.einsum("rhqk,rqhd->rkhd", d_scores, query_four, preferred_element_type=jnp.float32)
            * scale_factor
        )
        d_keys_all = lax.dynamic_update_slice_in_dim(d_keys_all, d_block_keys, first_row, 1)
        d_values_all = lax.dynamic_update_slice_in_dim(d_values_all, d_block_values, first_row, 1)
        return ((d_query, d_keys_all, d_values_all), None)

    zero_query = jnp.zeros((row_count, query_len, local_heads, HD), jnp.float32)
    zero_keys = jnp.zeros((row_count, key_len, local_heads, HD), jnp.float32)
    (d_query, d_keys_all, d_values_all), _ = lax.scan(
        backward_block, (zero_query, zero_keys, zero_keys), jnp.arange(block_count)
    )
    d_keys_sum, d_values_sum = (
        lax.psum_scatter(
            d_keys_all.reshape(row_count, key_len, head_width).astype(jnp.bfloat16),
            "fsdp",
            scatter_dimension=1,
            tiled=True,
        ).astype(jnp.float32),
        lax.psum_scatter(
            d_values_all.reshape(row_count, key_len, head_width).astype(jnp.bfloat16),
            "fsdp",
            scatter_dimension=1,
            tiled=True,
        ).astype(jnp.float32),
    )
    d_query_low = d_query.reshape(row_count, query_len, head_width).astype(jnp.bfloat16)
    dq_back, dk_back, dv_back = (
        lax.all_to_all(d_query_low, "seq", split_axis=1, concat_axis=2, tiled=True),
        lax.all_to_all(
            d_keys_sum.astype(jnp.bfloat16), "seq", split_axis=1, concat_axis=2, tiled=True
        ),
        lax.all_to_all(
            d_values_sum.astype(jnp.bfloat16), "seq", split_axis=1, concat_axis=2, tiled=True
        ),
    )
    d_turned = jnp.concatenate(
        [
            dq_back.reshape(token_count, head_count, HD),
            dk_back.reshape(token_count, head_count, HD),
        ],
        axis=1,
    ).astype(jnp.float32)
    (d_turn_input,) = turn_back(d_turned)
    d_mixed = jnp.concatenate(
        [
            d_turn_input.reshape(token_count, 2 * features),
            dv_back.reshape(token_count, features).astype(jnp.float32),
        ],
        axis=1,
    ).astype(jnp.bfloat16)
    d_qkv_bias = jnp.sum(d_mixed.astype(jnp.float32), axis=0)
    d_norm_in = backward_product(d_mixed, 0)
    d_flat_part, d_gain_one, d_bias_one = norm1_back(d_norm_in)
    d_inputs = d_middle + d_flat_part
    first_grad = grad_joint(in_low, d_mixed)
    second_grad = grad_joint(att_flat, d_branch)
    third_grad = grad_joint(mid_low, d_gate_up)
    fourth_grad = grad_joint(act_low, d_out)
    qkv_grad, out_grad, gate_up_grad, down_grad = (
        lax.all_gather(first_grad.astype(jnp.bfloat16), "seq", axis=0, tiled=True).astype(
            first_grad.dtype
        ),
        lax.all_gather(second_grad.astype(jnp.bfloat16), "seq", axis=0, tiled=True).astype(
            second_grad.dtype
        ),
        lax.all_gather(third_grad.astype(jnp.bfloat16), "seq", axis=0, tiled=True).astype(
            third_grad.dtype
        ),
        lax.all_gather(fourth_grad.astype(jnp.bfloat16), "seq", axis=0, tiled=True).astype(
            fourth_grad.dtype
        ),
    )
    gain_one, bias_one, bias_qkv, gain_two, bias_two = lax.psum(
        (d_gain_one, d_bias_one, d_qkv_bias, d_gain_two, d_bias_two), ("seq", "fsdp")
    )
    return (
        result.reshape(row_count, local_len, features),
        d_inputs.reshape(row_count, local_len, features),
        gain_one,
        bias_one,
        qkv_grad,
        bias_qkv,
        out_grad,
        gain_two,
        bias_two,
        gate_up_grad,
        down_grad,
    )


BLOCK = 512
BF = jnp.bfloat16
F32 = jnp.float32
SMALL = pl.CostEstimate(flops=1000, bytes_accessed=1000, transcendentals=0)


def swap(value, mask):
    return lax.ppermute(value, ("z", "core", "fsdp"), [(i, i ^ mask) for i in range(32)])


def shift(value, steps):
    return lax.ppermute(value, ("z", "core", "fsdp"), [(i, (i + 8 * steps) % 32) for i in range(32)])


def pick(stacked, index):
    return lax.dynamic_index_in_dim(stacked, index, 0, keepdims=False)


def exchange(value, axis="fsdp"):
    return lax.all_to_all(value, axis, split_axis=0, concat_axis=0, tiled=True)


def gather_near(value):
    half = value.shape[0] // 2
    by_x = swap(value, 1)
    by_y = swap(value, 2)
    return [value, by_x, by_y, swap(by_x[:half], 2), swap(by_y[half:], 1)]


def both_cores(near):
    return near + [swap(piece, 4) for piece in near]


def gather_pieces(value):
    return both_cores(gather_near(value))


def sum_quad(terms):
    return terms[0].astype(F32) + sum(swap(terms[m].astype(BF), m).astype(F32) for m in (1, 2, 3))


def sum_plane(near, far):
    arrived = swap(far.astype(BF), 4)
    return sum_quad([near[m].astype(F32) + arrived[m].astype(F32) for m in range(4)])


def dot(left, right):
    return jnp.dot(left, right, preferred_element_type=F32)


def dot_rows(left, right):
    return lax.dot_general(left, right, (((1,), (1,)), ((), ())), preferred_element_type=F32)


def dot_cols(left, right):
    return lax.dot_general(left, right, (((0,), (0,)), ((), ())), preferred_element_type=F32)


def turn_tables(row_len):
    half_rot = ROT // 2
    lane = jnp.arange(2 * HD, dtype=jnp.int32) % HD
    exponent = (lane % half_rot).astype(F32) * (2.0 / ROT)
    inverse = jnp.power(jnp.float32(10000.0), -exponent)
    angles = jnp.arange(row_len, dtype=jnp.int32).astype(F32)[:, None] * inverse[None, :]
    cosine = jnp.where(lane < ROT, jnp.cos(angles), 1.0)
    sine = jnp.sin(angles)
    ahead = jnp.where(lane < half_rot, -sine, 0.0)
    behind = jnp.where((lane >= half_rot) & (lane < ROT), sine, 0.0)
    return cosine, ahead, behind


def attend_kernel(
    split_ref, where_ref, mixed_ref, cos_ref, ahead_ref, behind_ref,
    q_ref, k_ref, v_ref, o_ref, log_ref, mine_ref, theirs_ref, kz, vz,
):
    local_len = mixed_ref.shape[2]
    row_len = q_ref.shape[0]
    low = lax.broadcasted_iota(jnp.int32, (local_len, 2 * HD), 1) < HD

    def prepare(i, carry):
        rows = pl.ds(pl.multiple_of(i * local_len, local_len), local_len)
        cosine, ahead, behind = cos_ref[rows], ahead_ref[rows], behind_ref[rows]

        def turn(x):
            return (
                x * cosine
                + pltpu.roll(x, 2 * HD - ROT // 2, 1) * ahead
                + pltpu.roll(x, ROT // 2, 1) * behind
            )

        first = mixed_ref[i, 0]
        second = mixed_ref[i, 1]
        turned0 = turn(first[:, : 2 * HD])
        turned1 = turn(second[:, : 2 * HD])
        q = jnp.where(low, turned0, pltpu.roll(turned1, HD, 1))
        k = jnp.where(low, pltpu.roll(turned0, HD, 1), turned1)
        v = jnp.where(low, first[:, 2 * HD :], second[:, 2 * HD :])
        q_ref[rows] = (q * HD**-0.5).astype(BF)
        k_ref[rows] = k.astype(BF)
        v_ref[rows] = v.astype(BF)
        kz[0, rows] = jnp.where(low, k, 0.0).astype(BF)
        kz[1, rows] = jnp.where(low, 0.0, k).astype(BF)
        vz[0, rows] = jnp.where(low, v, 0.0).astype(BF)
        vz[1, rows] = jnp.where(low, 0.0, v).astype(BF)
        return carry

    lax.fori_loop(0, row_len // local_len, prepare, 0)
    t_in = lax.broadcasted_iota(jnp.int32, (BLOCK, 1), 0)
    u_in = lax.broadcasted_iota(jnp.int32, (1, BLOCK), 1)
    low_q = lax.broadcasted_iota(jnp.int32, (BLOCK, 2 * HD), 1) < HD

    def query_block(qb, carry):
        rows = pl.ds(pl.multiple_of(qb * BLOCK, BLOCK), BLOCK)
        q = q_ref[rows]
        t = t_in + qb * BLOCK
        outs, logs = [], []
        for row in range(2):
            split = split_ref[row]
            start = jnp.where(t >= split, split, 0)

            def step(kb, state, diagonal, row=row, start=start):
                top, total, acc = state
                keys = pl.ds(pl.multiple_of(kb * BLOCK, BLOCK), BLOCK)
                u = u_in + kb * BLOCK
                scores = dot_rows(q, kz[row, keys])
                allowed = u >= start
                if diagonal:
                    allowed = allowed & (u <= t)
                scores = jnp.where(allowed, scores, MASKED)
                new_top = jnp.maximum(top, jnp.max(scores, axis=1, keepdims=True))
                probs = jnp.exp(scores - new_top)
                factor = jnp.exp(top - new_top)
                total = total * factor + jnp.sum(probs, axis=1, keepdims=True)
                acc = acc * factor + dot(probs.astype(BF), vz[row, keys])
                return new_top, total, acc

            state = (
                jnp.full((BLOCK, 1), MASKED, F32),
                jnp.zeros((BLOCK, 1), F32),
                jnp.zeros((BLOCK, 2 * HD), F32),
            )
            first_kb = jnp.where(qb * BLOCK >= split, split // BLOCK, 0)
            state = lax.fori_loop(
                first_kb, qb, lambda kb, state, step=step: step(kb, state, False), state
            )
            top, total, acc = step(qb, state, True)
            outs.append(acc / total)
            logs.append(top + jnp.log(total))
        o_ref[rows] = (outs[0] + outs[1]).astype(BF)
        turned = jnp.where(low_q, logs[0], logs[1]).T
        log_ref[0:1, rows] = turned[0:1]
        log_ref[1:2, rows] = turned[HD : HD + 1]
        step = lax.rem(qb - where_ref[0] + 4, 4)
        core = where_ref[1] // 4
        half = BLOCK // 2
        for ref, which in ((mine_ref, core), (theirs_ref, 1 - core)):
            ref[step] = o_ref[pl.ds(pl.multiple_of(qb * BLOCK + which * half, half), half)]
        return carry

    lax.fori_loop(0, row_len // BLOCK, query_block, 0)


def attend(split, where, mixed, tables):
    row_len = tables[0].shape[0]
    packed = jax.ShapeDtypeStruct((row_len, 2 * HD), BF)
    smem = pl.BlockSpec(memory_space=pltpu.SMEM)
    vmem = pl.BlockSpec(memory_space=pltpu.VMEM)
    pairs = 2 * row_len * row_len // 2
    return pl.pallas_call(
        attend_kernel,
        out_shape=(packed, packed, packed, packed, jax.ShapeDtypeStruct((2, row_len), F32))
        + (jax.ShapeDtypeStruct((4, row_len // 8, 2 * HD), BF),) * 2,
        in_specs=[smem, smem, vmem, vmem, vmem, vmem],
        out_specs=(vmem,) * 7,
        scratch_shapes=[pltpu.VMEM((2, row_len, 2 * HD), BF), pltpu.VMEM((2, row_len, 2 * HD), BF)],
        compiler_params=pltpu.CompilerParams(vmem_limit_bytes=48 * 2**20),
        cost_estimate=SMALL,
        name="attend",
    )(split, where, mixed, *tables)


def attend_back_kernel(
    split_ref, q_hbm, k_hbm, v_hbm, o_hbm, do_hbm, log_ref,
    cos_ref, ahead_ref, behind_ref,
    dmix_ref, dpos_ref, kz, vz, qz, dz, ktz, delta, dq_t, dk, dv,
    q_ref, k_ref, v_ref, o_ref, do_ref, sem,
):
    loads = [
        pltpu.make_async_copy(source, target, sem.at[n])
        for n, (source, target) in enumerate(
            ((k_hbm, k_ref), (v_hbm, v_ref), (q_hbm, q_ref), (do_hbm, do_ref), (o_hbm, o_ref))
        )
    ]
    for copy in loads:
        copy.start()
    for copy in loads:
        copy.wait()
    row_len = q_ref.shape[0]
    local_len = dmix_ref.shape[2]
    low = lax.broadcasted_iota(jnp.int32, (BLOCK, 2 * HD), 1) < HD
    low_t = lax.broadcasted_iota(jnp.int32, (2 * HD, BLOCK), 0) < HD
    lane = lax.broadcasted_iota(jnp.int32, (8, 2 * HD), 1)
    ones = [jnp.where(lane < HD, 1.0, 0.0).astype(BF), jnp.where(lane < HD, 0.0, 1.0).astype(BF)]

    def prepare(b, carry):
        rows = pl.ds(pl.multiple_of(b * BLOCK, BLOCK), BLOCK)
        zero = jnp.zeros((BLOCK, 2 * HD), F32)
        for ref, out in ((k_ref, kz), (v_ref, vz), (q_ref, qz), (do_ref, dz)):
            value = ref[rows].astype(F32)
            out[0, rows] = jnp.where(low, value, zero).astype(BF)
            out[1, rows] = jnp.where(low, zero, value).astype(BF)
        value = k_ref[rows].astype(F32).T
        ktz[0, :, rows] = jnp.where(low_t, value, 0.0).astype(BF)
        ktz[1, :, rows] = jnp.where(low_t, 0.0, value).astype(BF)
        product = do_ref[rows].astype(F32) * o_ref[rows].astype(F32)
        coarse = product.astype(BF)
        fine = (product - coarse.astype(F32)).astype(BF)
        for row in range(2):
            delta[row, :, rows] = dot_rows(ones[row], coarse) + dot_rows(ones[row], fine)
        dq_t[:, rows] = jnp.zeros((2 * HD, BLOCK), F32)
        return carry

    lax.fori_loop(0, row_len // BLOCK, prepare, 0)
    u_in = lax.broadcasted_iota(jnp.int32, (BLOCK, 1), 0)
    t_in = lax.broadcasted_iota(jnp.int32, (1, BLOCK), 1)

    def key_block(kb, carry):
        keys = pl.ds(pl.multiple_of(kb * BLOCK, BLOCK), BLOCK)
        u = u_in + kb * BLOCK
        sums_k, sums_v = [], []
        for row in range(2):
            split = split_ref[row]
            k_row = kz[row, keys]
            v_row = vz[row, keys]
            kt_row = ktz[row, :, keys]

            def step(qb, state, row=row, split=split, k_row=k_row, v_row=v_row, kt_row=kt_row):
                d_keys, d_values = state
                rows = pl.ds(pl.multiple_of(qb * BLOCK, BLOCK), BLOCK)
                t = t_in + qb * BLOCK
                start = jnp.where(t >= split, split, 0)
                allowed = (u >= start) & (u <= t)
                scores = dot_rows(k_row, q_ref[rows])
                probs = jnp.where(allowed, jnp.exp(scores - log_ref[pl.ds(row, 1), rows]), 0.0)
                d_probs = dot_rows(v_row, do_ref[rows])
                d_scores = (probs * (d_probs - delta[row, pl.ds(0, 1), rows])).astype(BF)
                d_values = d_values + dot(probs.astype(BF), dz[row, rows])
                d_keys = d_keys + dot(d_scores, qz[row, rows])
                dq_t[:, rows] += dot(kt_row, d_scores)
                return d_keys, d_values

            zero = jnp.zeros((BLOCK, 2 * HD), F32)
            last = jnp.where(
                (kb + 1) * BLOCK <= split, (split + BLOCK - 1) // BLOCK, row_len // BLOCK
            )
            d_keys, d_values = lax.fori_loop(kb, last, step, (zero, zero))
            sums_k.append(d_keys)
            sums_v.append(d_values)
        dk[keys] = sums_k[0] + sums_k[1]
        dv[keys] = sums_v[0] + sums_v[1]
        return carry

    lax.fori_loop(0, row_len // BLOCK, key_block, 0)
    low_l = lax.broadcasted_iota(jnp.int32, (local_len, 2 * HD), 1) < HD
    per = 2 * HD // local_len


    def finish(b, carry):
        start = pl.multiple_of(b * 2 * HD, 2 * HD)
        dq = dq_t[:, pl.ds(start, 2 * HD)].T * HD**-0.5
        for part in range(per):
            i = b * per + part
            rows = pl.ds(pl.multiple_of(i * local_len, local_len), local_len)
            cosine, ahead, behind = cos_ref[rows], ahead_ref[rows], behind_ref[rows]

            def turn(x, cosine=cosine, ahead=ahead, behind=behind):
                return (
                    x * cosine
                    - pltpu.roll(x, 2 * HD - ROT // 2, 1) * ahead
                    - pltpu.roll(x, ROT // 2, 1) * behind
                )

            q_part = turn(dq[part * local_len : (part + 1) * local_len])
            k_part = turn(dk[rows])
            v_part = dv[rows]
            first = jnp.where(low_l, q_part, pltpu.roll(k_part, HD, 1)).astype(BF)
            second = jnp.where(low_l, pltpu.roll(q_part, HD, 1), k_part).astype(BF)
            dpos_ref[rows, : 2 * HD] = first
            dpos_ref[rows, 2 * HD : 4 * HD] = second
            dpos_ref[rows, 4 * HD :] = v_part.astype(BF)
            dmix_ref[i, 0, :, : 2 * HD] = first
            dmix_ref[i, 1, :, : 2 * HD] = second
            dmix_ref[i, 0, :, 2 * HD :] = jnp.where(low_l, v_part, 0.0).astype(BF)
            dmix_ref[i, 1, :, 2 * HD :] = jnp.where(low_l, pltpu.roll(v_part, HD, 1), 0.0).astype(BF)
        return carry

    lax.fori_loop(0, row_len // (2 * HD), finish, 0)


def attend_back(split, q, k, v, out, d_out, logs, tables, local_len):
    row_len = q.shape[0]
    smem = pl.BlockSpec(memory_space=pltpu.SMEM)
    vmem = pl.BlockSpec(memory_space=pltpu.VMEM)
    masked = pltpu.VMEM((2, row_len, 2 * HD), BF)
    whole = pltpu.VMEM((row_len, 2 * HD), F32)
    pairs = 2 * row_len * row_len // 2
    return pl.pallas_call(
        attend_back_kernel,
        out_shape=(
            jax.ShapeDtypeStruct((row_len // local_len, 2, local_len, 4 * HD), BF),
        )
        + (jax.ShapeDtypeStruct((row_len, 6 * HD), BF),),
        in_specs=[smem] + [pl.BlockSpec(memory_space=pltpu.HBM)] * 5 + [vmem] * 4,
        out_specs=(vmem,) * 2,
        scratch_shapes=[
            masked, masked, masked, masked,
            pltpu.VMEM((2, 2 * HD, row_len), BF),
            pltpu.VMEM((2, 8, row_len), F32),
            pltpu.VMEM((2 * HD, row_len), F32),
            whole, whole,
        ]
        + [pltpu.VMEM((row_len, 2 * HD), BF)] * 5
        + [pltpu.SemaphoreType.DMA((5,))],
        compiler_params=pltpu.CompilerParams(vmem_limit_bytes=48 * 2**20),
        cost_estimate=SMALL,
        name="attend_back",
    )(split, q, k, v, out, d_out, logs, *tables)


def pick_heads_kernel(where_ref, q_ref, k_ref, v_ref, out_ref):
    wide = 2 * HD
    low = lax.broadcasted_iota(jnp.int32, (q_ref.shape[0], wide), 1) < HD
    for core in (0, 1):

        @pl.when(where_ref[1] // 4 == core)
        def _(core=core):
            def join(left, right):
                if core == 0:
                    return jnp.where(low, left, pltpu.roll(right, HD, 1)).astype(BF)
                return jnp.where(low, pltpu.roll(left, HD, 1), right).astype(BF)

            for z in range(4):
                cols = slice(z * wide, (z + 1) * wide)
                out_ref[:, cols] = join(q_ref[:, cols].astype(F32), k_ref[:, cols].astype(F32))
            for pair in range(2):
                left, right = (
                    v_ref[:, (2 * pair + n) * wide : (2 * pair + n + 1) * wide].astype(F32) for n in (0, 1)
                )
                out_ref[:, (4 + pair) * wide : (5 + pair) * wide] = join(left, right)


def pick_heads(where, weight):
    rows, columns = weight.shape
    wide = columns // 12
    blocks = [
        pl.BlockSpec((rows, wide), lambda chip, where, part=part: (0, part * 4 + chip)) for part in range(3)
    ]
    return pl.pallas_call(
        pick_heads_kernel,
        grid_spec=pltpu.PrefetchScalarGridSpec(
            num_scalar_prefetch=1,
            grid=(4,),
            in_specs=blocks,
            out_specs=pl.BlockSpec((None, rows, 12 * HD), lambda chip, where: (chip, 0, 0)),
        ),
        out_shape=jax.ShapeDtypeStruct((4, rows, 12 * HD), BF),
        compiler_params=pltpu.CompilerParams(vmem_limit_bytes=32 * 2**20),
        cost_estimate=SMALL,
        name="pick_heads",
    )(where, weight, weight, weight)


def small_call(kernel, name, out_shape, where, *arrays, flops=0, scratch=(), limit=32):
    size = sum(x.size * x.dtype.itemsize for x in arrays)
    vmem = pl.BlockSpec(memory_space=pltpu.VMEM)
    return pl.pallas_call(
        kernel,
        out_shape=out_shape,
        in_specs=[pl.BlockSpec(memory_space=pltpu.SMEM)] + [vmem] * len(arrays),
        out_specs=[vmem] * len(out_shape),
        scratch_shapes=scratch,
        compiler_params=pltpu.CompilerParams(vmem_limit_bytes=limit * 2**20),
        cost_estimate=SMALL,
        name=name,
    )(where, *arrays)


def pair_kernel(where_ref, mine_ref, theirs_ref, *outs):
    low = lax.broadcasted_iota(jnp.int32, mine_ref.shape[1:], 1) < HD
    for step, out in enumerate(outs):
        for core, (ref0, ref1) in enumerate(((mine_ref, theirs_ref), (theirs_ref, mine_ref))):

            @pl.when(where_ref[1] // 4 == core)
            def _(ref0=ref0, ref1=ref1):
                even, uneven = ref0[step].astype(F32), ref1[step].astype(F32)
                out[:, : 2 * HD] = jnp.where(low, even, pltpu.roll(uneven, HD, 1)).astype(BF)
                out[:, 2 * HD :] = jnp.where(low, pltpu.roll(even, HD, 1), uneven).astype(BF)


def out_project_kernel(where_ref, a0, a1, a2, a3, weight_ref, att_ref, o0, o1, o2, o3, sum_v):
    plane, rank = where_ref[0], where_ref[1] % 4
    span = a0.shape[0]
    for step, ref in enumerate((a0, a1, a2, a3)):
        lanes = pl.ds(pl.multiple_of(lax.rem(plane - step + 4, 4) * 2 * HD, 2 * HD), 2 * HD)
        for row in range(2):
            att_ref[row * span : (row + 1) * span, lanes] = ref[:, row * 2 * HD : (row + 1) * 2 * HD]
    sum_v[...] = dot(att_ref[...], weight_ref[...])
    part = span // 4
    for m, out in enumerate((o0, o1, o2, o3)):
        for row in range(2):
            rows = pl.ds(pl.multiple_of(row * span + (rank ^ m) * part, part), part)
            out[row * part : (row + 1) * part] = sum_v[rows].astype(out.dtype)


def d_att_kernel(where_ref, p0, p1, p2, p3_low, p3_high, weight_ref, branch_ref, heads_ref):
    rank = where_ref[1] % 4
    span = heads_ref.shape[1]
    part = span // 4
    for m, pieces in enumerate(((p0,), (p1,), (p2,), (p3_low, p3_high))):
        for row in range(2):
            rows = pl.ds(pl.multiple_of(row * span + (rank ^ m) * part, part), part)
            if len(pieces) == 2:
                branch_ref[rows] = pieces[row][...]
            else:
                branch_ref[rows] = pieces[0][row * part : (row + 1) * part]
    d_att = dot_rows(branch_ref[...], weight_ref[...])
    low = lax.broadcasted_iota(jnp.int32, heads_ref.shape[1:], 1) < HD
    for z in range(4):
        lanes = slice(z * 2 * HD, (z + 1) * 2 * HD)
        row0, row1 = d_att[:span, lanes], d_att[span:, lanes]
        heads_ref[2 * z] = jnp.where(low, row0, pltpu.roll(row1, HD, 1)).astype(BF)
        heads_ref[2 * z + 1] = jnp.where(low, pltpu.roll(row0, HD, 1), row1).astype(BF)


def d_in_kernel(where_ref, in_ref, weight_ref, near_ref, far_ref, x_v, d_v):
    core, rank = where_ref[1] // 4, where_ref[1] % 4
    reach, wide = in_ref.shape[1], 2 * HD
    features = weight_ref.shape[0]
    low = lax.broadcasted_iota(jnp.int32, (reach, wide), 1) < HD
    for z in range(4):
        for row in range(2):
            x_v[row * reach : (row + 1) * reach, z * wide : (z + 1) * wide] = in_ref[
                z, :, row * wide : (row + 1) * wide
            ]
    for pair in range(2):
        cols = slice((4 + pair) * wide, (5 + pair) * wide)
        one, two = (in_ref[2 * pair + n, :, 2 * wide :].astype(F32) for n in (0, 1))
        x_v[:reach, cols] = jnp.where(low, one, pltpu.roll(two, HD, 1)).astype(BF)
        x_v[reach:, cols] = jnp.where(low, pltpu.roll(one, HD, 1), two).astype(BF)
    part = reach // 8
    span = d_v.shape[1]

    def columns(n, carry):
        cols = pl.ds(pl.multiple_of(n * span, span), span)
        d_v[...] = dot_rows(x_v[...], weight_ref[cols])
        for ref, which in ((near_ref, core), (far_ref, 1 - core)):
            for m in range(4):
                for row in range(2):
                    first = row * reach + which * 4 * part + (rank ^ m) * part
                    rows = pl.ds(pl.multiple_of(first, part), part)
                    ref[m, row * part : (row + 1) * part, cols] = d_v[rows].astype(BF)
        return carry

    lax.fori_loop(0, features // span, columns, 0)


def hidden_kernel(where_ref, *refs, steps, own):
    n_mid, n_out = (10, 2) if own else (1, 4 * len(steps))
    mids, outs, refs = refs[:n_mid], refs[n_mid : n_mid + n_out], refs[n_mid + n_out :]
    gate_ref, up_ref, down_ref = refs[:3]
    refs = refs[3:] if own else refs[7:]
    alls, refs = refs[:4], refs[4:]
    d_mids, acts, refs = (refs[:2], refs[2:4], refs[4:]) if own else ((), (), refs)
    mid_v, out_v, gate_up_v, down_v, act_v, d_gate_v, d_up_v, sem_in, sem_w, sem_out = refs[:10]
    rows, features = mid_v.shape[1:]
    width, tile = down_v.shape[0], 256
    tiles = width // tile
    plane, mine = where_ref[0], where_ref[1]
    core = mine // 4
    shard = gate_ref.shape[1]
    step = rows // 4
    halves = 2 * len(steps)

    def blocks(h):
        base = lax.rem(plane + 4 - steps[h // 2], 4) * (2 * rows)
        return [
            pl.ds(pl.multiple_of(base + (mine ^ (4 * (h % 2) + m)) * step, step), step) for m in range(4)
        ]

    def loads(h):
        slot = h % 2
        if own:
            pieces, out_pieces = mids[5 * h : 5 * h + 5], outs[h : h + 1]
        else:
            pieces = [mids[0].at[block] for block in blocks(h)]
            out_pieces = outs[2 * h : 2 * h + 2]
        found = []
        for held, sources in ((mid_v, pieces), (out_v, out_pieces)):
            at = 0
            for source in sources:
                size = source.shape[0]
                found.append((source, held.at[slot, pl.ds(at, size)]))
                at += size
        return [pltpu.make_async_copy(x, y, sem_in.at[slot, n]) for n, (x, y) in enumerate(found)]

    def stores(h):
        slot = h % 2
        return [
            pltpu.make_async_copy(
                held.at[slot, pl.ds(m * step, step)], target.at[block], sem_out.at[slot, n, m]
            )
            for n, (held, target) in enumerate(zip((act_v, d_gate_v, d_up_v, out_v), alls))
            for m, block in enumerate(blocks(h))
        ]

    def tile_copies(j):
        cols = pl.ds(j * tile, tile)
        found = [
            (ref.at[m, :, cols], gate_up_v.at[g, pl.ds(m * shard, shard), cols])
            for g, ref in enumerate((gate_ref, up_ref))
            for m in range(4)
        ]
        first = pl.multiple_of(core * (down_ref.shape[0] - width) + j * tile, 128)
        found.append((down_ref.at[pl.ds(first, tile)], down_v.at[cols]))
        return [pltpu.make_async_copy(x, y, sem_w.at[j, n]) for n, (x, y) in enumerate(found)]

    def wait_tile(j):
        for copy in weight_copies[j]:
            copy.wait()
        if j == 0:

            @pl.when(core == 1)
            def _():
                gate_up_v[:, :, : 2 * width - down_ref.shape[0]] = jnp.zeros(
                    (2, features, 2 * width - down_ref.shape[0]), BF
                )

    def compute(slot, cols):
        gate = dot(mid_v[slot], gate_up_v[0, :, cols])
        up = dot(mid_v[slot], gate_up_v[1, :, cols])
        d_act = dot_rows(out_v[slot], down_v[cols])
        sig = 1.0 / (1.0 + jnp.exp(-gate))
        silu = gate * sig
        act_v[slot, :, cols] = (silu * up).astype(BF)
        d_gate_v[slot, :, cols] = (d_act * up * (sig + silu * (1.0 - sig))).astype(BF)
        d_up_v[slot, :, cols] = (d_act * silu).astype(BF)

    weight_copies = [tile_copies(j) for j in range(tiles)]
    for copies in [weight_copies[0], loads(0)] + weight_copies[1:] + [loads(1)]:
        for copy in copies:
            copy.start()
    for h in range(halves):
        slot = h % 2
        for copy in loads(h):
            copy.wait()
        if h == 0:
            for j in range(tiles):
                wait_tile(j)
                compute(0, pl.ds(j * tile, tile))
        else:
            compute(slot, pl.ds(0, tile))
            if h + 1 < halves:
                for copy in stores(h - 1):
                    copy.wait()
                for copy in loads(h + 1):
                    copy.start()

            def part(j, carry, slot=slot):
                compute(slot, pl.ds(pl.multiple_of(j * tile, tile), tile))
                return carry

            lax.fori_loop(1, tiles, part, 0)
        for copy in stores(h):
            copy.start()
    left = []
    if own:
        sum_v = refs[10]
        span = 512
        for i in (1, 0):
            for m in range(4):
                part = pl.ds(m * step, step)
                left.append(
                    pltpu.make_async_copy(act_v.at[i, part], acts[i].at[m], sem_out.at[i, 4, m])
                )
                left[-1].start()

            def term(n, carry, i=i):
                cols = pl.ds(pl.multiple_of(n * span, span), span)
                sum_v[i, :, cols] = (
                    dot_rows(d_gate_v[i], gate_up_v[0, cols]) + dot_rows(d_up_v[i], gate_up_v[1, cols])
                ).astype(BF)
                return carry

            lax.fori_loop(0, features // span, term, 0)
            for m in range(4):
                part = pl.ds(m * step, step)
                left.append(
                    pltpu.make_async_copy(sum_v.at[i, part], d_mids[i].at[m], sem_out.at[i, 5, m])
                )
                left[-1].start()
    for h in (halves - 2, halves - 1):
        left += stores(h)
    for copy in left:
        copy.wait()


def hidden_layer(where, mids, outs, weights, total, steps=(0,), before=None):
    own = before is None
    features = outs[0].shape[1]
    rows, width = total // 8, weights[0].shape[2]
    narrow = jax.ShapeDtypeStruct((total, width), BF)
    wide = jax.ShapeDtypeStruct((total, features), BF)
    term = jax.ShapeDtypeStruct((4, rows // 4, features), BF)
    act = jax.ShapeDtypeStruct((4, rows // 4, width), BF)
    held = pltpu.VMEM((2, rows, features), BF)
    small = pltpu.VMEM((2, rows, width), BF)
    dma = pltpu.SemaphoreType.DMA
    count = len(mids) + len(outs)
    kept = [] if own else list(before)
    hbm = pl.BlockSpec(memory_space=pltpu.HBM)
    found = pl.pallas_call(
        functools.partial(hidden_kernel, steps=steps, own=own),
        in_specs=[pl.BlockSpec(memory_space=pltpu.SMEM)] + [hbm] * (count + 3 + len(kept)),
        out_specs=[hbm] * (8 if own else 4),
        out_shape=[narrow, narrow, narrow, wide] + ([term, term, act, act] if own else []),
        input_output_aliases={count + 4 + n: n for n in range(len(kept))},
        scratch_shapes=[
            held, held,
            pltpu.VMEM((2, features, width), BF),
            pltpu.VMEM((width, features), BF),
            small, small, small,
            dma((2, 9)), dma((width // 256, 9)), dma((2, 6, 4)),
        ]
        + ([held] if own else []),
        compiler_params=pltpu.CompilerParams(vmem_limit_bytes=48 * 2**20),
        cost_estimate=SMALL,
        name="hidden",
    )(where, *mids, *outs, *weights, *kept)
    return list(found[:4]), list(found[4:])


def weight_grad_kernel(left_ref, right_ref, out_ref):
    out_ref[...] = dot_cols(left_ref[...], right_ref[...]).astype(BF)


def weight_grad(left, right):
    tokens, features = left.shape
    width = right.shape[1]
    step = 256
    return pl.pallas_call(
        weight_grad_kernel,
        grid=(features // step,),
        in_specs=[
            pl.BlockSpec((tokens, step), lambda i: (0, i)),
            pl.BlockSpec((tokens, width), lambda i: (0, 0), pipeline_mode=pl.Buffered(1)),
        ],
        out_specs=pl.BlockSpec((step, width), lambda i: (i, 0)),
        out_shape=jax.ShapeDtypeStruct((features, width), BF),
        compiler_params=pltpu.CompilerParams(vmem_limit_bytes=48 * 2**20),
        cost_estimate=SMALL,
        name="weight_grad",
    )(left, right)


def place_columns_kernel(where_ref, own_ref, other_ref, *rest):
    out_ref = rest[-1]
    wide = own_ref.shape[-1]
    extra = out_ref.shape[-1] - wide

    @pl.when(where_ref[0] == 0)
    def _():
        out_ref[:, :wide] = own_ref[...].astype(F32)
        out_ref[:, wide:] = other_ref[:, wide - extra :].astype(F32)

    @pl.when(where_ref[0] == 1)
    def _():
        out_ref[:, :wide] = other_ref[...].astype(F32)
        out_ref[:, wide:] = own_ref[:, wide - extra :].astype(F32)


def place_columns(core, own, other, before, chip_width, kind):
    chips, rows, wide = own.shape
    cut = rows // 2
    half = pl.BlockSpec((None, cut, wide), lambda chip, b, core: (chip, b, 0))
    return pl.pallas_call(
        place_columns_kernel,
        grid_spec=pltpu.PrefetchScalarGridSpec(
            num_scalar_prefetch=1,
            grid=(chips, rows // cut),
            in_specs=[half, half] + ([] if before is None else [pl.BlockSpec(memory_space=pl.ANY)]),
            out_specs=pl.BlockSpec((cut, chip_width), lambda chip, b, core: (b, kind * chips + chip)),
        ),
        out_shape=jax.ShapeDtypeStruct((rows, 2 * chips * chip_width), F32),
        input_output_aliases={} if before is None else {3: 0},
        compiler_params=pltpu.CompilerParams(vmem_limit_bytes=32 * 2**20),
        cost_estimate=SMALL,
        name="place_columns",
    )(core, own, other, *([] if before is None else [before]))


def place_down_kernel(core_ref, own_ref, other_ref, out_ref, *, lead):
    first = pl.program_id(0) < lead
    mine = first == (core_ref[0] == 0)

    @pl.when(mine)
    def _():
        out_ref[...] = own_ref[...].astype(F32)

    @pl.when(jnp.logical_not(mine))
    def _():
        out_ref[...] = other_ref[...].astype(F32)


def place_down(core, own, other, total):
    width, features = own.shape
    step = 128
    count, lead = total // step, width // step
    skip = 2 * lead - count

    def block(of_core):
        def index(i, core):
            which = core[0] if of_core else 1 - core[0]
            return (jnp.where(which == 0, jnp.minimum(i, lead - 1), jnp.maximum(i - lead + skip, 0)), 0)

        return pl.BlockSpec((step, features), index)

    return pl.pallas_call(
        functools.partial(place_down_kernel, lead=lead),
        grid_spec=pltpu.PrefetchScalarGridSpec(
            num_scalar_prefetch=1,
            grid=(count,),
            in_specs=[block(True), block(False)],
            out_specs=pl.BlockSpec((step, features), lambda i, core: (i, 0)),
        ),
        out_shape=jax.ShapeDtypeStruct((total, features), F32),
        cost_estimate=SMALL,
        name="place_down",
    )(core, own, other)


def place_qkv_kernel(where_ref, own_ref, other_ref, out_ref):
    cut = own_ref.shape[2]
    core = where_ref[0]
    for ref, half in ((own_ref, core), (other_ref, 1 - core)):
        rows = pl.ds(pl.multiple_of(half * cut, cut), cut)
        for z in range(4):
            out_ref[rows, z * 2 * HD : (z + 1) * 2 * HD] = ref[z, 0].astype(F32)


def place_qkv(where, own, other):
    _, _, cut, wide = own.shape
    parts = wide // (2 * HD)
    piece = pl.BlockSpec((4, 1, cut, 2 * HD), lambda part, chip, where: (0, chip ^ where[1], 0, part))
    return pl.pallas_call(
        place_qkv_kernel,
        grid_spec=pltpu.PrefetchScalarGridSpec(
            num_scalar_prefetch=1,
            grid=(parts, 4),
            in_specs=[piece, piece],
            out_specs=pl.BlockSpec((2 * cut, 8 * HD), lambda part, chip, where: (0, part * 4 + chip)),
        ),
        out_shape=jax.ShapeDtypeStruct((2 * cut, parts * 32 * HD), F32),
        cost_estimate=SMALL,
        name="place_qkv",
    )(where, own, other)


def tie(*values):
    return lax.optimization_barrier(values)


def plane_plan(
    inputs,
    segments,
    norm1_gain,
    norm1_bias,
    qkv_weight,
    qkv_bias,
    out_weight,
    norm2_gain,
    norm2_bias,
    gate_up_weight,
    down_weight,
    cotangent,
):
    row_count, local_len, features = inputs.shape
    row_len = segments.shape[1]
    tokens = row_count * local_len
    plane, core, rank = lax.axis_index("z"), lax.axis_index("core"), lax.axis_index("fsdp")
    seq = plane * 2 + core
    own = core * 4 + rank
    shard = features // 4
    hidden = gate_up_weight.shape[1] // 2
    chip_width = hidden // 4
    width = -(-chip_width // 256) * 128
    tables = turn_tables(row_len)
    split = jnp.sum((segments == 0).astype(jnp.int32), axis=1)
    where = jnp.stack([plane, own]).astype(jnp.int32)

    def head_columns(chip):
        parts = [
            lax.dynamic_slice_in_dim(qkv_weight, (chip * 8 + seq) * HD + part * features, HD, 1)
            for part in (0, 1, 2)
        ]
        return jnp.concatenate(parts + parts[2:], axis=1)

    head_weight = exchange(jnp.stack([head_columns(chip) for chip in range(4)])).reshape(features, 4 * HD)
    picked = pick_heads(where, qkv_weight)
    head_first = (rank * 8 + seq) * HD
    bias_parts = [
        lax.dynamic_slice_in_dim(qkv_bias, head_first + part * features, HD, 0) for part in (0, 1, 2)
    ]
    head_bias = jnp.concatenate(bias_parts + bias_parts[2:])
    hidden_first = core * (chip_width - width)

    def hidden_columns(kind):
        firsts = [hidden_first + chip * chip_width + kind * hidden for chip in range(4)]
        return jnp.stack([lax.dynamic_slice_in_dim(gate_up_weight, first, width, 1) for first in firsts])

    gate_weight, up_weight = hidden_columns(0), hidden_columns(1)

    flat = inputs.reshape(tokens, features).astype(F32)
    normed_in, norm1_back = jax.vjp(layer_norm, flat, norm1_gain, norm1_bias)
    everywhere = ("z", "core", "fsdp")
    in_all = lax.all_gather(normed_in.astype(BF), everywhere, axis=0, tiled=True)
    d_out = cotangent.reshape(tokens, features)
    out_near = jnp.concatenate(gather_near(d_out), axis=0)
    out_far = swap(out_near, 4)
    in_all, out_near, out_far, gate_weight, up_weight, head_weight, picked, *tables = tie(
        in_all, out_near, out_far, gate_weight, up_weight, head_weight, picked, *tables
    )
    lows, highs = [out_near[: 2 * tokens]], [out_near[2 * tokens :]]

    mixed = (dot(in_all, head_weight) + head_bias).reshape(
        row_len // local_len, row_count, local_len, 4 * HD
    )
    q, k, v, out_heads, logs, mine, theirs, gate_weight, low, up_weight = tie(
        *attend(split, where, mixed, tables), exchange(gate_weight), shift(lows[0], 1), up_weight
    )
    lows.append(low)
    span = row_len // 8
    pair = jax.ShapeDtypeStruct((span, 4 * HD), BF)
    pairs = small_call(pair_kernel, "pair", [pair] * 4, where, mine, swap(theirs, 4))
    arrived = [pairs[0]] + [shift(pairs[n], n) for n in (1, 2, 3)]
    square = row_count * span
    block = jax.ShapeDtypeStruct((tokens, features), BF)
    blocks = jax.ShapeDtypeStruct((4, tokens, features), BF)
    att, *branch = small_call(
        out_project_kernel,
        "out_project",
        [jax.ShapeDtypeStruct((square, shard), BF), jax.ShapeDtypeStruct((tokens, features), F32)]
        + [block] * 3,
        where,
        *arrived,
        out_weight,
        scratch=[pltpu.VMEM((square, features), F32)],
    )
    branch_sum, up_weight, high = tie(sum_quad(branch), exchange(up_weight), shift(highs[0], 1))
    highs.append(high)
    hidden_weights = [gate_weight, up_weight, down_weight]
    middle = flat + branch_sum
    normed_mid, norm2_back = jax.vjp(layer_norm, middle, norm2_gain, norm2_bias)
    mid_low = normed_mid.astype(BF)

    mid_pieces = gather_pieces(mid_low)
    *mid_pieces, mid_own, low = tie(*mid_pieces, mid_low, shift(lows[1], 1))
    lows.append(low)
    mid_all = lax.all_gather(mid_own, everywhere, axis=0, tiled=True)
    total = row_count * row_len
    hidden_all, (d_near, d_far, act_near, act_far) = hidden_layer(
        where, mid_pieces, [out_near, out_far], hidden_weights, total
    )
    d_near, d_far, high = tie(d_near, d_far, shift(highs[1], 1))
    highs.append(high)
    d_norm_mid, low = tie(sum_plane(d_near, d_far), shift(lows[2], 1))
    lows.append(low)
    d_middle_part, d_gain_two, d_bias_two = norm2_back(d_norm_mid)
    d_middle = d_out.astype(F32) + d_middle_part

    d_pieces = gather_near(d_middle.astype(BF))
    d_branch, d_heads = small_call(
        d_att_kernel,
        "d_att",
        [
            jax.ShapeDtypeStruct((square, features), BF),
            jax.ShapeDtypeStruct((8, span, 2 * HD), BF),
        ],
        where,
        *d_pieces,
        out_weight,
    )
    d_heads = exchange(d_heads, ("z", "core")).reshape(row_len, 2 * HD)
    d_heads, high_own = tie(d_heads, highs[2])
    d_packed, d_mixed, mid_all, high = tie(
        *attend_back(split, q, k, v, out_heads, d_heads, logs, tables, local_len)[::-1],
        mid_all,
        shift(high_own, 1),
    )
    highs.append(high)

    arrived = exchange(d_packed.reshape(4, row_len // 4, 6 * HD), "z")
    d_mixed = d_mixed.reshape(row_len * row_count, 4 * HD)
    head_grad = dot_cols(in_all, d_mixed)[:, : 3 * HD].astype(BF)
    cut = shard // 2
    head_grad = head_grad.reshape(4, 2, cut, 3 * HD)
    mine = lax.dynamic_index_in_dim(head_grad, core, 1, keepdims=False)
    theirs = swap(lax.dynamic_index_in_dim(head_grad, 1 - core, 1, keepdims=False), 4)
    first, second = jnp.where(core == 0, mine, theirs), jnp.where(core == 0, theirs, mine)
    pairs = jnp.concatenate(
        [half[:, :, p * HD : (p + 1) * HD] for p in range(3) for half in (first, second)], axis=2
    )
    down = lax.dynamic_slice_in_dim(down_weight, hidden_first, width, 0)
    result_sum = sum_plane(
        dot(act_near.reshape(4 * tokens, width), down).reshape(4, tokens, features),
        dot(act_far.reshape(4 * tokens, width), down).astype(BF).reshape(4, tokens, features),
    )

    def rest(steps, before):
        outs = [
            piece for n in steps for piece in (lows[n], highs[n], swap(lows[n], 4), swap(highs[n], 4))
        ]
        return hidden_layer(where, [mid_all], outs, hidden_weights, total, steps, before)[0]

    hidden_all = rest((1, 2), hidden_all)
    arrived, result_sum, pairs, att, d_branch, picked, *hidden_all = tie(
        arrived, result_sum, pairs, att, d_branch, picked, *hidden_all
    )
    result = middle + result_sum

    pairs = [pick(pairs, rank ^ m) for m in range(4)]
    pairs = [pairs[0]] + [swap(pairs[m], m) for m in (1, 2, 3)]
    head_all = exchange(picked).reshape(features, 12 * HD)
    out_part = dot_cols(att, d_branch).astype(BF)
    out_part = lax.psum_scatter(out_part, ("z", "core"), scatter_dimension=0, tiled=True)
    act_all, d_gate_all, d_up_all, out_all = rest((3,), hidden_all)
    head_all, d_gate_grad, d_up_all, act_all, arrived, out_part, *pairs = tie(
        head_all, weight_grad(mid_all, d_gate_all), d_up_all, act_all, arrived, out_part, *pairs
    )

    by_chip = (4, shard, width)
    near, far = small_call(
        d_in_kernel,
        "d_in",
        [blocks] * 2,
        where,
        arrived,
        head_all,
        scratch=[
            pltpu.VMEM((8 * tokens, 12 * HD), BF),
            pltpu.VMEM((8 * tokens, 512), F32),
        ],
        limit=48,
    )
    heads = lax.all_gather(jnp.stack(pairs), "z", axis=0)
    gate_parts, d_up_grad, near, far, act_all = tie(
        exchange(d_gate_grad.reshape(by_chip)),
        weight_grad(mid_all, d_up_all),
        near,
        swap(far, 4),
        act_all,
    )
    d_norm_in, down_own, d_up_grad = tie(
        sum_quad([near[m].astype(F32) + far[m].astype(F32) for m in range(4)]),
        weight_grad(act_all, out_all),
        d_up_grad,
    )

    core_index = core.reshape(1).astype(jnp.int32)
    up_parts = exchange(d_up_grad.reshape(by_chip))
    out_rows = lax.all_gather(out_part, ("z", "core"), axis=0, tiled=True)
    gate_up_grad = place_columns(core_index, gate_parts, swap(gate_parts, 4), None, chip_width, 0)
    down_grad = place_down(core_index, down_own, swap(down_own, 4), chip_width)
    d_flat_part, d_gain_one, d_bias_one = norm1_back(d_norm_in)
    d_inputs = d_middle + d_flat_part
    bias_sum = jnp.sum(d_mixed.astype(F32), axis=0)
    bias_own = jnp.zeros((3 * features,), F32)
    for part in range(3):
        bias_own = lax.dynamic_update_slice_in_dim(
            bias_own, bias_sum[part * HD : (part + 1) * HD], head_first + part * features, 0
        )
    sums = jnp.concatenate([d_gain_one, d_bias_one, bias_own, d_gain_two, d_bias_two])
    sums = sums + swap(sums, 4)
    sums = sums + sum(shift(sums, n) for n in (1, 2, 3))
    qkv_grad = place_qkv(jnp.stack([core, rank]).astype(jnp.int32), heads, swap(heads, 4))
    up_parts, sums, gate_up_grad, down_grad, qkv_grad = tie(
        up_parts, sums, gate_up_grad, down_grad, qkv_grad
    )
    sums = sums + sum(swap(sums, m) for m in (1, 2, 3))
    out_grad = out_rows.astype(F32)
    gate_up_grad = place_columns(
        core_index, up_parts, swap(up_parts, 4), gate_up_grad, chip_width, 1
    )
    return (
        result.reshape(row_count, local_len, features),
        d_inputs.reshape(row_count, local_len, features),
        sums[:features],
        sums[features : 2 * features],
        qkv_grad,
        sums[2 * features : 5 * features],
        out_grad,
        sums[5 * features : 6 * features],
        sums[6 * features :],
        gate_up_grad,
        down_grad,
    )


def solution(mesh):
    planes = (mesh.shape["seq"], mesh.shape["fsdp"]) == (8, 4)
    plan = plane_plan if planes else general_plan
    if planes:
        mesh = jax.sharding.Mesh(mesh.devices.reshape(4, 2, 4), ("z", "core", "fsdp"))
    spread = P(None, (*mesh.axis_names,), None)
    placed = (
        spread,
        P(),
        P(),
        P(),
        P("fsdp", None),
        P(),
        P("fsdp", None),
        P(),
        P(),
        P("fsdp", None),
        P("fsdp", None),
        spread,
    )
    return jax.shard_map(
        plan,
        mesh=mesh,
        in_specs=placed,
        out_specs=(
            spread,
            spread,
            P(),
            P(),
            P("fsdp", None),
            P(),
            P("fsdp", None),
            P(),
            P(),
            P("fsdp", None),
            P("fsdp", None),
        ),
        check_vma=False,
    )
```

```python
import functools

import jax
import jax.numpy as jnp
from jax import lax
from jax.experimental import pallas as pl
from jax.experimental.pallas import tpu as pltpu
from jax.sharding import PartitionSpec as P

HD = 64
ROT = 16


EPSILON = 1e-05
MASKED = -1e30


def layer_norm(values, norm_gain, offset):
    average = jnp.mean(values, axis=-1, keepdims=True)
    centred = values - average
    variance = jnp.mean(centred * centred, axis=-1, keepdims=True)
    return centred * lax.rsqrt(variance + EPSILON) * norm_gain + offset


def rotate(values, positions):
    half_rot = ROT // 2
    exponent = jnp.arange(half_rot, dtype=jnp.float32) * (2.0 / ROT)
    inverse = jnp.power(jnp.float32(10000.0), -exponent)
    angles = positions.astype(jnp.float32)[:, None] * inverse[None, :]
    cosine = jnp.cos(angles)[:, None, :]
    sine = jnp.sin(angles)[:, None, :]
    first = values[:, :, :half_rot]
    second = values[:, :, half_rot:ROT]
    return jnp.concatenate(
        [first * cosine - second * sine, second * cosine + first * sine, values[:, :, ROT:]], axis=2
    )


def fold_rows(left, shard):
    return jnp.dot(
        left, lax.all_gather(shard, "fsdp", axis=0, tiled=True), preferred_element_type=jnp.float32
    )


def map_back(grad_rows, shard):
    return lax.dot_general(
        grad_rows,
        lax.all_gather(shard, "fsdp", axis=0, tiled=True),
        (((1,), (1,)), ((), ())),
        preferred_element_type=jnp.float32,
    )


def grad_joint(left, right_side):
    seq_count = lax.axis_size("seq")
    fsdp_count = lax.axis_size("fsdp")
    token_count, total_rows = left.shape
    share = total_rows // (seq_count * fsdp_count)
    permuted = (
        left.reshape(token_count, fsdp_count, seq_count, share)
        .transpose(0, 2, 1, 3)
        .reshape(token_count, total_rows)
    )
    return lax.psum_scatter(
        lax.dot_general(
            permuted, right_side, (((0,), (0,)), ((), ())), preferred_element_type=jnp.float32
        ),
        ("seq", "fsdp"),
        scatter_dimension=0,
        tiled=True,
    )


def general_plan(
    inputs,
    segments,
    norm1_gain,
    norm1_bias,
    qkv_weight,
    qkv_bias,
    out_weight,
    norm2_gain,
    norm2_bias,
    gate_up_weight,
    down_weight,
    cotangent,
):
    row_count, local_len, features = inputs.shape
    fsdp_count = lax.axis_size("fsdp")
    fsdp_rank = lax.axis_index("fsdp")
    block_rank = lax.axis_index("seq") * fsdp_count + fsdp_rank
    token_count = row_count * local_len
    head_count = features // HD
    ff_width = gate_up_weight.shape[1] // 2
    scale_factor = HD ** (-0.5)
    flat = inputs.reshape(token_count, features).astype(jnp.float32)
    local_pos = block_rank * local_len + jnp.arange(local_len, dtype=jnp.int32)
    positions = jnp.tile(local_pos, row_count)
    weight_set = (qkv_weight, out_weight, gate_up_weight, down_weight)

    def forward_product(left, slot_index):
        return fold_rows(left, weight_set[slot_index])

    def backward_product(grad_rows, slot_index):
        return map_back(grad_rows, weight_set[slot_index])

    normed_in, norm1_back = jax.vjp(layer_norm, flat, norm1_gain, norm1_bias)
    in_low = normed_in.astype(jnp.bfloat16)
    mixed = forward_product(in_low, 0) + qkv_bias
    turn_input = mixed[:, : 2 * features].reshape(token_count, 2 * head_count, HD)
    turned, turn_back = jax.vjp(lambda values: rotate(values, positions), turn_input)
    turned_low = turned.astype(jnp.bfloat16)
    queries = turned_low[:, :head_count].reshape(row_count, local_len, features)
    keys_loc = turned_low[:, head_count:].reshape(row_count, local_len, features)
    values_loc = (
        mixed[:, 2 * features :].astype(jnp.bfloat16).reshape(row_count, local_len, features)
    )
    head_query, head_key, head_value = (
        lax.all_to_all(queries, "seq", split_axis=2, concat_axis=1, tiled=True),
        lax.all_to_all(keys_loc, "seq", split_axis=2, concat_axis=1, tiled=True),
        lax.all_to_all(values_loc, "seq", split_axis=2, concat_axis=1, tiled=True),
    )
    all_keys, all_values = (
        lax.all_gather(head_key, "fsdp", axis=1, tiled=True),
        lax.all_gather(head_value, "fsdp", axis=1, tiled=True),
    )
    query_len = head_query.shape[1]
    key_len = all_keys.shape[1]
    head_width = head_query.shape[2]
    local_heads = head_width // HD
    query_four = head_query.reshape(row_count, query_len, local_heads, HD)
    keys_four = all_keys.reshape(row_count, key_len, local_heads, HD)
    values_four = all_values.reshape(row_count, key_len, local_heads, HD)
    query_index = jnp.arange(query_len, dtype=jnp.int32)
    query_pos = (
        query_index // local_len * fsdp_count + fsdp_rank
    ) * local_len + query_index % local_len
    key_index = jnp.arange(key_len, dtype=jnp.int32)
    key_pos = (
        key_index % query_len // local_len * fsdp_count + key_index // query_len
    ) * local_len + key_index % local_len
    query_seg = jnp.take(segments, query_pos, axis=1)
    key_seg = jnp.take(segments, key_pos, axis=1)
    span = min(512, key_len)
    block_count = key_len // span

    def block_inputs(block_index):
        first_row = block_index * span
        block_keys = lax.dynamic_slice_in_dim(keys_four, first_row, span, 1)
        block_values = lax.dynamic_slice_in_dim(values_four, first_row, span, 1)
        block_pos = lax.dynamic_slice_in_dim(key_pos, first_row, span, 0)
        block_seg = lax.dynamic_slice_in_dim(key_seg, first_row, span, 1)
        allowed = (query_seg[:, :, None] == block_seg[:, None, :]) & (
            block_pos[None, None, :] <= query_pos[None, :, None]
        )
        scores = (
            jnp.einsum(
                "rqhd,rkhd->rhqk", query_four, block_keys, preferred_element_type=jnp.float32
            )
            * scale_factor
        )
        return (first_row, block_keys, block_values, allowed[:, None], scores)

    def forward_block(carry, block_index):
        row_top, running, weighted = carry
        first_row, block_keys, block_values, allowed, scores = block_inputs(block_index)
        new_top = jnp.maximum(row_top, jnp.max(jnp.where(allowed, scores, MASKED), axis=-1))
        probs = jnp.where(allowed, jnp.exp(scores - new_top[..., None]), 0.0)
        factor = jnp.exp(row_top - new_top)
        running = running * factor + jnp.sum(probs, axis=-1)
        weighted = weighted * factor[..., None] + jnp.einsum(
            "rhqk,rkhd->rhqd",
            probs.astype(jnp.bfloat16),
            block_values,
            preferred_element_type=jnp.float32,
        )
        return ((new_top, running, weighted), None)

    start_top = jnp.full((row_count, local_heads, query_len), MASKED, jnp.float32)
    start_total = jnp.zeros((row_count, local_heads, query_len), jnp.float32)
    start_weighted = jnp.zeros((row_count, local_heads, query_len, HD), jnp.float32)
    (row_top, running, weighted), _ = lax.scan(
        forward_block, (start_top, start_total, start_weighted), jnp.arange(block_count)
    )
    log_total = row_top + jnp.log(running)
    attended_heads = (
        (weighted / running[..., None])
        .transpose(0, 2, 1, 3)
        .reshape(row_count, query_len, head_width)
        .astype(jnp.bfloat16)
    )
    attended_loc = lax.all_to_all(attended_heads, "seq", split_axis=1, concat_axis=2, tiled=True)
    att_flat = attended_loc.reshape(token_count, features)
    middle = flat + forward_product(att_flat, 1)
    normed_mid, norm2_back = jax.vjp(layer_norm, middle, norm2_gain, norm2_bias)
    mid_low = normed_mid.astype(jnp.bfloat16)
    gate_up = forward_product(mid_low, 2)
    act_value, silu_back = jax.vjp(
        lambda gate_part, up_part: jax.nn.silu(gate_part) * up_part,
        gate_up[:, :ff_width],
        gate_up[:, ff_width:],
    )
    act_low = act_value.astype(jnp.bfloat16)
    result = middle + forward_product(act_low, 3)
    d_out = cotangent.reshape(token_count, features)
    d_act = backward_product(d_out, 3)
    d_gate, d_up = silu_back(d_act)
    d_gate_up = jnp.concatenate([d_gate, d_up], axis=1).astype(jnp.bfloat16)
    d_mid_norm = backward_product(d_gate_up, 2)
    d_middle_part, d_gain_two, d_bias_two = norm2_back(d_mid_norm)
    d_middle = d_out.astype(jnp.float32) + d_middle_part
    d_branch = d_middle.astype(jnp.bfloat16)
    d_attended = (
        backward_product(d_branch, 1).astype(jnp.bfloat16).reshape(row_count, local_len, features)
    )
    d_heads = lax.all_to_all(d_attended, "seq", split_axis=2, concat_axis=1, tiled=True)
    d_heads_four = d_heads.reshape(row_count, query_len, local_heads, HD)
    attended_four = attended_heads.reshape(row_count, query_len, local_heads, HD)
    delta = jnp.einsum(
        "rqhd,rqhd->rhq", d_heads_four.astype(jnp.float32), attended_four.astype(jnp.float32)
    )

    def backward_block(carry, block_index):
        d_query, d_keys_all, d_values_all = carry
        first_row, block_keys, block_values, allowed, scores = block_inputs(block_index)
        probs = jnp.where(allowed, jnp.exp(scores - log_total[..., None]), 0.0)
        d_block_values = jnp.einsum(
            "rhqk,rqhd->rkhd",
            probs.astype(jnp.bfloat16),
            d_heads_four,
            preferred_element_type=jnp.float32,
        )
        d_probs = jnp.einsum(
            "rqhd,rkhd->rhqk", d_heads_four, block_values, preferred_element_type=jnp.float32
        )
        d_scores = (probs * (d_probs - delta[..., None])).astype(jnp.bfloat16)
        d_query = (
            d_query
            + jnp.einsum(
                "rhqk,rkhd->rqhd", d_scores, block_keys, preferred_element_type=jnp.float32
            )
            * scale_factor
        )
        d_block_keys = (
            jnp.einsum("rhqk,rqhd->rkhd", d_scores, query_four, preferred_element_type=jnp.float32)
            * scale_factor
        )
        d_keys_all = lax.dynamic_update_slice_in_dim(d_keys_all, d_block_keys, first_row, 1)
        d_values_all = lax.dynamic_update_slice_in_dim(d_values_all, d_block_values, first_row, 1)
        return ((d_query, d_keys_all, d_values_all), None)

    zero_query = jnp.zeros((row_count, query_len, local_heads, HD), jnp.float32)
    zero_keys = jnp.zeros((row_count, key_len, local_heads, HD), jnp.float32)
    (d_query, d_keys_all, d_values_all), _ = lax.scan(
        backward_block, (zero_query, zero_keys, zero_keys), jnp.arange(block_count)
    )
    d_keys_sum, d_values_sum = (
        lax.psum_scatter(
            d_keys_all.reshape(row_count, key_len, head_width).astype(jnp.bfloat16),
            "fsdp",
            scatter_dimension=1,
            tiled=True,
        ).astype(jnp.float32),
        lax.psum_scatter(
            d_values_all.reshape(row_count, key_len, head_width).astype(jnp.bfloat16),
            "fsdp",
            scatter_dimension=1,
            tiled=True,
        ).astype(jnp.float32),
    )
    d_query_low = d_query.reshape(row_count, query_len, head_width).astype(jnp.bfloat16)
    dq_back, dk_back, dv_back = (
        lax.all_to_all(d_query_low, "seq", split_axis=1, concat_axis=2, tiled=True),
        lax.all_to_all(
            d_keys_sum.astype(jnp.bfloat16), "seq", split_axis=1, concat_axis=2, tiled=True
        ),
        lax.all_to_all(
            d_values_sum.astype(jnp.bfloat16), "seq", split_axis=1, concat_axis=2, tiled=True
        ),
    )
    d_turned = jnp.concatenate(
        [
            dq_back.reshape(token_count, head_count, HD),
            dk_back.reshape(token_count, head_count, HD),
        ],
        axis=1,
    ).astype(jnp.float32)
    (d_turn_input,) = turn_back(d_turned)
    d_mixed = jnp.concatenate(
        [
            d_turn_input.reshape(token_count, 2 * features),
            dv_back.reshape(token_count, features).astype(jnp.float32),
        ],
        axis=1,
    ).astype(jnp.bfloat16)
    d_qkv_bias = jnp.sum(d_mixed.astype(jnp.float32), axis=0)
    d_norm_in = backward_product(d_mixed, 0)
    d_flat_part, d_gain_one, d_bias_one = norm1_back(d_norm_in)
    d_inputs = d_middle + d_flat_part
    first_grad = grad_joint(in_low, d_mixed)
    second_grad = grad_joint(att_flat, d_branch)
    third_grad = grad_joint(mid_low, d_gate_up)
    fourth_grad = grad_joint(act_low, d_out)
    qkv_grad, out_grad, gate_up_grad, down_grad = (
        lax.all_gather(first_grad.astype(jnp.bfloat16), "seq", axis=0, tiled=True).astype(
            first_grad.dtype
        ),
        lax.all_gather(second_grad.astype(jnp.bfloat16), "seq", axis=0, tiled=True).astype(
            second_grad.dtype
        ),
        lax.all_gather(third_grad.astype(jnp.bfloat16), "seq", axis=0, tiled=True).astype(
            third_grad.dtype
        ),
        lax.all_gather(fourth_grad.astype(jnp.bfloat16), "seq", axis=0, tiled=True).astype(
            fourth_grad.dtype
        ),
    )
    gain_one, bias_one, bias_qkv, gain_two, bias_two = lax.psum(
        (d_gain_one, d_bias_one, d_qkv_bias, d_gain_two, d_bias_two), ("seq", "fsdp")
    )
    return (
        result.reshape(row_count, local_len, features),
        d_inputs.reshape(row_count, local_len, features),
        gain_one,
        bias_one,
        qkv_grad,
        bias_qkv,
        out_grad,
        gain_two,
        bias_two,
        gate_up_grad,
        down_grad,
    )


BLOCK = 512
BF = jnp.bfloat16
F32 = jnp.float32
SMALL = pl.CostEstimate(flops=1000, bytes_accessed=1000, transcendentals=0)


def swap(value, mask):
    return lax.ppermute(value, ("z", "core", "fsdp"), [(i, i ^ mask) for i in range(32)])


def shift(value, steps):
    return lax.ppermute(value, ("z", "core", "fsdp"), [(i, (i + 8 * steps) % 32) for i in range(32)])


def pick(stacked, index):
    return lax.dynamic_index_in_dim(stacked, index, 0, keepdims=False)


def exchange(value, axis="fsdp"):
    return lax.all_to_all(value, axis, split_axis=0, concat_axis=0, tiled=True)


def gather_near(value):
    half = value.shape[0] // 2
    by_x = swap(value, 1)
    by_y = swap(value, 2)
    return [value, by_x, by_y, swap(by_x[:half], 2), swap(by_y[half:], 1)]


def both_cores(near):
    return near + [swap(piece, 4) for piece in near]


def gather_pieces(value):
    return both_cores(gather_near(value))


def sum_quad(terms):
    return terms[0].astype(F32) + sum(swap(terms[m].astype(BF), m).astype(F32) for m in (1, 2, 3))


def sum_plane(near, far):
    arrived = swap(far.astype(BF), 4)
    return sum_quad([near[m].astype(F32) + arrived[m].astype(F32) for m in range(4)])


def dot(left, right):
    return jnp.dot(left, right, preferred_element_type=F32)


def dot_rows(left, right):
    return lax.dot_general(left, right, (((1,), (1,)), ((), ())), preferred_element_type=F32)


def dot_cols(left, right):
    return lax.dot_general(left, right, (((0,), (0,)), ((), ())), preferred_element_type=F32)


def turn_tables(row_len):
    half_rot = ROT // 2
    lane = jnp.arange(2 * HD, dtype=jnp.int32) % HD
    exponent = (lane % half_rot).astype(F32) * (2.0 / ROT)
    inverse = jnp.power(jnp.float32(10000.0), -exponent)
    angles = jnp.arange(row_len, dtype=jnp.int32).astype(F32)[:, None] * inverse[None, :]
    cosine = jnp.where(lane < ROT, jnp.cos(angles), 1.0)
    sine = jnp.sin(angles)
    ahead = jnp.where(lane < half_rot, -sine, 0.0)
    behind = jnp.where((lane >= half_rot) & (lane < ROT), sine, 0.0)
    return cosine, ahead, behind


def attend_kernel(
    split_ref, where_ref, mixed_ref, cos_ref, ahead_ref, behind_ref,
    q_ref, k_ref, v_ref, o_ref, log_ref, mine_ref, theirs_ref, kz, vz,
):
    local_len = mixed_ref.shape[2]
    row_len = q_ref.shape[0]
    low = lax.broadcasted_iota(jnp.int32, (local_len, 2 * HD), 1) < HD

    def prepare(i, carry):
        rows = pl.ds(pl.multiple_of(i * local_len, local_len), local_len)
        cosine, ahead, behind = cos_ref[rows], ahead_ref[rows], behind_ref[rows]

        def turn(x):
            return (
                x * cosine
                + pltpu.roll(x, 2 * HD - ROT // 2, 1) * ahead
                + pltpu.roll(x, ROT // 2, 1) * behind
            )

        first = mixed_ref[i, 0]
        second = mixed_ref[i, 1]
        turned0 = turn(first[:, : 2 * HD])
        turned1 = turn(second[:, : 2 * HD])
        q = jnp.where(low, turned0, pltpu.roll(turned1, HD, 1))
        k = jnp.where(low, pltpu.roll(turned0, HD, 1), turned1)
        v = jnp.where(low, first[:, 2 * HD :], second[:, 2 * HD :])
        q_ref[rows] = (q * HD**-0.5).astype(BF)
        k_ref[rows] = k.astype(BF)
        v_ref[rows] = v.astype(BF)
        kz[0, rows] = jnp.where(low, k, 0.0).astype(BF)
        kz[1, rows] = jnp.where(low, 0.0, k).astype(BF)
        vz[0, rows] = jnp.where(low, v, 0.0).astype(BF)
        vz[1, rows] = jnp.where(low, 0.0, v).astype(BF)
        return carry

    lax.fori_loop(0, row_len // local_len, prepare, 0)
    t_in = lax.broadcasted_iota(jnp.int32, (BLOCK, 1), 0)
    u_in = lax.broadcasted_iota(jnp.int32, (1, BLOCK), 1)
    low_q = lax.broadcasted_iota(jnp.int32, (BLOCK, 2 * HD), 1) < HD

    def query_block(qb, carry):
        rows = pl.ds(pl.multiple_of(qb * BLOCK, BLOCK), BLOCK)
        q = q_ref[rows]
        t = t_in + qb * BLOCK
        outs, logs = [], []
        for row in range(2):
            split = split_ref[row]
            start = jnp.where(t >= split, split, 0)

            def step(kb, state, diagonal, row=row, start=start):
                top, total, acc = state
                keys = pl.ds(pl.multiple_of(kb * BLOCK, BLOCK), BLOCK)
                u = u_in + kb * BLOCK
                scores = dot_rows(q, kz[row, keys])
                allowed = u >= start
                if diagonal:
                    allowed = allowed & (u <= t)
                scores = jnp.where(allowed, scores, MASKED)
                new_top = jnp.maximum(top, jnp.max(scores, axis=1, keepdims=True))
                probs = jnp.exp(scores - new_top)
                factor = jnp.exp(top - new_top)
                total = total * factor + jnp.sum(probs, axis=1, keepdims=True)
                acc = acc * factor + dot(probs.astype(BF), vz[row, keys])
                return new_top, total, acc

            state = (
                jnp.full((BLOCK, 1), MASKED, F32),
                jnp.zeros((BLOCK, 1), F32),
                jnp.zeros((BLOCK, 2 * HD), F32),
            )
            first_kb = jnp.where(qb * BLOCK >= split, split // BLOCK, 0)
            state = lax.fori_loop(
                first_kb, qb, lambda kb, state, step=step: step(kb, state, False), state
            )
            top, total, acc = step(qb, state, True)
            outs.append(acc / total)
            logs.append(top + jnp.log(total))
        o_ref[rows] = (outs[0] + outs[1]).astype(BF)
        turned = jnp.where(low_q, logs[0], logs[1]).T
        log_ref[0:1, rows] = turned[0:1]
        log_ref[1:2, rows] = turned[HD : HD + 1]
        step = lax.rem(qb - where_ref[0] + 4, 4)
        core = where_ref[1] // 4
        half = BLOCK // 2
        for ref, which in ((mine_ref, core), (theirs_ref, 1 - core)):
            ref[step] = o_ref[pl.ds(pl.multiple_of(qb * BLOCK + which * half, half), half)]
        return carry

    lax.fori_loop(0, row_len // BLOCK, query_block, 0)


def attend(split, where, mixed, tables):
    row_len = tables[0].shape[0]
    packed = jax.ShapeDtypeStruct((row_len, 2 * HD), BF)
    smem = pl.BlockSpec(memory_space=pltpu.SMEM)
    vmem = pl.BlockSpec(memory_space=pltpu.VMEM)
    pairs = 2 * row_len * row_len // 2
    return pl.pallas_call(
        attend_kernel,
        out_shape=(packed, packed, packed, packed, jax.ShapeDtypeStruct((2, row_len), F32))
        + (jax.ShapeDtypeStruct((4, row_len // 8, 2 * HD), BF),) * 2,
        in_specs=[smem, smem, vmem, vmem, vmem, vmem],
        out_specs=(vmem,) * 7,
        scratch_shapes=[pltpu.VMEM((2, row_len, 2 * HD), BF), pltpu.VMEM((2, row_len, 2 * HD), BF)],
        compiler_params=pltpu.CompilerParams(vmem_limit_bytes=26 * 2**20),
        cost_estimate=SMALL,
        name="attend",
    )(split, where, mixed, *tables)


def attend_back_kernel(
    split_ref, q_hbm, k_hbm, v_hbm, o_hbm, do_hbm, log_ref,
    cos_ref, ahead_ref, behind_ref,
    dmix_ref, dpos_ref, kz, vz, qz, dz, ktz, delta, dq_t, dk, dv,
    q_ref, k_ref, v_ref, o_ref, do_ref, sem,
):
    loads = [
        pltpu.make_async_copy(source, target, sem.at[n])
        for n, (source, target) in enumerate(
            ((k_hbm, k_ref), (v_hbm, v_ref), (q_hbm, q_ref), (do_hbm, do_ref), (o_hbm, o_ref))
        )
    ]
    for copy in loads:
        copy.start()
    for copy in loads:
        copy.wait()
    row_len = q_ref.shape[0]
    local_len = dmix_ref.shape[2]
    low = lax.broadcasted_iota(jnp.int32, (BLOCK, 2 * HD), 1) < HD
    low_t = lax.broadcasted_iota(jnp.int32, (2 * HD, BLOCK), 0) < HD
    lane = lax.broadcasted_iota(jnp.int32, (8, 2 * HD), 1)
    ones = [jnp.where(lane < HD, 1.0, 0.0).astype(BF), jnp.where(lane < HD, 0.0, 1.0).astype(BF)]

    def prepare(b, carry):
        rows = pl.ds(pl.multiple_of(b * BLOCK, BLOCK), BLOCK)
        zero = jnp.zeros((BLOCK, 2 * HD), F32)
        for ref, out in ((k_ref, kz), (v_ref, vz), (q_ref, qz), (do_ref, dz)):
            value = ref[rows].astype(F32)
            out[0, rows] = jnp.where(low, value, zero).astype(BF)
            out[1, rows] = jnp.where(low, zero, value).astype(BF)
        value = k_ref[rows].astype(F32).T
        ktz[0, :, rows] = jnp.where(low_t, value, 0.0).astype(BF)
        ktz[1, :, rows] = jnp.where(low_t, 0.0, value).astype(BF)
        product = do_ref[rows].astype(F32) * o_ref[rows].astype(F32)
        coarse = product.astype(BF)
        fine = (product - coarse.astype(F32)).astype(BF)
        for row in range(2):
            delta[row, :, rows] = dot_rows(ones[row], coarse) + dot_rows(ones[row], fine)
        dq_t[:, rows] = jnp.zeros((2 * HD, BLOCK), F32)
        return carry

    lax.fori_loop(0, row_len // BLOCK, prepare, 0)
    u_in = lax.broadcasted_iota(jnp.int32, (BLOCK, 1), 0)
    t_in = lax.broadcasted_iota(jnp.int32, (1, BLOCK), 1)

    def key_block(kb, carry):
        keys = pl.ds(pl.multiple_of(kb * BLOCK, BLOCK), BLOCK)
        u = u_in + kb * BLOCK
        sums_k, sums_v = [], []
        for row in range(2):
            split = split_ref[row]
            k_row = kz[row, keys]
            v_row = vz[row, keys]
            kt_row = ktz[row, :, keys]

            def step(qb, state, row=row, split=split, k_row=k_row, v_row=v_row, kt_row=kt_row):
                d_keys, d_values = state
                rows = pl.ds(pl.multiple_of(qb * BLOCK, BLOCK), BLOCK)
                t = t_in + qb * BLOCK
                start = jnp.where(t >= split, split, 0)
                allowed = (u >= start) & (u <= t)
                scores = dot_rows(k_row, q_ref[rows])
                probs = jnp.where(allowed, jnp.exp(scores - log_ref[pl.ds(row, 1), rows]), 0.0)
                d_probs = dot_rows(v_row, do_ref[rows])
                d_scores = (probs * (d_probs - delta[row, pl.ds(0, 1), rows])).astype(BF)
                d_values = d_values + dot(probs.astype(BF), dz[row, rows])
                d_keys = d_keys + dot(d_scores, qz[row, rows])
                dq_t[:, rows] += dot(kt_row, d_scores)
                return d_keys, d_values

            zero = jnp.zeros((BLOCK, 2 * HD), F32)
            last = jnp.where(
                (kb + 1) * BLOCK <= split, (split + BLOCK - 1) // BLOCK, row_len // BLOCK
            )
            d_keys, d_values = lax.fori_loop(kb, last, step, (zero, zero))
            sums_k.append(d_keys)
            sums_v.append(d_values)
        dk[keys] = sums_k[0] + sums_k[1]
        dv[keys] = sums_v[0] + sums_v[1]
        return carry

    lax.fori_loop(0, row_len // BLOCK, key_block, 0)
    low_l = lax.broadcasted_iota(jnp.int32, (local_len, 2 * HD), 1) < HD
    per = 2 * HD // local_len


    def finish(b, carry):
        start = pl.multiple_of(b * 2 * HD, 2 * HD)
        dq = dq_t[:, pl.ds(start, 2 * HD)].T * HD**-0.5
        for part in range(per):
            i = b * per + part
            rows = pl.ds(pl.multiple_of(i * local_len, local_len), local_len)
            cosine, ahead, behind = cos_ref[rows], ahead_ref[rows], behind_ref[rows]

            def turn(x, cosine=cosine, ahead=ahead, behind=behind):
                return (
                    x * cosine
                    - pltpu.roll(x, 2 * HD - ROT // 2, 1) * ahead
                    - pltpu.roll(x, ROT // 2, 1) * behind
                )

            q_part = turn(dq[part * local_len : (part + 1) * local_len])
            k_part = turn(dk[rows])
            v_part = dv[rows]
            first = jnp.where(low_l, q_part, pltpu.roll(k_part, HD, 1)).astype(BF)
            second = jnp.where(low_l, pltpu.roll(q_part, HD, 1), k_part).astype(BF)
            dpos_ref[rows, : 2 * HD] = first
            dpos_ref[rows, 2 * HD : 4 * HD] = second
            dpos_ref[rows, 4 * HD :] = v_part.astype(BF)
            dmix_ref[i, 0, :, : 2 * HD] = first
            dmix_ref[i, 1, :, : 2 * HD] = second
            dmix_ref[i, 0, :, 2 * HD :] = jnp.where(low_l, v_part, 0.0).astype(BF)
            dmix_ref[i, 1, :, 2 * HD :] = jnp.where(low_l, pltpu.roll(v_part, HD, 1), 0.0).astype(BF)
        return carry

    lax.fori_loop(0, row_len // (2 * HD), finish, 0)


def attend_back(split, q, k, v, out, d_out, logs, tables, local_len):
    row_len = q.shape[0]
    smem = pl.BlockSpec(memory_space=pltpu.SMEM)
    vmem = pl.BlockSpec(memory_space=pltpu.VMEM)
    masked = pltpu.VMEM((2, row_len, 2 * HD), BF)
    whole = pltpu.VMEM((row_len, 2 * HD), F32)
    pairs = 2 * row_len * row_len // 2
    return pl.pallas_call(
        attend_back_kernel,
        out_shape=(
            jax.ShapeDtypeStruct((row_len // local_len, 2, local_len, 4 * HD), BF),
        )
        + (jax.ShapeDtypeStruct((row_len, 6 * HD), BF),),
        in_specs=[smem] + [pl.BlockSpec(memory_space=pltpu.HBM)] * 5 + [vmem] * 4,
        out_specs=(vmem,) * 2,
        scratch_shapes=[
            masked, masked, masked, masked,
            pltpu.VMEM((2, 2 * HD, row_len), BF),
            pltpu.VMEM((2, 8, row_len), F32),
            pltpu.VMEM((2 * HD, row_len), F32),
            whole, whole,
        ]
        + [pltpu.VMEM((row_len, 2 * HD), BF)] * 5
        + [pltpu.SemaphoreType.DMA((5,))],
        compiler_params=pltpu.CompilerParams(vmem_limit_bytes=34 * 2**20),
        cost_estimate=SMALL,
        name="attend_back",
    )(split, q, k, v, out, d_out, logs, *tables)


def pick_heads_kernel(where_ref, q_ref, k_ref, v_ref, out_ref):
    wide = 2 * HD
    low = lax.broadcasted_iota(jnp.int32, (q_ref.shape[0], wide), 1) < HD
    for core in (0, 1):

        @pl.when(where_ref[1] // 4 == core)
        def _(core=core):
            def join(left, right):
                if core == 0:
                    return jnp.where(low, left, pltpu.roll(right, HD, 1)).astype(BF)
                return jnp.where(low, pltpu.roll(left, HD, 1), right).astype(BF)

            for z in range(4):
                cols = slice(z * wide, (z + 1) * wide)
                out_ref[:, cols] = join(q_ref[:, cols].astype(F32), k_ref[:, cols].astype(F32))
            for pair in range(2):
                left, right = (
                    v_ref[:, (2 * pair + n) * wide : (2 * pair + n + 1) * wide].astype(F32) for n in (0, 1)
                )
                out_ref[:, (4 + pair) * wide : (5 + pair) * wide] = join(left, right)


def pick_heads(where, weight):
    rows, columns = weight.shape
    wide = columns // 12
    blocks = [
        pl.BlockSpec((rows, wide), lambda chip, where, part=part: (0, part * 4 + chip)) for part in range(3)
    ]
    return pl.pallas_call(
        pick_heads_kernel,
        grid_spec=pltpu.PrefetchScalarGridSpec(
            num_scalar_prefetch=1,
            grid=(4,),
            in_specs=blocks,
            out_specs=pl.BlockSpec((None, rows, 12 * HD), lambda chip, where: (chip, 0, 0)),
        ),
        out_shape=jax.ShapeDtypeStruct((4, rows, 12 * HD), BF),
        compiler_params=pltpu.CompilerParams(vmem_limit_bytes=32 * 2**20),
        cost_estimate=SMALL,
        name="pick_heads",
    )(where, weight, weight, weight)


def small_call(kernel, name, out_shape, where, *arrays, flops=0, scratch=(), limit=20):
    size = sum(x.size * x.dtype.itemsize for x in arrays)
    vmem = pl.BlockSpec(memory_space=pltpu.VMEM)
    return pl.pallas_call(
        kernel,
        out_shape=out_shape,
        in_specs=[pl.BlockSpec(memory_space=pltpu.SMEM)] + [vmem] * len(arrays),
        out_specs=[vmem] * len(out_shape),
        scratch_shapes=scratch,
        compiler_params=pltpu.CompilerParams(vmem_limit_bytes=limit * 2**20),
        cost_estimate=SMALL,
        name=name,
    )(where, *arrays)


def pair_kernel(where_ref, mine_ref, theirs_ref, *outs):
    low = lax.broadcasted_iota(jnp.int32, mine_ref.shape[1:], 1) < HD
    for step, out in enumerate(outs):
        for core, (ref0, ref1) in enumerate(((mine_ref, theirs_ref), (theirs_ref, mine_ref))):

            @pl.when(where_ref[1] // 4 == core)
            def _(ref0=ref0, ref1=ref1):
                even, uneven = ref0[step].astype(F32), ref1[step].astype(F32)
                out[:, : 2 * HD] = jnp.where(low, even, pltpu.roll(uneven, HD, 1)).astype(BF)
                out[:, 2 * HD :] = jnp.where(low, pltpu.roll(even, HD, 1), uneven).astype(BF)


def out_project_kernel(where_ref, a0, a1, a2, a3, weight_ref, att_ref, o0, o1, o2, o3, sum_v):
    plane, rank = where_ref[0], where_ref[1] % 4
    span = a0.shape[0]
    for step, ref in enumerate((a0, a1, a2, a3)):
        lanes = pl.ds(pl.multiple_of(lax.rem(plane - step + 4, 4) * 2 * HD, 2 * HD), 2 * HD)
        for row in range(2):
            att_ref[row * span : (row + 1) * span, lanes] = ref[:, row * 2 * HD : (row + 1) * 2 * HD]
    sum_v[...] = dot(att_ref[...], weight_ref[...])
    part = span // 4
    for m, out in enumerate((o0, o1, o2, o3)):
        for row in range(2):
            rows = pl.ds(pl.multiple_of(row * span + (rank ^ m) * part, part), part)
            out[row * part : (row + 1) * part] = sum_v[rows].astype(out.dtype)


def d_att_kernel(where_ref, p0, p1, p2, p3_low, p3_high, weight_ref, branch_ref, heads_ref):
    rank = where_ref[1] % 4
    span = heads_ref.shape[1]
    part = span // 4
    for m, pieces in enumerate(((p0,), (p1,), (p2,), (p3_low, p3_high))):
        for row in range(2):
            rows = pl.ds(pl.multiple_of(row * span + (rank ^ m) * part, part), part)
            if len(pieces) == 2:
                branch_ref[rows] = pieces[row][...]
            else:
                branch_ref[rows] = pieces[0][row * part : (row + 1) * part]
    d_att = dot_rows(branch_ref[...], weight_ref[...])
    low = lax.broadcasted_iota(jnp.int32, heads_ref.shape[1:], 1) < HD
    for z in range(4):
        lanes = slice(z * 2 * HD, (z + 1) * 2 * HD)
        row0, row1 = d_att[:span, lanes], d_att[span:, lanes]
        heads_ref[2 * z] = jnp.where(low, row0, pltpu.roll(row1, HD, 1)).astype(BF)
        heads_ref[2 * z + 1] = jnp.where(low, pltpu.roll(row0, HD, 1), row1).astype(BF)


def d_in_kernel(where_ref, in_ref, weight_ref, near_ref, far_ref, x_v, d_v):
    core, rank = where_ref[1] // 4, where_ref[1] % 4
    reach, wide = in_ref.shape[1], 2 * HD
    features = weight_ref.shape[0]
    low = lax.broadcasted_iota(jnp.int32, (reach, wide), 1) < HD
    for z in range(4):
        for row in range(2):
            x_v[row * reach : (row + 1) * reach, z * wide : (z + 1) * wide] = in_ref[
                z, :, row * wide : (row + 1) * wide
            ]
    for pair in range(2):
        cols = slice((4 + pair) * wide, (5 + pair) * wide)
        one, two = (in_ref[2 * pair + n, :, 2 * wide :].astype(F32) for n in (0, 1))
        x_v[:reach, cols] = jnp.where(low, one, pltpu.roll(two, HD, 1)).astype(BF)
        x_v[reach:, cols] = jnp.where(low, pltpu.roll(one, HD, 1), two).astype(BF)
    part = reach // 8
    span = d_v.shape[1]

    def columns(n, carry):
        cols = pl.ds(pl.multiple_of(n * span, span), span)
        d_v[...] = dot_rows(x_v[...], weight_ref[cols])
        for ref, which in ((near_ref, core), (far_ref, 1 - core)):
            for m in range(4):
                for row in range(2):
                    first = row * reach + which * 4 * part + (rank ^ m) * part
                    rows = pl.ds(pl.multiple_of(first, part), part)
                    ref[m, row * part : (row + 1) * part, cols] = d_v[rows].astype(BF)
        return carry

    lax.fori_loop(0, features // span, columns, 0)


def hidden_kernel(where_ref, *refs, steps, own):
    n_mid, n_out = (10, 2) if own else (1, 4 * len(steps))
    mids, outs, refs = refs[:n_mid], refs[n_mid : n_mid + n_out], refs[n_mid + n_out :]
    gate_ref, up_ref, down_ref = refs[:3]
    refs = refs[3:] if own else refs[7:]
    alls, refs = refs[:4], refs[4:]
    d_mids, acts, refs = (refs[:2], refs[2:4], refs[4:]) if own else ((), (), refs)
    mid_v, out_v, gate_up_v, down_v, act_v, d_gate_v, d_up_v, sem_in, sem_w, sem_out = refs[:10]
    rows, features = mid_v.shape[1:]
    width, tile = down_v.shape[0], 256
    tiles = width // tile
    plane, mine = where_ref[0], where_ref[1]
    core = mine // 4
    shard = gate_ref.shape[1]
    step = rows // 4
    halves = 2 * len(steps)

    def blocks(h):
        base = lax.rem(plane + 4 - steps[h // 2], 4) * (2 * rows)
        return [
            pl.ds(pl.multiple_of(base + (mine ^ (4 * (h % 2) + m)) * step, step), step) for m in range(4)
        ]

    def loads(h):
        slot = h % 2
        if own:
            pieces, out_pieces = mids[5 * h : 5 * h + 5], outs[h : h + 1]
        else:
            pieces = [mids[0].at[block] for block in blocks(h)]
            out_pieces = outs[2 * h : 2 * h + 2]
        found = []
        for held, sources in ((mid_v, pieces), (out_v, out_pieces)):
            at = 0
            for source in sources:
                size = source.shape[0]
                found.append((source, held.at[slot, pl.ds(at, size)]))
                at += size
        return [pltpu.make_async_copy(x, y, sem_in.at[slot, n]) for n, (x, y) in enumerate(found)]

    def stores(h):
        slot = h % 2
        return [
            pltpu.make_async_copy(
                held.at[slot, pl.ds(m * step, step)], target.at[block], sem_out.at[slot, n, m]
            )
            for n, (held, target) in enumerate(zip((act_v, d_gate_v, d_up_v, out_v), alls))
            for m, block in enumerate(blocks(h))
        ]

    def tile_copies(j):
        cols = pl.ds(j * tile, tile)
        found = [
            (ref.at[m, :, cols], gate_up_v.at[g, pl.ds(m * shard, shard), cols])
            for g, ref in enumerate((gate_ref, up_ref))
            for m in range(4)
        ]
        first = pl.multiple_of(core * (down_ref.shape[0] - width) + j * tile, 128)
        found.append((down_ref.at[pl.ds(first, tile)], down_v.at[cols]))
        return [pltpu.make_async_copy(x, y, sem_w.at[j, n]) for n, (x, y) in enumerate(found)]

    def wait_tile(j):
        for copy in weight_copies[j]:
            copy.wait()
        if j == 0:

            @pl.when(core == 1)
            def _():
                gate_up_v[:, :, : 2 * width - down_ref.shape[0]] = jnp.zeros(
                    (2, features, 2 * width - down_ref.shape[0]), BF
                )

    def compute(slot, cols):
        gate = dot(mid_v[slot], gate_up_v[0, :, cols])
        up = dot(mid_v[slot], gate_up_v[1, :, cols])
        d_act = dot_rows(out_v[slot], down_v[cols])
        sig = 1.0 / (1.0 + jnp.exp(-gate))
        silu = gate * sig
        act_v[slot, :, cols] = (silu * up).astype(BF)
        d_gate_v[slot, :, cols] = (d_act * up * (sig + silu * (1.0 - sig))).astype(BF)
        d_up_v[slot, :, cols] = (d_act * silu).astype(BF)

    weight_copies = [tile_copies(j) for j in range(tiles)]
    for copies in [weight_copies[0], loads(0)] + weight_copies[1:] + [loads(1)]:
        for copy in copies:
            copy.start()
    for h in range(halves):
        slot = h % 2
        for copy in loads(h):
            copy.wait()
        if h == 0:
            for j in range(tiles):
                wait_tile(j)
                compute(0, pl.ds(j * tile, tile))
        else:
            compute(slot, pl.ds(0, tile))
            if h + 1 < halves:
                for copy in stores(h - 1):
                    copy.wait()
                for copy in loads(h + 1):
                    copy.start()

            def part(j, carry, slot=slot):
                compute(slot, pl.ds(pl.multiple_of(j * tile, tile), tile))
                return carry

            lax.fori_loop(1, tiles, part, 0)
        for copy in stores(h):
            copy.start()
    left = []
    if own:
        sum_v = refs[10]
        span = 512
        for i in (1, 0):
            for m in range(4):
                part = pl.ds(m * step, step)
                left.append(
                    pltpu.make_async_copy(act_v.at[i, part], acts[i].at[m], sem_out.at[i, 4, m])
                )
                left[-1].start()

            def term(n, carry, i=i):
                cols = pl.ds(pl.multiple_of(n * span, span), span)
                sum_v[i, :, cols] = (
                    dot_rows(d_gate_v[i], gate_up_v[0, cols]) + dot_rows(d_up_v[i], gate_up_v[1, cols])
                ).astype(BF)
                return carry

            lax.fori_loop(0, features // span, term, 0)
            for m in range(4):
                part = pl.ds(m * step, step)
                left.append(
                    pltpu.make_async_copy(sum_v.at[i, part], d_mids[i].at[m], sem_out.at[i, 5, m])
                )
                left[-1].start()
    for h in (halves - 2, halves - 1):
        left += stores(h)
    for copy in left:
        copy.wait()


def hidden_layer(where, mids, outs, weights, total, steps=(0,), before=None):
    own = before is None
    features = outs[0].shape[1]
    rows, width = total // 8, weights[0].shape[2]
    narrow = jax.ShapeDtypeStruct((total, width), BF)
    wide = jax.ShapeDtypeStruct((total, features), BF)
    term = jax.ShapeDtypeStruct((4, rows // 4, features), BF)
    act = jax.ShapeDtypeStruct((4, rows // 4, width), BF)
    held = pltpu.VMEM((2, rows, features), BF)
    small = pltpu.VMEM((2, rows, width), BF)
    dma = pltpu.SemaphoreType.DMA
    count = len(mids) + len(outs)
    kept = [] if own else list(before)
    hbm = pl.BlockSpec(memory_space=pltpu.HBM)
    found = pl.pallas_call(
        functools.partial(hidden_kernel, steps=steps, own=own),
        in_specs=[pl.BlockSpec(memory_space=pltpu.SMEM)] + [hbm] * (count + 3 + len(kept)),
        out_specs=[hbm] * (8 if own else 4),
        out_shape=[narrow, narrow, narrow, wide] + ([term, term, act, act] if own else []),
        input_output_aliases={count + 4 + n: n for n in range(len(kept))},
        scratch_shapes=[
            held, held,
            pltpu.VMEM((2, features, width), BF),
            pltpu.VMEM((width, features), BF),
            small, small, small,
            dma((2, 9)), dma((width // 256, 9)), dma((2, 6, 4)),
        ]
        + ([held] if own else []),
        compiler_params=pltpu.CompilerParams(vmem_limit_bytes=(38 if own else 32) * 2**20),
        cost_estimate=SMALL,
        name="hidden",
    )(where, *mids, *outs, *weights, *kept)
    return list(found[:4]), list(found[4:])


def weight_grad_kernel(left_ref, right_ref, out_ref):
    out_ref[...] = dot_cols(left_ref[...], right_ref[...]).astype(BF)


def weight_grad(left, right):
    tokens, features = left.shape
    width = right.shape[1]
    step = 256
    return pl.pallas_call(
        weight_grad_kernel,
        grid=(features // step,),
        in_specs=[
            pl.BlockSpec((tokens, step), lambda i: (0, i)),
            pl.BlockSpec((tokens, width), lambda i: (0, 0), pipeline_mode=pl.Buffered(1)),
        ],
        out_specs=pl.BlockSpec((step, width), lambda i: (i, 0)),
        out_shape=jax.ShapeDtypeStruct((features, width), BF),
        compiler_params=pltpu.CompilerParams(vmem_limit_bytes=48 * 2**20),
        cost_estimate=SMALL,
        name="weight_grad",
    )(left, right)


def place_columns_kernel(where_ref, own_ref, other_ref, *rest):
    out_ref = rest[-1]
    wide = own_ref.shape[-1]
    extra = out_ref.shape[-1] - wide

    @pl.when(where_ref[0] == 0)
    def _():
        out_ref[:, :wide] = own_ref[...].astype(F32)
        out_ref[:, wide:] = other_ref[:, wide - extra :].astype(F32)

    @pl.when(where_ref[0] == 1)
    def _():
        out_ref[:, :wide] = other_ref[...].astype(F32)
        out_ref[:, wide:] = own_ref[:, wide - extra :].astype(F32)


def place_columns(core, own, other, before, chip_width, kind):
    chips, rows, wide = own.shape
    cut = rows // 2
    half = pl.BlockSpec((None, cut, wide), lambda chip, b, core: (chip, b, 0))
    return pl.pallas_call(
        place_columns_kernel,
        grid_spec=pltpu.PrefetchScalarGridSpec(
            num_scalar_prefetch=1,
            grid=(chips, rows // cut),
            in_specs=[half, half] + ([] if before is None else [pl.BlockSpec(memory_space=pl.ANY)]),
            out_specs=pl.BlockSpec((cut, chip_width), lambda chip, b, core: (b, kind * chips + chip)),
        ),
        out_shape=jax.ShapeDtypeStruct((rows, 2 * chips * chip_width), F32),
        input_output_aliases={} if before is None else {3: 0},
        compiler_params=pltpu.CompilerParams(vmem_limit_bytes=32 * 2**20),
        cost_estimate=SMALL,
        name="place_columns",
    )(core, own, other, *([] if before is None else [before]))


def place_down_kernel(core_ref, own_ref, other_ref, out_ref, *, lead):
    first = pl.program_id(0) < lead
    mine = first == (core_ref[0] == 0)

    @pl.when(mine)
    def _():
        out_ref[...] = own_ref[...].astype(F32)

    @pl.when(jnp.logical_not(mine))
    def _():
        out_ref[...] = other_ref[...].astype(F32)


def place_down(core, own, other, total):
    width, features = own.shape
    step = 128
    count, lead = total // step, width // step
    skip = 2 * lead - count

    def block(of_core):
        def index(i, core):
            which = core[0] if of_core else 1 - core[0]
            return (jnp.where(which == 0, jnp.minimum(i, lead - 1), jnp.maximum(i - lead + skip, 0)), 0)

        return pl.BlockSpec((step, features), index)

    return pl.pallas_call(
        functools.partial(place_down_kernel, lead=lead),
        grid_spec=pltpu.PrefetchScalarGridSpec(
            num_scalar_prefetch=1,
            grid=(count,),
            in_specs=[block(True), block(False)],
            out_specs=pl.BlockSpec((step, features), lambda i, core: (i, 0)),
        ),
        out_shape=jax.ShapeDtypeStruct((total, features), F32),
        cost_estimate=SMALL,
        name="place_down",
    )(core, own, other)


def place_qkv_kernel(where_ref, own_ref, other_ref, out_ref):
    cut = own_ref.shape[2]
    core = where_ref[0]
    for ref, half in ((own_ref, core), (other_ref, 1 - core)):
        rows = pl.ds(pl.multiple_of(half * cut, cut), cut)
        for z in range(4):
            out_ref[rows, z * 2 * HD : (z + 1) * 2 * HD] = ref[z, 0].astype(F32)


def place_qkv(where, own, other):
    _, _, cut, wide = own.shape
    parts = wide // (2 * HD)
    piece = pl.BlockSpec((4, 1, cut, 2 * HD), lambda part, chip, where: (0, chip ^ where[1], 0, part))
    return pl.pallas_call(
        place_qkv_kernel,
        grid_spec=pltpu.PrefetchScalarGridSpec(
            num_scalar_prefetch=1,
            grid=(parts, 4),
            in_specs=[piece, piece],
            out_specs=pl.BlockSpec((2 * cut, 8 * HD), lambda part, chip, where: (0, part * 4 + chip)),
        ),
        out_shape=jax.ShapeDtypeStruct((2 * cut, parts * 32 * HD), F32),
        cost_estimate=SMALL,
        name="place_qkv",
    )(where, own, other)


def tie(*values):
    return lax.optimization_barrier(values)


def plane_plan(
    inputs,
    segments,
    norm1_gain,
    norm1_bias,
    qkv_weight,
    qkv_bias,
    out_weight,
    norm2_gain,
    norm2_bias,
    gate_up_weight,
    down_weight,
    cotangent,
):
    row_count, local_len, features = inputs.shape
    row_len = segments.shape[1]
    tokens = row_count * local_len
    plane, core, rank = lax.axis_index("z"), lax.axis_index("core"), lax.axis_index("fsdp")
    seq = plane * 2 + core
    own = core * 4 + rank
    shard = features // 4
    hidden = gate_up_weight.shape[1] // 2
    chip_width = hidden // 4
    width = -(-chip_width // 256) * 128
    tables = turn_tables(row_len)
    split = jnp.sum((segments == 0).astype(jnp.int32), axis=1)
    where = jnp.stack([plane, own]).astype(jnp.int32)

    def head_columns(chip):
        parts = [
            lax.dynamic_slice_in_dim(qkv_weight, (chip * 8 + seq) * HD + part * features, HD, 1)
            for part in (0, 1, 2)
        ]
        return jnp.concatenate(parts + parts[2:], axis=1)

    head_weight = exchange(jnp.stack([head_columns(chip) for chip in range(4)])).reshape(features, 4 * HD)
    picked = pick_heads(where, qkv_weight)
    head_first = (rank * 8 + seq) * HD
    bias_parts = [
        lax.dynamic_slice_in_dim(qkv_bias, head_first + part * features, HD, 0) for part in (0, 1, 2)
    ]
    head_bias = jnp.concatenate(bias_parts + bias_parts[2:])
    hidden_first = core * (chip_width - width)

    def hidden_columns(kind):
        firsts = [hidden_first + chip * chip_width + kind * hidden for chip in range(4)]
        return jnp.stack([lax.dynamic_slice_in_dim(gate_up_weight, first, width, 1) for first in firsts])

    gate_weight, up_weight = hidden_columns(0), hidden_columns(1)

    flat = inputs.reshape(tokens, features).astype(F32)
    normed_in, norm1_back = jax.vjp(layer_norm, flat, norm1_gain, norm1_bias)
    everywhere = ("z", "core", "fsdp")
    in_all = lax.all_gather(normed_in.astype(BF), everywhere, axis=0, tiled=True)
    d_out = cotangent.reshape(tokens, features)
    out_near = jnp.concatenate(gather_near(d_out), axis=0)
    out_far = swap(out_near, 4)
    in_all, out_near, out_far, gate_weight, up_weight, head_weight, picked, *tables = tie(
        in_all, out_near, out_far, gate_weight, up_weight, head_weight, picked, *tables
    )
    lows, highs = [out_near[: 2 * tokens]], [out_near[2 * tokens :]]

    mixed = (dot(in_all, head_weight) + head_bias).reshape(
        row_len // local_len, row_count, local_len, 4 * HD
    )
    q, k, v, out_heads, logs, mine, theirs, gate_weight, low, up_weight = tie(
        *attend(split, where, mixed, tables), exchange(gate_weight), shift(lows[0], 1), up_weight
    )
    lows.append(low)
    span = row_len // 8
    pair = jax.ShapeDtypeStruct((span, 4 * HD), BF)
    pairs = small_call(pair_kernel, "pair", [pair] * 4, where, mine, swap(theirs, 4))
    arrived = [pairs[0]] + [shift(pairs[n], n) for n in (1, 2, 3)]
    square = row_count * span
    block = jax.ShapeDtypeStruct((tokens, features), BF)
    blocks = jax.ShapeDtypeStruct((4, tokens, features), BF)
    att, *branch = small_call(
        out_project_kernel,
        "out_project",
        [jax.ShapeDtypeStruct((square, shard), BF), jax.ShapeDtypeStruct((tokens, features), F32)]
        + [block] * 3,
        where,
        *arrived,
        out_weight,
        scratch=[pltpu.VMEM((square, features), F32)],
    )
    branch_sum, up_weight, high = tie(sum_quad(branch), exchange(up_weight), shift(highs[0], 1))
    highs.append(high)
    hidden_weights = [gate_weight, up_weight, down_weight]
    middle = flat + branch_sum
    normed_mid, norm2_back = jax.vjp(layer_norm, middle, norm2_gain, norm2_bias)
    mid_low = normed_mid.astype(BF)

    mid_pieces = gather_pieces(mid_low)
    *mid_pieces, mid_own, low = tie(*mid_pieces, mid_low, shift(lows[1], 1))
    lows.append(low)
    mid_all = lax.all_gather(mid_own, everywhere, axis=0, tiled=True)
    total = row_count * row_len
    hidden_all, (d_near, d_far, act_near, act_far) = hidden_layer(
        where, mid_pieces, [out_near, out_far], hidden_weights, total
    )
    d_near, d_far, high = tie(d_near, d_far, shift(highs[1], 1))
    highs.append(high)
    d_norm_mid, low = tie(sum_plane(d_near, d_far), shift(lows[2], 1))
    lows.append(low)
    d_middle_part, d_gain_two, d_bias_two = norm2_back(d_norm_mid)
    d_middle = d_out.astype(F32) + d_middle_part

    d_pieces = gather_near(d_middle.astype(BF))
    d_branch, d_heads = small_call(
        d_att_kernel,
        "d_att",
        [
            jax.ShapeDtypeStruct((square, features), BF),
            jax.ShapeDtypeStruct((8, span, 2 * HD), BF),
        ],
        where,
        *d_pieces,
        out_weight,
    )
    d_heads = exchange(d_heads, ("z", "core")).reshape(row_len, 2 * HD)
    d_heads, high_own = tie(d_heads, highs[2])
    d_packed, d_mixed, mid_all, high = tie(
        *attend_back(split, q, k, v, out_heads, d_heads, logs, tables, local_len)[::-1],
        mid_all,
        shift(high_own, 1),
    )
    highs.append(high)

    arrived = exchange(d_packed.reshape(4, row_len // 4, 6 * HD), "z")
    d_mixed = d_mixed.reshape(row_len * row_count, 4 * HD)
    head_grad = dot_cols(in_all, d_mixed)[:, : 3 * HD].astype(BF)
    cut = shard // 2
    head_grad = head_grad.reshape(4, 2, cut, 3 * HD)
    mine = lax.dynamic_index_in_dim(head_grad, core, 1, keepdims=False)
    theirs = swap(lax.dynamic_index_in_dim(head_grad, 1 - core, 1, keepdims=False), 4)
    first, second = jnp.where(core == 0, mine, theirs), jnp.where(core == 0, theirs, mine)
    pairs = jnp.concatenate(
        [half[:, :, p * HD : (p + 1) * HD] for p in range(3) for half in (first, second)], axis=2
    )
    down = lax.dynamic_slice_in_dim(down_weight, hidden_first, width, 0)
    result_sum = sum_plane(
        dot(act_near.reshape(4 * tokens, width), down).reshape(4, tokens, features),
        dot(act_far.reshape(4 * tokens, width), down).astype(BF).reshape(4, tokens, features),
    )

    def rest(steps, before):
        outs = [
            piece for n in steps for piece in (lows[n], highs[n], swap(lows[n], 4), swap(highs[n], 4))
        ]
        return hidden_layer(where, [mid_all], outs, hidden_weights, total, steps, before)[0]

    hidden_all = rest((1, 2), hidden_all)
    arrived, result_sum, pairs, att, d_branch, picked, *hidden_all = tie(
        arrived, result_sum, pairs, att, d_branch, picked, *hidden_all
    )
    result = middle + result_sum

    pairs = [pick(pairs, rank ^ m) for m in range(4)]
    pairs = [pairs[0]] + [swap(pairs[m], m) for m in (1, 2, 3)]
    head_all = exchange(picked).reshape(features, 12 * HD)
    out_part = dot_cols(att, d_branch).astype(BF)
    out_part = lax.psum_scatter(out_part, ("z", "core"), scatter_dimension=0, tiled=True)
    act_all, d_gate_all, d_up_all, out_all = rest((3,), hidden_all)
    head_all, d_gate_grad, d_up_all, act_all, arrived, out_part, *pairs = tie(
        head_all, weight_grad(mid_all, d_gate_all), d_up_all, act_all, arrived, out_part, *pairs
    )

    by_chip = (4, shard, width)
    near, far = small_call(
        d_in_kernel,
        "d_in",
        [blocks] * 2,
        where,
        arrived,
        head_all,
        scratch=[
            pltpu.VMEM((8 * tokens, 12 * HD), BF),
            pltpu.VMEM((8 * tokens, 512), F32),
        ],
        limit=24,
    )
    heads = lax.all_gather(jnp.stack(pairs), "z", axis=0)
    gate_parts, d_up_grad, near, far, act_all = tie(
        exchange(d_gate_grad.reshape(by_chip)),
        weight_grad(mid_all, d_up_all),
        near,
        swap(far, 4),
        act_all,
    )
    d_norm_in, down_own, d_up_grad = tie(
        sum_quad([near[m].astype(F32) + far[m].astype(F32) for m in range(4)]),
        weight_grad(act_all, out_all),
        d_up_grad,
    )

    core_index = core.reshape(1).astype(jnp.int32)
    up_parts = exchange(d_up_grad.reshape(by_chip))
    out_rows = lax.all_gather(out_part, ("z", "core"), axis=0, tiled=True)
    gate_up_grad = place_columns(core_index, gate_parts, swap(gate_parts, 4), None, chip_width, 0)
    down_grad = place_down(core_index, down_own, swap(down_own, 4), chip_width)
    d_flat_part, d_gain_one, d_bias_one = norm1_back(d_norm_in)
    d_inputs = d_middle + d_flat_part
    bias_sum = jnp.sum(d_mixed.astype(F32), axis=0)
    bias_own = jnp.zeros((3 * features,), F32)
    for part in range(3):
        bias_own = lax.dynamic_update_slice_in_dim(
            bias_own, bias_sum[part * HD : (part + 1) * HD], head_first + part * features, 0
        )
    sums = jnp.concatenate([d_gain_one, d_bias_one, bias_own, d_gain_two, d_bias_two])
    sums = sums + swap(sums, 4)
    sums = sums + sum(shift(sums, n) for n in (1, 2, 3))
    qkv_grad = place_qkv(jnp.stack([core, rank]).astype(jnp.int32), heads, swap(heads, 4))
    up_parts, sums, gate_up_grad, down_grad, qkv_grad = tie(
        up_parts, sums, gate_up_grad, down_grad, qkv_grad
    )
    sums = sums + sum(swap(sums, m) for m in (1, 2, 3))
    out_grad = out_rows.astype(F32)
    gate_up_grad = place_columns(
        core_index, up_parts, swap(up_parts, 4), gate_up_grad, chip_width, 1
    )
    return (
        result.reshape(row_count, local_len, features),
        d_inputs.reshape(row_count, local_len, features),
        sums[:features],
        sums[features : 2 * features],
        qkv_grad,
        sums[2 * features : 5 * features],
        out_grad,
        sums[5 * features : 6 * features],
        sums[6 * features :],
        gate_up_grad,
        down_grad,
    )


def solution(mesh):
    planes = (mesh.shape["seq"], mesh.shape["fsdp"]) == (8, 4)
    plan = plane_plan if planes else general_plan
    if planes:
        mesh = jax.sharding.Mesh(mesh.devices.reshape(4, 2, 4), ("z", "core", "fsdp"))
    spread = P(None, (*mesh.axis_names,), None)
    placed = (
        spread,
        P(),
        P(),
        P(),
        P("fsdp", None),
        P(),
        P("fsdp", None),
        P(),
        P(),
        P("fsdp", None),
        P("fsdp", None),
        spread,
    )
    return jax.shard_map(
        plan,
        mesh=mesh,
        in_specs=placed,
        out_specs=(
            spread,
            spread,
            P(),
            P(),
            P("fsdp", None),
            P(),
            P("fsdp", None),
            P(),
            P(),
            P("fsdp", None),
            P("fsdp", None),
        ),
        check_vma=False,
    )
```

```python
import functools

import jax
import jax.numpy as jnp
from jax import lax
from jax.experimental import pallas as pl
from jax.experimental.pallas import tpu as pltpu
from jax.sharding import PartitionSpec as P

HD = 64
ROT = 16


EPSILON = 1e-05
MASKED = -1e30


def layer_norm(values, norm_gain, offset):
    average = jnp.mean(values, axis=-1, keepdims=True)
    centred = values - average
    variance = jnp.mean(centred * centred, axis=-1, keepdims=True)
    return centred * lax.rsqrt(variance + EPSILON) * norm_gain + offset


def rotate(values, positions):
    half_rot = ROT // 2
    exponent = jnp.arange(half_rot, dtype=jnp.float32) * (2.0 / ROT)
    inverse = jnp.power(jnp.float32(10000.0), -exponent)
    angles = positions.astype(jnp.float32)[:, None] * inverse[None, :]
    cosine = jnp.cos(angles)[:, None, :]
    sine = jnp.sin(angles)[:, None, :]
    first = values[:, :, :half_rot]
    second = values[:, :, half_rot:ROT]
    return jnp.concatenate(
        [first * cosine - second * sine, second * cosine + first * sine, values[:, :, ROT:]], axis=2
    )


def fold_rows(left, shard):
    return jnp.dot(
        left, lax.all_gather(shard, "fsdp", axis=0, tiled=True), preferred_element_type=jnp.float32
    )


def map_back(grad_rows, shard):
    return lax.dot_general(
        grad_rows,
        lax.all_gather(shard, "fsdp", axis=0, tiled=True),
        (((1,), (1,)), ((), ())),
        preferred_element_type=jnp.float32,
    )


def grad_joint(left, right_side):
    seq_count = lax.axis_size("seq")
    fsdp_count = lax.axis_size("fsdp")
    token_count, total_rows = left.shape
    share = total_rows // (seq_count * fsdp_count)
    permuted = (
        left.reshape(token_count, fsdp_count, seq_count, share)
        .transpose(0, 2, 1, 3)
        .reshape(token_count, total_rows)
    )
    return lax.psum_scatter(
        lax.dot_general(
            permuted, right_side, (((0,), (0,)), ((), ())), preferred_element_type=jnp.float32
        ),
        ("seq", "fsdp"),
        scatter_dimension=0,
        tiled=True,
    )


def general_plan(
    inputs,
    segments,
    norm1_gain,
    norm1_bias,
    qkv_weight,
    qkv_bias,
    out_weight,
    norm2_gain,
    norm2_bias,
    gate_up_weight,
    down_weight,
    cotangent,
):
    row_count, local_len, features = inputs.shape
    fsdp_count = lax.axis_size("fsdp")
    fsdp_rank = lax.axis_index("fsdp")
    block_rank = lax.axis_index("seq") * fsdp_count + fsdp_rank
    token_count = row_count * local_len
    head_count = features // HD
    ff_width = gate_up_weight.shape[1] // 2
    scale_factor = HD ** (-0.5)
    flat = inputs.reshape(token_count, features).astype(jnp.float32)
    local_pos = block_rank * local_len + jnp.arange(local_len, dtype=jnp.int32)
    positions = jnp.tile(local_pos, row_count)
    weight_set = (qkv_weight, out_weight, gate_up_weight, down_weight)

    def forward_product(left, slot_index):
        return fold_rows(left, weight_set[slot_index])

    def backward_product(grad_rows, slot_index):
        return map_back(grad_rows, weight_set[slot_index])

    normed_in, norm1_back = jax.vjp(layer_norm, flat, norm1_gain, norm1_bias)
    in_low = normed_in.astype(jnp.bfloat16)
    mixed = forward_product(in_low, 0) + qkv_bias
    turn_input = mixed[:, : 2 * features].reshape(token_count, 2 * head_count, HD)
    turned, turn_back = jax.vjp(lambda values: rotate(values, positions), turn_input)
    turned_low = turned.astype(jnp.bfloat16)
    queries = turned_low[:, :head_count].reshape(row_count, local_len, features)
    keys_loc = turned_low[:, head_count:].reshape(row_count, local_len, features)
    values_loc = (
        mixed[:, 2 * features :].astype(jnp.bfloat16).reshape(row_count, local_len, features)
    )
    head_query, head_key, head_value = (
        lax.all_to_all(queries, "seq", split_axis=2, concat_axis=1, tiled=True),
        lax.all_to_all(keys_loc, "seq", split_axis=2, concat_axis=1, tiled=True),
        lax.all_to_all(values_loc, "seq", split_axis=2, concat_axis=1, tiled=True),
    )
    all_keys, all_values = (
        lax.all_gather(head_key, "fsdp", axis=1, tiled=True),
        lax.all_gather(head_value, "fsdp", axis=1, tiled=True),
    )
    query_len = head_query.shape[1]
    key_len = all_keys.shape[1]
    head_width = head_query.shape[2]
    local_heads = head_width // HD
    query_four = head_query.reshape(row_count, query_len, local_heads, HD)
    keys_four = all_keys.reshape(row_count, key_len, local_heads, HD)
    values_four = all_values.reshape(row_count, key_len, local_heads, HD)
    query_index = jnp.arange(query_len, dtype=jnp.int32)
    query_pos = (
        query_index // local_len * fsdp_count + fsdp_rank
    ) * local_len + query_index % local_len
    key_index = jnp.arange(key_len, dtype=jnp.int32)
    key_pos = (
        key_index % query_len // local_len * fsdp_count + key_index // query_len
    ) * local_len + key_index % local_len
    query_seg = jnp.take(segments, query_pos, axis=1)
    key_seg = jnp.take(segments, key_pos, axis=1)
    span = min(512, key_len)
    block_count = key_len // span

    def block_inputs(block_index):
        first_row = block_index * span
        block_keys = lax.dynamic_slice_in_dim(keys_four, first_row, span, 1)
        block_values = lax.dynamic_slice_in_dim(values_four, first_row, span, 1)
        block_pos = lax.dynamic_slice_in_dim(key_pos, first_row, span, 0)
        block_seg = lax.dynamic_slice_in_dim(key_seg, first_row, span, 1)
        allowed = (query_seg[:, :, None] == block_seg[:, None, :]) & (
            block_pos[None, None, :] <= query_pos[None, :, None]
        )
        scores = (
            jnp.einsum(
                "rqhd,rkhd->rhqk", query_four, block_keys, preferred_element_type=jnp.float32
            )
            * scale_factor
        )
        return (first_row, block_keys, block_values, allowed[:, None], scores)

    def forward_block(carry, block_index):
        row_top, running, weighted = carry
        first_row, block_keys, block_values, allowed, scores = block_inputs(block_index)
        new_top = jnp.maximum(row_top, jnp.max(jnp.where(allowed, scores, MASKED), axis=-1))
        probs = jnp.where(allowed, jnp.exp(scores - new_top[..., None]), 0.0)
        factor = jnp.exp(row_top - new_top)
        running = running * factor + jnp.sum(probs, axis=-1)
        weighted = weighted * factor[..., None] + jnp.einsum(
            "rhqk,rkhd->rhqd",
            probs.astype(jnp.bfloat16),
            block_values,
            preferred_element_type=jnp.float32,
        )
        return ((new_top, running, weighted), None)

    start_top = jnp.full((row_count, local_heads, query_len), MASKED, jnp.float32)
    start_total = jnp.zeros((row_count, local_heads, query_len), jnp.float32)
    start_weighted = jnp.zeros((row_count, local_heads, query_len, HD), jnp.float32)
    (row_top, running, weighted), _ = lax.scan(
        forward_block, (start_top, start_total, start_weighted), jnp.arange(block_count)
    )
    log_total = row_top + jnp.log(running)
    attended_heads = (
        (weighted / running[..., None])
        .transpose(0, 2, 1, 3)
        .reshape(row_count, query_len, head_width)
        .astype(jnp.bfloat16)
    )
    attended_loc = lax.all_to_all(attended_heads, "seq", split_axis=1, concat_axis=2, tiled=True)
    att_flat = attended_loc.reshape(token_count, features)
    middle = flat + forward_product(att_flat, 1)
    normed_mid, norm2_back = jax.vjp(layer_norm, middle, norm2_gain, norm2_bias)
    mid_low = normed_mid.astype(jnp.bfloat16)
    gate_up = forward_product(mid_low, 2)
    act_value, silu_back = jax.vjp(
        lambda gate_part, up_part: jax.nn.silu(gate_part) * up_part,
        gate_up[:, :ff_width],
        gate_up[:, ff_width:],
    )
    act_low = act_value.astype(jnp.bfloat16)
    result = middle + forward_product(act_low, 3)
    d_out = cotangent.reshape(token_count, features)
    d_act = backward_product(d_out, 3)
    d_gate, d_up = silu_back(d_act)
    d_gate_up = jnp.concatenate([d_gate, d_up], axis=1).astype(jnp.bfloat16)
    d_mid_norm = backward_product(d_gate_up, 2)
    d_middle_part, d_gain_two, d_bias_two = norm2_back(d_mid_norm)
    d_middle = d_out.astype(jnp.float32) + d_middle_part
    d_branch = d_middle.astype(jnp.bfloat16)
    d_attended = (
        backward_product(d_branch, 1).astype(jnp.bfloat16).reshape(row_count, local_len, features)
    )
    d_heads = lax.all_to_all(d_attended, "seq", split_axis=2, concat_axis=1, tiled=True)
    d_heads_four = d_heads.reshape(row_count, query_len, local_heads, HD)
    attended_four = attended_heads.reshape(row_count, query_len, local_heads, HD)
    delta = jnp.einsum(
        "rqhd,rqhd->rhq", d_heads_four.astype(jnp.float32), attended_four.astype(jnp.float32)
    )

    def backward_block(carry, block_index):
        d_query, d_keys_all, d_values_all = carry
        first_row, block_keys, block_values, allowed, scores = block_inputs(block_index)
        probs = jnp.where(allowed, jnp.exp(scores - log_total[..., None]), 0.0)
        d_block_values = jnp.einsum(
            "rhqk,rqhd->rkhd",
            probs.astype(jnp.bfloat16),
            d_heads_four,
            preferred_element_type=jnp.float32,
        )
        d_probs = jnp.einsum(
            "rqhd,rkhd->rhqk", d_heads_four, block_values, preferred_element_type=jnp.float32
        )
        d_scores = (probs * (d_probs - delta[..., None])).astype(jnp.bfloat16)
        d_query = (
            d_query
            + jnp.einsum(
                "rhqk,rkhd->rqhd", d_scores, block_keys, preferred_element_type=jnp.float32
            )
            * scale_factor
        )
        d_block_keys = (
            jnp.einsum("rhqk,rqhd->rkhd", d_scores, query_four, preferred_element_type=jnp.float32)
            * scale_factor
        )
        d_keys_all = lax.dynamic_update_slice_in_dim(d_keys_all, d_block_keys, first_row, 1)
        d_values_all = lax.dynamic_update_slice_in_dim(d_values_all, d_block_values, first_row, 1)
        return ((d_query, d_keys_all, d_values_all), None)

    zero_query = jnp.zeros((row_count, query_len, local_heads, HD), jnp.float32)
    zero_keys = jnp.zeros((row_count, key_len, local_heads, HD), jnp.float32)
    (d_query, d_keys_all, d_values_all), _ = lax.scan(
        backward_block, (zero_query, zero_keys, zero_keys), jnp.arange(block_count)
    )
    d_keys_sum, d_values_sum = (
        lax.psum_scatter(
            d_keys_all.reshape(row_count, key_len, head_width).astype(jnp.bfloat16),
            "fsdp",
            scatter_dimension=1,
            tiled=True,
        ).astype(jnp.float32),
        lax.psum_scatter(
            d_values_all.reshape(row_count, key_len, head_width).astype(jnp.bfloat16),
            "fsdp",
            scatter_dimension=1,
            tiled=True,
        ).astype(jnp.float32),
    )
    d_query_low = d_query.reshape(row_count, query_len, head_width).astype(jnp.bfloat16)
    dq_back, dk_back, dv_back = (
        lax.all_to_all(d_query_low, "seq", split_axis=1, concat_axis=2, tiled=True),
        lax.all_to_all(
            d_keys_sum.astype(jnp.bfloat16), "seq", split_axis=1, concat_axis=2, tiled=True
        ),
        lax.all_to_all(
            d_values_sum.astype(jnp.bfloat16), "seq", split_axis=1, concat_axis=2, tiled=True
        ),
    )
    d_turned = jnp.concatenate(
        [
            dq_back.reshape(token_count, head_count, HD),
            dk_back.reshape(token_count, head_count, HD),
        ],
        axis=1,
    ).astype(jnp.float32)
    (d_turn_input,) = turn_back(d_turned)
    d_mixed = jnp.concatenate(
        [
            d_turn_input.reshape(token_count, 2 * features),
            dv_back.reshape(token_count, features).astype(jnp.float32),
        ],
        axis=1,
    ).astype(jnp.bfloat16)
    d_qkv_bias = jnp.sum(d_mixed.astype(jnp.float32), axis=0)
    d_norm_in = backward_product(d_mixed, 0)
    d_flat_part, d_gain_one, d_bias_one = norm1_back(d_norm_in)
    d_inputs = d_middle + d_flat_part
    first_grad = grad_joint(in_low, d_mixed)
    second_grad = grad_joint(att_flat, d_branch)
    third_grad = grad_joint(mid_low, d_gate_up)
    fourth_grad = grad_joint(act_low, d_out)
    qkv_grad, out_grad, gate_up_grad, down_grad = (
        lax.all_gather(first_grad.astype(jnp.bfloat16), "seq", axis=0, tiled=True).astype(
            first_grad.dtype
        ),
        lax.all_gather(second_grad.astype(jnp.bfloat16), "seq", axis=0, tiled=True).astype(
            second_grad.dtype
        ),
        lax.all_gather(third_grad.astype(jnp.bfloat16), "seq", axis=0, tiled=True).astype(
            third_grad.dtype
        ),
        lax.all_gather(fourth_grad.astype(jnp.bfloat16), "seq", axis=0, tiled=True).astype(
            fourth_grad.dtype
        ),
    )
    gain_one, bias_one, bias_qkv, gain_two, bias_two = lax.psum(
        (d_gain_one, d_bias_one, d_qkv_bias, d_gain_two, d_bias_two), ("seq", "fsdp")
    )
    return (
        result.reshape(row_count, local_len, features),
        d_inputs.reshape(row_count, local_len, features),
        gain_one,
        bias_one,
        qkv_grad,
        bias_qkv,
        out_grad,
        gain_two,
        bias_two,
        gate_up_grad,
        down_grad,
    )


BLOCK = 512
BF = jnp.bfloat16
F32 = jnp.float32
SMALL = pl.CostEstimate(flops=1000, bytes_accessed=1000, transcendentals=0)


def swap(value, mask):
    return lax.ppermute(value, ("z", "core", "fsdp"), [(i, i ^ mask) for i in range(32)])


def shift(value, steps):
    return lax.ppermute(value, ("z", "core", "fsdp"), [(i, (i + 8 * steps) % 32) for i in range(32)])


def pick(stacked, index):
    return lax.dynamic_index_in_dim(stacked, index, 0, keepdims=False)


def exchange(value, axis="fsdp"):
    return lax.all_to_all(value, axis, split_axis=0, concat_axis=0, tiled=True)


def gather_near(value):
    half = value.shape[0] // 2
    by_x = swap(value, 1)
    by_y = swap(value, 2)
    return [value, by_x, by_y, swap(by_x[:half], 2), swap(by_y[half:], 1)]


def both_cores(near):
    return near + [swap(piece, 4) for piece in near]


def gather_pieces(value):
    return both_cores(gather_near(value))


def sum_quad(terms):
    return terms[0].astype(F32) + sum(swap(terms[m].astype(BF), m).astype(F32) for m in (1, 2, 3))


def sum_plane(near, far):
    arrived = swap(far.astype(BF), 4)
    return sum_quad([near[m].astype(F32) + arrived[m].astype(F32) for m in range(4)])


def dot(left, right):
    return jnp.dot(left, right, preferred_element_type=F32)


def dot_rows(left, right):
    return lax.dot_general(left, right, (((1,), (1,)), ((), ())), preferred_element_type=F32)


def dot_cols(left, right):
    return lax.dot_general(left, right, (((0,), (0,)), ((), ())), preferred_element_type=F32)


def turn_tables(row_len):
    half_rot = ROT // 2
    lane = jnp.arange(2 * HD, dtype=jnp.int32) % HD
    exponent = (lane % half_rot).astype(F32) * (2.0 / ROT)
    inverse = jnp.power(jnp.float32(10000.0), -exponent)
    angles = jnp.arange(row_len, dtype=jnp.int32).astype(F32)[:, None] * inverse[None, :]
    cosine = jnp.where(lane < ROT, jnp.cos(angles), 1.0)
    sine = jnp.sin(angles)
    ahead = jnp.where(lane < half_rot, -sine, 0.0)
    behind = jnp.where((lane >= half_rot) & (lane < ROT), sine, 0.0)
    return cosine, ahead, behind


def attend_kernel(
    split_ref, where_ref, mixed_ref, cos_ref, ahead_ref, behind_ref,
    q_ref, k_ref, v_ref, o_ref, log_ref, mine_ref, theirs_ref, kz, vz,
):
    local_len = mixed_ref.shape[2]
    row_len = q_ref.shape[0]
    low = lax.broadcasted_iota(jnp.int32, (local_len, 2 * HD), 1) < HD

    def prepare(i, carry):
        rows = pl.ds(pl.multiple_of(i * local_len, local_len), local_len)
        cosine, ahead, behind = cos_ref[rows], ahead_ref[rows], behind_ref[rows]

        def turn(x):
            return (
                x * cosine
                + pltpu.roll(x, 2 * HD - ROT // 2, 1) * ahead
                + pltpu.roll(x, ROT // 2, 1) * behind
            )

        first = mixed_ref[i, 0]
        second = mixed_ref[i, 1]
        turned0 = turn(first[:, : 2 * HD])
        turned1 = turn(second[:, : 2 * HD])
        q = jnp.where(low, turned0, pltpu.roll(turned1, HD, 1))
        k = jnp.where(low, pltpu.roll(turned0, HD, 1), turned1)
        v = jnp.where(low, first[:, 2 * HD :], second[:, 2 * HD :])
        q_ref[rows] = (q * HD**-0.5).astype(BF)
        k_ref[rows] = k.astype(BF)
        v_ref[rows] = v.astype(BF)
        kz[0, rows] = jnp.where(low, k, 0.0).astype(BF)
        kz[1, rows] = jnp.where(low, 0.0, k).astype(BF)
        vz[0, rows] = jnp.where(low, v, 0.0).astype(BF)
        vz[1, rows] = jnp.where(low, 0.0, v).astype(BF)
        return carry

    lax.fori_loop(0, row_len // local_len, prepare, 0)
    t_in = lax.broadcasted_iota(jnp.int32, (BLOCK, 1), 0)
    u_in = lax.broadcasted_iota(jnp.int32, (1, BLOCK), 1)
    low_q = lax.broadcasted_iota(jnp.int32, (BLOCK, 2 * HD), 1) < HD

    def query_block(qb, carry):
        rows = pl.ds(pl.multiple_of(qb * BLOCK, BLOCK), BLOCK)
        q = q_ref[rows]
        t = t_in + qb * BLOCK
        outs, logs = [], []
        for row in range(2):
            split = split_ref[row]
            start = jnp.where(t >= split, split, 0)

            def step(kb, state, diagonal, row=row, start=start):
                top, total, acc = state
                keys = pl.ds(pl.multiple_of(kb * BLOCK, BLOCK), BLOCK)
                u = u_in + kb * BLOCK
                scores = dot_rows(q, kz[row, keys])
                allowed = u >= start
                if diagonal:
                    allowed = allowed & (u <= t)
                scores = jnp.where(allowed, scores, MASKED)
                new_top = jnp.maximum(top, jnp.max(scores, axis=1, keepdims=True))
                probs = jnp.exp(scores - new_top)
                factor = jnp.exp(top - new_top)
                total = total * factor + jnp.sum(probs, axis=1, keepdims=True)
                acc = acc * factor + dot(probs.astype(BF), vz[row, keys])
                return new_top, total, acc

            state = (
                jnp.full((BLOCK, 1), MASKED, F32),
                jnp.zeros((BLOCK, 1), F32),
                jnp.zeros((BLOCK, 2 * HD), F32),
            )
            first_kb = jnp.where(qb * BLOCK >= split, split // BLOCK, 0)
            state = lax.fori_loop(
                first_kb, qb, lambda kb, state, step=step: step(kb, state, False), state
            )
            top, total, acc = step(qb, state, True)
            outs.append(acc / total)
            logs.append(top + jnp.log(total))
        o_ref[rows] = (outs[0] + outs[1]).astype(BF)
        turned = jnp.where(low_q, logs[0], logs[1]).T
        log_ref[0:1, rows] = turned[0:1]
        log_ref[1:2, rows] = turned[HD : HD + 1]
        step = lax.rem(qb - where_ref[0] + 4, 4)
        core = where_ref[1] // 4
        half = BLOCK // 2
        for ref, which in ((mine_ref, core), (theirs_ref, 1 - core)):
            ref[step] = o_ref[pl.ds(pl.multiple_of(qb * BLOCK + which * half, half), half)]
        return carry

    lax.fori_loop(0, row_len // BLOCK, query_block, 0)


def attend(split, where, mixed, tables):
    row_len = tables[0].shape[0]
    packed = jax.ShapeDtypeStruct((row_len, 2 * HD), BF)
    smem = pl.BlockSpec(memory_space=pltpu.SMEM)
    vmem = pl.BlockSpec(memory_space=pltpu.VMEM)
    pairs = 2 * row_len * row_len // 2
    return pl.pallas_call(
        attend_kernel,
        out_shape=(packed, packed, packed, packed, jax.ShapeDtypeStruct((2, row_len), F32))
        + (jax.ShapeDtypeStruct((4, row_len // 8, 2 * HD), BF),) * 2,
        in_specs=[smem, smem, vmem, vmem, vmem, vmem],
        out_specs=(vmem,) * 7,
        scratch_shapes=[pltpu.VMEM((2, row_len, 2 * HD), BF), pltpu.VMEM((2, row_len, 2 * HD), BF)],
        compiler_params=pltpu.CompilerParams(vmem_limit_bytes=56 * 2**20),
        cost_estimate=SMALL,
        name="attend",
    )(split, where, mixed, *tables)


def attend_back_kernel(
    split_ref, q_hbm, k_hbm, v_hbm, o_hbm, do_hbm, log_ref,
    cos_ref, ahead_ref, behind_ref,
    dmix_ref, dpos_ref, kz, vz, qz, dz, ktz, delta, dq_t, dk, dv,
    q_ref, k_ref, v_ref, o_ref, do_ref, sem,
):
    loads = [
        pltpu.make_async_copy(source, target, sem.at[n])
        for n, (source, target) in enumerate(
            ((k_hbm, k_ref), (v_hbm, v_ref), (q_hbm, q_ref), (do_hbm, do_ref), (o_hbm, o_ref))
        )
    ]
    for copy in loads:
        copy.start()
    for copy in loads:
        copy.wait()
    row_len = q_ref.shape[0]
    local_len = dmix_ref.shape[2]
    low = lax.broadcasted_iota(jnp.int32, (BLOCK, 2 * HD), 1) < HD
    low_t = lax.broadcasted_iota(jnp.int32, (2 * HD, BLOCK), 0) < HD
    lane = lax.broadcasted_iota(jnp.int32, (8, 2 * HD), 1)
    ones = [jnp.where(lane < HD, 1.0, 0.0).astype(BF), jnp.where(lane < HD, 0.0, 1.0).astype(BF)]

    def prepare(b, carry):
        rows = pl.ds(pl.multiple_of(b * BLOCK, BLOCK), BLOCK)
        zero = jnp.zeros((BLOCK, 2 * HD), F32)
        for ref, out in ((k_ref, kz), (v_ref, vz), (q_ref, qz), (do_ref, dz)):
            value = ref[rows].astype(F32)
            out[0, rows] = jnp.where(low, value, zero).astype(BF)
            out[1, rows] = jnp.where(low, zero, value).astype(BF)
        value = k_ref[rows].astype(F32).T
        ktz[0, :, rows] = jnp.where(low_t, value, 0.0).astype(BF)
        ktz[1, :, rows] = jnp.where(low_t, 0.0, value).astype(BF)
        product = do_ref[rows].astype(F32) * o_ref[rows].astype(F32)
        coarse = product.astype(BF)
        fine = (product - coarse.astype(F32)).astype(BF)
        for row in range(2):
            delta[row, :, rows] = dot_rows(ones[row], coarse) + dot_rows(ones[row], fine)
        dq_t[:, rows] = jnp.zeros((2 * HD, BLOCK), F32)
        return carry

    lax.fori_loop(0, row_len // BLOCK, prepare, 0)
    u_in = lax.broadcasted_iota(jnp.int32, (BLOCK, 1), 0)
    t_in = lax.broadcasted_iota(jnp.int32, (1, BLOCK), 1)

    def key_block(kb, carry):
        keys = pl.ds(pl.multiple_of(kb * BLOCK, BLOCK), BLOCK)
        u = u_in + kb * BLOCK
        sums_k, sums_v = [], []
        for row in range(2):
            split = split_ref[row]
            k_row = kz[row, keys]
            v_row = vz[row, keys]
            kt_row = ktz[row, :, keys]

            def step(qb, state, row=row, split=split, k_row=k_row, v_row=v_row, kt_row=kt_row):
                d_keys, d_values = state
                rows = pl.ds(pl.multiple_of(qb * BLOCK, BLOCK), BLOCK)
                t = t_in + qb * BLOCK
                start = jnp.where(t >= split, split, 0)
                allowed = (u >= start) & (u <= t)
                scores = dot_rows(k_row, q_ref[rows])
                probs = jnp.where(allowed, jnp.exp(scores - log_ref[pl.ds(row, 1), rows]), 0.0)
                d_probs = dot_rows(v_row, do_ref[rows])
                d_scores = (probs * (d_probs - delta[row, pl.ds(0, 1), rows])).astype(BF)
                d_values = d_values + dot(probs.astype(BF), dz[row, rows])
                d_keys = d_keys + dot(d_scores, qz[row, rows])
                dq_t[:, rows] += dot(kt_row, d_scores)
                return d_keys, d_values

            zero = jnp.zeros((BLOCK, 2 * HD), F32)
            last = jnp.where(
                (kb + 1) * BLOCK <= split, (split + BLOCK - 1) // BLOCK, row_len // BLOCK
            )
            d_keys, d_values = lax.fori_loop(kb, last, step, (zero, zero))
            sums_k.append(d_keys)
            sums_v.append(d_values)
        dk[keys] = sums_k[0] + sums_k[1]
        dv[keys] = sums_v[0] + sums_v[1]
        return carry

    lax.fori_loop(0, row_len // BLOCK, key_block, 0)
    low_l = lax.broadcasted_iota(jnp.int32, (local_len, 2 * HD), 1) < HD
    per = 2 * HD // local_len


    def finish(b, carry):
        start = pl.multiple_of(b * 2 * HD, 2 * HD)
        dq = dq_t[:, pl.ds(start, 2 * HD)].T * HD**-0.5
        for part in range(per):
            i = b * per + part
            rows = pl.ds(pl.multiple_of(i * local_len, local_len), local_len)
            cosine, ahead, behind = cos_ref[rows], ahead_ref[rows], behind_ref[rows]

            def turn(x, cosine=cosine, ahead=ahead, behind=behind):
                return (
                    x * cosine
                    - pltpu.roll(x, 2 * HD - ROT // 2, 1) * ahead
                    - pltpu.roll(x, ROT // 2, 1) * behind
                )

            q_part = turn(dq[part * local_len : (part + 1) * local_len])
            k_part = turn(dk[rows])
            v_part = dv[rows]
            first = jnp.where(low_l, q_part, pltpu.roll(k_part, HD, 1)).astype(BF)
            second = jnp.where(low_l, pltpu.roll(q_part, HD, 1), k_part).astype(BF)
            dpos_ref[rows, : 2 * HD] = first
            dpos_ref[rows, 2 * HD : 4 * HD] = second
            dpos_ref[rows, 4 * HD :] = v_part.astype(BF)
            dmix_ref[i, 0, :, : 2 * HD] = first
            dmix_ref[i, 1, :, : 2 * HD] = second
            dmix_ref[i, 0, :, 2 * HD :] = jnp.where(low_l, v_part, 0.0).astype(BF)
            dmix_ref[i, 1, :, 2 * HD :] = jnp.where(low_l, pltpu.roll(v_part, HD, 1), 0.0).astype(BF)
        return carry

    lax.fori_loop(0, row_len // (2 * HD), finish, 0)


def attend_back(split, q, k, v, out, d_out, logs, tables, local_len):
    row_len = q.shape[0]
    smem = pl.BlockSpec(memory_space=pltpu.SMEM)
    vmem = pl.BlockSpec(memory_space=pltpu.VMEM)
    masked = pltpu.VMEM((2, row_len, 2 * HD), BF)
    whole = pltpu.VMEM((row_len, 2 * HD), F32)
    pairs = 2 * row_len * row_len // 2
    return pl.pallas_call(
        attend_back_kernel,
        out_shape=(
            jax.ShapeDtypeStruct((row_len // local_len, 2, local_len, 4 * HD), BF),
        )
        + (jax.ShapeDtypeStruct((row_len, 6 * HD), BF),),
        in_specs=[smem] + [pl.BlockSpec(memory_space=pltpu.HBM)] * 5 + [vmem] * 4,
        out_specs=(vmem,) * 2,
        scratch_shapes=[
            masked, masked, masked, masked,
            pltpu.VMEM((2, 2 * HD, row_len), BF),
            pltpu.VMEM((2, 8, row_len), F32),
            pltpu.VMEM((2 * HD, row_len), F32),
            whole, whole,
        ]
        + [pltpu.VMEM((row_len, 2 * HD), BF)] * 5
        + [pltpu.SemaphoreType.DMA((5,))],
        compiler_params=pltpu.CompilerParams(vmem_limit_bytes=56 * 2**20),
        cost_estimate=SMALL,
        name="attend_back",
    )(split, q, k, v, out, d_out, logs, *tables)


def pick_heads_kernel(where_ref, q_ref, k_ref, v_ref, out_ref):
    wide = 2 * HD
    low = lax.broadcasted_iota(jnp.int32, (q_ref.shape[0], wide), 1) < HD
    for core in (0, 1):

        @pl.when(where_ref[1] // 4 == core)
        def _(core=core):
            def join(left, right):
                if core == 0:
                    return jnp.where(low, left, pltpu.roll(right, HD, 1)).astype(BF)
                return jnp.where(low, pltpu.roll(left, HD, 1), right).astype(BF)

            for z in range(4):
                cols = slice(z * wide, (z + 1) * wide)
                out_ref[:, cols] = join(q_ref[:, cols].astype(F32), k_ref[:, cols].astype(F32))
            for pair in range(2):
                left, right = (
                    v_ref[:, (2 * pair + n) * wide : (2 * pair + n + 1) * wide].astype(F32) for n in (0, 1)
                )
                out_ref[:, (4 + pair) * wide : (5 + pair) * wide] = join(left, right)


def pick_heads(where, weight):
    rows, columns = weight.shape
    wide = columns // 12
    blocks = [
        pl.BlockSpec((rows, wide), lambda chip, where, part=part: (0, part * 4 + chip)) for part in range(3)
    ]
    return pl.pallas_call(
        pick_heads_kernel,
        grid_spec=pltpu.PrefetchScalarGridSpec(
            num_scalar_prefetch=1,
            grid=(4,),
            in_specs=blocks,
            out_specs=pl.BlockSpec((None, rows, 12 * HD), lambda chip, where: (chip, 0, 0)),
        ),
        out_shape=jax.ShapeDtypeStruct((4, rows, 12 * HD), BF),
        compiler_params=pltpu.CompilerParams(vmem_limit_bytes=56 * 2**20),
        cost_estimate=SMALL,
        name="pick_heads",
    )(where, weight, weight, weight)


def small_call(kernel, name, out_shape, where, *arrays, flops=0, scratch=(), limit=56):
    size = sum(x.size * x.dtype.itemsize for x in arrays)
    vmem = pl.BlockSpec(memory_space=pltpu.VMEM)
    return pl.pallas_call(
        kernel,
        out_shape=out_shape,
        in_specs=[pl.BlockSpec(memory_space=pltpu.SMEM)] + [vmem] * len(arrays),
        out_specs=[vmem] * len(out_shape),
        scratch_shapes=scratch,
        compiler_params=pltpu.CompilerParams(vmem_limit_bytes=limit * 2**20),
        cost_estimate=SMALL,
        name=name,
    )(where, *arrays)


def pair_kernel(where_ref, mine_ref, theirs_ref, *outs):
    low = lax.broadcasted_iota(jnp.int32, mine_ref.shape[1:], 1) < HD
    for step, out in enumerate(outs):
        for core, (ref0, ref1) in enumerate(((mine_ref, theirs_ref), (theirs_ref, mine_ref))):

            @pl.when(where_ref[1] // 4 == core)
            def _(ref0=ref0, ref1=ref1):
                even, uneven = ref0[step].astype(F32), ref1[step].astype(F32)
                out[:, : 2 * HD] = jnp.where(low, even, pltpu.roll(uneven, HD, 1)).astype(BF)
                out[:, 2 * HD :] = jnp.where(low, pltpu.roll(even, HD, 1), uneven).astype(BF)


def out_project_kernel(where_ref, a0, a1, a2, a3, weight_ref, att_ref, o0, o1, o2, o3, sum_v):
    plane, rank = where_ref[0], where_ref[1] % 4
    span = a0.shape[0]
    for step, ref in enumerate((a0, a1, a2, a3)):
        lanes = pl.ds(pl.multiple_of(lax.rem(plane - step + 4, 4) * 2 * HD, 2 * HD), 2 * HD)
        for row in range(2):
            att_ref[row * span : (row + 1) * span, lanes] = ref[:, row * 2 * HD : (row + 1) * 2 * HD]
    sum_v[...] = dot(att_ref[...], weight_ref[...])
    part = span // 4
    for m, out in enumerate((o0, o1, o2, o3)):
        for row in range(2):
            rows = pl.ds(pl.multiple_of(row * span + (rank ^ m) * part, part), part)
            out[row * part : (row + 1) * part] = sum_v[rows].astype(out.dtype)


def d_att_kernel(where_ref, p0, p1, p2, p3_low, p3_high, weight_ref, branch_ref, heads_ref):
    rank = where_ref[1] % 4
    span = heads_ref.shape[1]
    part = span // 4
    for m, pieces in enumerate(((p0,), (p1,), (p2,), (p3_low, p3_high))):
        for row in range(2):
            rows = pl.ds(pl.multiple_of(row * span + (rank ^ m) * part, part), part)
            if len(pieces) == 2:
                branch_ref[rows] = pieces[row][...]
            else:
                branch_ref[rows] = pieces[0][row * part : (row + 1) * part]
    d_att = dot_rows(branch_ref[...], weight_ref[...])
    low = lax.broadcasted_iota(jnp.int32, heads_ref.shape[1:], 1) < HD
    for z in range(4):
        lanes = slice(z * 2 * HD, (z + 1) * 2 * HD)
        row0, row1 = d_att[:span, lanes], d_att[span:, lanes]
        heads_ref[2 * z] = jnp.where(low, row0, pltpu.roll(row1, HD, 1)).astype(BF)
        heads_ref[2 * z + 1] = jnp.where(low, pltpu.roll(row0, HD, 1), row1).astype(BF)


def d_in_kernel(where_ref, in_ref, weight_ref, near_ref, far_ref, x_v, d_v):
    core, rank = where_ref[1] // 4, where_ref[1] % 4
    reach, wide = in_ref.shape[1], 2 * HD
    features = weight_ref.shape[0]
    low = lax.broadcasted_iota(jnp.int32, (reach, wide), 1) < HD
    for z in range(4):
        for row in range(2):
            x_v[row * reach : (row + 1) * reach, z * wide : (z + 1) * wide] = in_ref[
                z, :, row * wide : (row + 1) * wide
            ]
    for pair in range(2):
        cols = slice((4 + pair) * wide, (5 + pair) * wide)
        one, two = (in_ref[2 * pair + n, :, 2 * wide :].astype(F32) for n in (0, 1))
        x_v[:reach, cols] = jnp.where(low, one, pltpu.roll(two, HD, 1)).astype(BF)
        x_v[reach:, cols] = jnp.where(low, pltpu.roll(one, HD, 1), two).astype(BF)
    part = reach // 8
    span = d_v.shape[1]

    def columns(n, carry):
        cols = pl.ds(pl.multiple_of(n * span, span), span)
        d_v[...] = dot_rows(x_v[...], weight_ref[cols])
        for ref, which in ((near_ref, core), (far_ref, 1 - core)):
            for m in range(4):
                for row in range(2):
                    first = row * reach + which * 4 * part + (rank ^ m) * part
                    rows = pl.ds(pl.multiple_of(first, part), part)
                    ref[m, row * part : (row + 1) * part, cols] = d_v[rows].astype(BF)
        return carry

    lax.fori_loop(0, features // span, columns, 0)


def hidden_kernel(where_ref, *refs, steps, own):
    n_mid, n_out = (10, 2) if own else (1, 4 * len(steps))
    mids, outs, refs = refs[:n_mid], refs[n_mid : n_mid + n_out], refs[n_mid + n_out :]
    gate_ref, up_ref, down_ref = refs[:3]
    refs = refs[3:] if own else refs[7:]
    alls, refs = refs[:4], refs[4:]
    d_mids, acts, refs = (refs[:2], refs[2:4], refs[4:]) if own else ((), (), refs)
    mid_v, out_v, gate_up_v, down_v, act_v, d_gate_v, d_up_v, sem_in, sem_w, sem_out = refs[:10]
    rows, features = mid_v.shape[1:]
    width, tile = down_v.shape[0], 256
    tiles = width // tile
    plane, mine = where_ref[0], where_ref[1]
    core = mine // 4
    shard = gate_ref.shape[1]
    step = rows // 4
    halves = 2 * len(steps)

    def blocks(h):
        base = lax.rem(plane + 4 - steps[h // 2], 4) * (2 * rows)
        return [
            pl.ds(pl.multiple_of(base + (mine ^ (4 * (h % 2) + m)) * step, step), step) for m in range(4)
        ]

    def loads(h):
        slot = h % 2
        if own:
            pieces, out_pieces = mids[5 * h : 5 * h + 5], outs[h : h + 1]
        else:
            pieces = [mids[0].at[block] for block in blocks(h)]
            out_pieces = outs[2 * h : 2 * h + 2]
        found = []
        for held, sources in ((mid_v, pieces), (out_v, out_pieces)):
            at = 0
            for source in sources:
                size = source.shape[0]
                found.append((source, held.at[slot, pl.ds(at, size)]))
                at += size
        return [pltpu.make_async_copy(x, y, sem_in.at[slot, n]) for n, (x, y) in enumerate(found)]

    def stores(h):
        slot = h % 2
        return [
            pltpu.make_async_copy(
                held.at[slot, pl.ds(m * step, step)], target.at[block], sem_out.at[slot, n, m]
            )
            for n, (held, target) in enumerate(zip((act_v, d_gate_v, d_up_v, out_v), alls))
            for m, block in enumerate(blocks(h))
        ]

    def tile_copies(j):
        cols = pl.ds(j * tile, tile)
        found = [
            (ref.at[m, :, cols], gate_up_v.at[g, pl.ds(m * shard, shard), cols])
            for g, ref in enumerate((gate_ref, up_ref))
            for m in range(4)
        ]
        first = pl.multiple_of(core * (down_ref.shape[0] - width) + j * tile, 128)
        found.append((down_ref.at[pl.ds(first, tile)], down_v.at[cols]))
        return [pltpu.make_async_copy(x, y, sem_w.at[j, n]) for n, (x, y) in enumerate(found)]

    def wait_tile(j):
        for copy in weight_copies[j]:
            copy.wait()
        if j == 0:

            @pl.when(core == 1)
            def _():
                gate_up_v[:, :, : 2 * width - down_ref.shape[0]] = jnp.zeros(
                    (2, features, 2 * width - down_ref.shape[0]), BF
                )

    def compute(slot, cols):
        gate = dot(mid_v[slot], gate_up_v[0, :, cols])
        up = dot(mid_v[slot], gate_up_v[1, :, cols])
        d_act = dot_rows(out_v[slot], down_v[cols])
        sig = 1.0 / (1.0 + jnp.exp(-gate))
        silu = gate * sig
        act_v[slot, :, cols] = (silu * up).astype(BF)
        d_gate_v[slot, :, cols] = (d_act * up * (sig + silu * (1.0 - sig))).astype(BF)
        d_up_v[slot, :, cols] = (d_act * silu).astype(BF)

    weight_copies = [tile_copies(j) for j in range(tiles)]
    for copies in [weight_copies[0], loads(0)] + weight_copies[1:] + [loads(1)]:
        for copy in copies:
            copy.start()
    for h in range(halves):
        slot = h % 2
        for copy in loads(h):
            copy.wait()
        if h == 0:
            for j in range(tiles):
                wait_tile(j)
                compute(0, pl.ds(j * tile, tile))
        else:
            compute(slot, pl.ds(0, tile))
            if h + 1 < halves:
                for copy in stores(h - 1):
                    copy.wait()
                for copy in loads(h + 1):
                    copy.start()

            def part(j, carry, slot=slot):
                compute(slot, pl.ds(pl.multiple_of(j * tile, tile), tile))
                return carry

            lax.fori_loop(1, tiles, part, 0)
        for copy in stores(h):
            copy.start()
    left = []
    if own:
        sum_v = refs[10]
        span = 512
        for i in (1, 0):
            for m in range(4):
                part = pl.ds(m * step, step)
                left.append(
                    pltpu.make_async_copy(act_v.at[i, part], acts[i].at[m], sem_out.at[i, 4, m])
                )
                left[-1].start()

            def term(n, carry, i=i):
                cols = pl.ds(pl.multiple_of(n * span, span), span)
                sum_v[i, :, cols] = (
                    dot_rows(d_gate_v[i], gate_up_v[0, cols]) + dot_rows(d_up_v[i], gate_up_v[1, cols])
                ).astype(BF)
                return carry

            lax.fori_loop(0, features // span, term, 0)
            for m in range(4):
                part = pl.ds(m * step, step)
                left.append(
                    pltpu.make_async_copy(sum_v.at[i, part], d_mids[i].at[m], sem_out.at[i, 5, m])
                )
                left[-1].start()
    for h in (halves - 2, halves - 1):
        left += stores(h)
    for copy in left:
        copy.wait()


def hidden_layer(where, mids, outs, weights, total, steps=(0,), before=None):
    own = before is None
    features = outs[0].shape[1]
    rows, width = total // 8, weights[0].shape[2]
    narrow = jax.ShapeDtypeStruct((total, width), BF)
    wide = jax.ShapeDtypeStruct((total, features), BF)
    term = jax.ShapeDtypeStruct((4, rows // 4, features), BF)
    act = jax.ShapeDtypeStruct((4, rows // 4, width), BF)
    held = pltpu.VMEM((2, rows, features), BF)
    small = pltpu.VMEM((2, rows, width), BF)
    dma = pltpu.SemaphoreType.DMA
    count = len(mids) + len(outs)
    kept = [] if own else list(before)
    hbm = pl.BlockSpec(memory_space=pltpu.HBM)
    found = pl.pallas_call(
        functools.partial(hidden_kernel, steps=steps, own=own),
        in_specs=[pl.BlockSpec(memory_space=pltpu.SMEM)] + [hbm] * (count + 3 + len(kept)),
        out_specs=[hbm] * (8 if own else 4),
        out_shape=[narrow, narrow, narrow, wide] + ([term, term, act, act] if own else []),
        input_output_aliases={count + 4 + n: n for n in range(len(kept))},
        scratch_shapes=[
            held, held,
            pltpu.VMEM((2, features, width), BF),
            pltpu.VMEM((width, features), BF),
            small, small, small,
            dma((2, 9)), dma((width // 256, 9)), dma((2, 6, 4)),
        ]
        + ([held] if own else []),
        compiler_params=pltpu.CompilerParams(vmem_limit_bytes=56 * 2**20),
        cost_estimate=SMALL,
        name="hidden",
    )(where, *mids, *outs, *weights, *kept)
    return list(found[:4]), list(found[4:])


def weight_grad_kernel(left_ref, right_ref, out_ref):
    out_ref[...] = dot_cols(left_ref[...], right_ref[...]).astype(BF)


def weight_grad(left, right):
    tokens, features = left.shape
    width = right.shape[1]
    step = 256
    return pl.pallas_call(
        weight_grad_kernel,
        grid=(features // step,),
        in_specs=[
            pl.BlockSpec((tokens, step), lambda i: (0, i)),
            pl.BlockSpec((tokens, width), lambda i: (0, 0), pipeline_mode=pl.Buffered(1)),
        ],
        out_specs=pl.BlockSpec((step, width), lambda i: (i, 0)),
        out_shape=jax.ShapeDtypeStruct((features, width), BF),
        compiler_params=pltpu.CompilerParams(vmem_limit_bytes=56 * 2**20),
        cost_estimate=SMALL,
        name="weight_grad",
    )(left, right)


def place_columns_kernel(where_ref, own_ref, other_ref, *rest):
    out_ref = rest[-1]
    wide = own_ref.shape[-1]
    extra = out_ref.shape[-1] - wide

    @pl.when(where_ref[0] == 0)
    def _():
        out_ref[:, :wide] = own_ref[...].astype(F32)
        out_ref[:, wide:] = other_ref[:, wide - extra :].astype(F32)

    @pl.when(where_ref[0] == 1)
    def _():
        out_ref[:, :wide] = other_ref[...].astype(F32)
        out_ref[:, wide:] = own_ref[:, wide - extra :].astype(F32)


def place_columns(core, own, other, before, chip_width, kind):
    chips, rows, wide = own.shape
    cut = rows // 2
    half = pl.BlockSpec((None, cut, wide), lambda chip, b, core: (chip, b, 0))
    return pl.pallas_call(
        place_columns_kernel,
        grid_spec=pltpu.PrefetchScalarGridSpec(
            num_scalar_prefetch=1,
            grid=(chips, rows // cut),
            in_specs=[half, half] + ([] if before is None else [pl.BlockSpec(memory_space=pl.ANY)]),
            out_specs=pl.BlockSpec((cut, chip_width), lambda chip, b, core: (b, kind * chips + chip)),
        ),
        out_shape=jax.ShapeDtypeStruct((rows, 2 * chips * chip_width), F32),
        input_output_aliases={} if before is None else {3: 0},
        compiler_params=pltpu.CompilerParams(vmem_limit_bytes=56 * 2**20),
        cost_estimate=SMALL,
        name="place_columns",
    )(core, own, other, *([] if before is None else [before]))


def place_down_kernel(core_ref, own_ref, other_ref, out_ref, *, lead):
    first = pl.program_id(0) < lead
    mine = first == (core_ref[0] == 0)

    @pl.when(mine)
    def _():
        out_ref[...] = own_ref[...].astype(F32)

    @pl.when(jnp.logical_not(mine))
    def _():
        out_ref[...] = other_ref[...].astype(F32)


def place_down(core, own, other, total):
    width, features = own.shape
    step = 128
    count, lead = total // step, width // step
    skip = 2 * lead - count

    def block(of_core):
        def index(i, core):
            which = core[0] if of_core else 1 - core[0]
            return (jnp.where(which == 0, jnp.minimum(i, lead - 1), jnp.maximum(i - lead + skip, 0)), 0)

        return pl.BlockSpec((step, features), index)

    return pl.pallas_call(
        functools.partial(place_down_kernel, lead=lead),
        grid_spec=pltpu.PrefetchScalarGridSpec(
            num_scalar_prefetch=1,
            grid=(count,),
            in_specs=[block(True), block(False)],
            out_specs=pl.BlockSpec((step, features), lambda i, core: (i, 0)),
        ),
        out_shape=jax.ShapeDtypeStruct((total, features), F32),
        cost_estimate=SMALL,
        name="place_down",
    )(core, own, other)


def place_qkv_kernel(where_ref, own_ref, other_ref, out_ref):
    cut = own_ref.shape[2]
    core = where_ref[0]
    for ref, half in ((own_ref, core), (other_ref, 1 - core)):
        rows = pl.ds(pl.multiple_of(half * cut, cut), cut)
        for z in range(4):
            out_ref[rows, z * 2 * HD : (z + 1) * 2 * HD] = ref[z, 0].astype(F32)


def place_qkv(where, own, other):
    _, _, cut, wide = own.shape
    parts = wide // (2 * HD)
    piece = pl.BlockSpec((4, 1, cut, 2 * HD), lambda part, chip, where: (0, chip ^ where[1], 0, part))
    return pl.pallas_call(
        place_qkv_kernel,
        grid_spec=pltpu.PrefetchScalarGridSpec(
            num_scalar_prefetch=1,
            grid=(parts, 4),
            in_specs=[piece, piece],
            out_specs=pl.BlockSpec((2 * cut, 8 * HD), lambda part, chip, where: (0, part * 4 + chip)),
        ),
        out_shape=jax.ShapeDtypeStruct((2 * cut, parts * 32 * HD), F32),
        cost_estimate=SMALL,
        name="place_qkv",
    )(where, own, other)


def tie(*values):
    return lax.optimization_barrier(values)


def plane_plan(
    inputs,
    segments,
    norm1_gain,
    norm1_bias,
    qkv_weight,
    qkv_bias,
    out_weight,
    norm2_gain,
    norm2_bias,
    gate_up_weight,
    down_weight,
    cotangent,
):
    row_count, local_len, features = inputs.shape
    row_len = segments.shape[1]
    tokens = row_count * local_len
    plane, core, rank = lax.axis_index("z"), lax.axis_index("core"), lax.axis_index("fsdp")
    seq = plane * 2 + core
    own = core * 4 + rank
    shard = features // 4
    hidden = gate_up_weight.shape[1] // 2
    chip_width = hidden // 4
    width = -(-chip_width // 256) * 128
    tables = turn_tables(row_len)
    split = jnp.sum((segments == 0).astype(jnp.int32), axis=1)
    where = jnp.stack([plane, own]).astype(jnp.int32)

    def head_columns(chip):
        parts = [
            lax.dynamic_slice_in_dim(qkv_weight, (chip * 8 + seq) * HD + part * features, HD, 1)
            for part in (0, 1, 2)
        ]
        return jnp.concatenate(parts + parts[2:], axis=1)

    head_weight = exchange(jnp.stack([head_columns(chip) for chip in range(4)])).reshape(features, 4 * HD)
    picked = pick_heads(where, qkv_weight)
    head_first = (rank * 8 + seq) * HD
    bias_parts = [
        lax.dynamic_slice_in_dim(qkv_bias, head_first + part * features, HD, 0) for part in (0, 1, 2)
    ]
    head_bias = jnp.concatenate(bias_parts + bias_parts[2:])
    hidden_first = core * (chip_width - width)

    def hidden_columns(kind):
        firsts = [hidden_first + chip * chip_width + kind * hidden for chip in range(4)]
        return jnp.stack([lax.dynamic_slice_in_dim(gate_up_weight, first, width, 1) for first in firsts])

    gate_weight, up_weight = hidden_columns(0), hidden_columns(1)

    flat = inputs.reshape(tokens, features).astype(F32)
    normed_in, norm1_back = jax.vjp(layer_norm, flat, norm1_gain, norm1_bias)
    everywhere = ("z", "core", "fsdp")
    in_all = lax.all_gather(normed_in.astype(BF), everywhere, axis=0, tiled=True)
    d_out = cotangent.reshape(tokens, features)
    out_near = jnp.concatenate(gather_near(d_out), axis=0)
    out_far = swap(out_near, 4)
    in_all, out_near, out_far, gate_weight, up_weight, head_weight, picked, *tables = tie(
        in_all, out_near, out_far, gate_weight, up_weight, head_weight, picked, *tables
    )
    lows, highs = [out_near[: 2 * tokens]], [out_near[2 * tokens :]]

    mixed = (dot(in_all, head_weight) + head_bias).reshape(
        row_len // local_len, row_count, local_len, 4 * HD
    )
    q, k, v, out_heads, logs, mine, theirs, gate_weight, low, up_weight = tie(
        *attend(split, where, mixed, tables), exchange(gate_weight), shift(lows[0], 1), up_weight
    )
    lows.append(low)
    span = row_len // 8
    pair = jax.ShapeDtypeStruct((span, 4 * HD), BF)
    pairs = small_call(pair_kernel, "pair", [pair] * 4, where, mine, swap(theirs, 4))
    arrived = [pairs[0]] + [shift(pairs[n], n) for n in (1, 2, 3)]
    square = row_count * span
    block = jax.ShapeDtypeStruct((tokens, features), BF)
    blocks = jax.ShapeDtypeStruct((4, tokens, features), BF)
    att, *branch = small_call(
        out_project_kernel,
        "out_project",
        [jax.ShapeDtypeStruct((square, shard), BF), jax.ShapeDtypeStruct((tokens, features), F32)]
        + [block] * 3,
        where,
        *arrived,
        out_weight,
        scratch=[pltpu.VMEM((square, features), F32)],
    )
    branch_sum, up_weight, high = tie(sum_quad(branch), exchange(up_weight), shift(highs[0], 1))
    highs.append(high)
    hidden_weights = [gate_weight, up_weight, down_weight]
    middle = flat + branch_sum
    normed_mid, norm2_back = jax.vjp(layer_norm, middle, norm2_gain, norm2_bias)
    mid_low = normed_mid.astype(BF)

    mid_pieces = gather_pieces(mid_low)
    *mid_pieces, mid_own, low = tie(*mid_pieces, mid_low, shift(lows[1], 1))
    lows.append(low)
    mid_all = lax.all_gather(mid_own, everywhere, axis=0, tiled=True)
    total = row_count * row_len
    hidden_all, (d_near, d_far, act_near, act_far) = hidden_layer(
        where, mid_pieces, [out_near, out_far], hidden_weights, total
    )
    d_near, d_far, high = tie(d_near, d_far, shift(highs[1], 1))
    highs.append(high)
    d_norm_mid, low = tie(sum_plane(d_near, d_far), shift(lows[2], 1))
    lows.append(low)
    d_middle_part, d_gain_two, d_bias_two = norm2_back(d_norm_mid)
    d_middle = d_out.astype(F32) + d_middle_part

    d_pieces = gather_near(d_middle.astype(BF))
    d_branch, d_heads = small_call(
        d_att_kernel,
        "d_att",
        [
            jax.ShapeDtypeStruct((square, features), BF),
            jax.ShapeDtypeStruct((8, span, 2 * HD), BF),
        ],
        where,
        *d_pieces,
        out_weight,
    )
    d_heads = exchange(d_heads, ("z", "core")).reshape(row_len, 2 * HD)
    d_heads, high_own = tie(d_heads, highs[2])
    d_packed, d_mixed, mid_all, high = tie(
        *attend_back(split, q, k, v, out_heads, d_heads, logs, tables, local_len)[::-1],
        mid_all,
        shift(high_own, 1),
    )
    highs.append(high)

    arrived = exchange(d_packed.reshape(4, row_len // 4, 6 * HD), "z")
    d_mixed = d_mixed.reshape(row_len * row_count, 4 * HD)
    head_grad = dot_cols(in_all, d_mixed)[:, : 3 * HD].astype(BF)
    cut = shard // 2
    head_grad = head_grad.reshape(4, 2, cut, 3 * HD)
    mine = lax.dynamic_index_in_dim(head_grad, core, 1, keepdims=False)
    theirs = swap(lax.dynamic_index_in_dim(head_grad, 1 - core, 1, keepdims=False), 4)
    first, second = jnp.where(core == 0, mine, theirs), jnp.where(core == 0, theirs, mine)
    pairs = jnp.concatenate(
        [half[:, :, p * HD : (p + 1) * HD] for p in range(3) for half in (first, second)], axis=2
    )
    down = lax.dynamic_slice_in_dim(down_weight, hidden_first, width, 0)
    result_sum = sum_plane(
        dot(act_near.reshape(4 * tokens, width), down).reshape(4, tokens, features),
        dot(act_far.reshape(4 * tokens, width), down).astype(BF).reshape(4, tokens, features),
    )

    def rest(steps, before):
        outs = [
            piece for n in steps for piece in (lows[n], highs[n], swap(lows[n], 4), swap(highs[n], 4))
        ]
        return hidden_layer(where, [mid_all], outs, hidden_weights, total, steps, before)[0]

    hidden_all = rest((1, 2), hidden_all)
    arrived, result_sum, pairs, att, d_branch, picked, *hidden_all = tie(
        arrived, result_sum, pairs, att, d_branch, picked, *hidden_all
    )
    result = middle + result_sum

    pairs = [pick(pairs, rank ^ m) for m in range(4)]
    pairs = [pairs[0]] + [swap(pairs[m], m) for m in (1, 2, 3)]
    head_all = exchange(picked).reshape(features, 12 * HD)
    out_part = dot_cols(att, d_branch).astype(BF)
    out_part = lax.psum_scatter(out_part, ("z", "core"), scatter_dimension=0, tiled=True)
    act_all, d_gate_all, d_up_all, out_all = rest((3,), hidden_all)
    head_all, d_gate_grad, d_up_all, act_all, arrived, out_part, *pairs = tie(
        head_all, weight_grad(mid_all, d_gate_all), d_up_all, act_all, arrived, out_part, *pairs
    )

    by_chip = (4, shard, width)
    near, far = small_call(
        d_in_kernel,
        "d_in",
        [blocks] * 2,
        where,
        arrived,
        head_all,
        scratch=[
            pltpu.VMEM((8 * tokens, 12 * HD), BF),
            pltpu.VMEM((8 * tokens, 512), F32),
        ],
        limit=56,
    )
    heads = lax.all_gather(jnp.stack(pairs), "z", axis=0)
    gate_parts, d_up_grad, near, far, act_all = tie(
        exchange(d_gate_grad.reshape(by_chip)),
        weight_grad(mid_all, d_up_all),
        near,
        swap(far, 4),
        act_all,
    )
    d_norm_in, down_own, d_up_grad = tie(
        sum_quad([near[m].astype(F32) + far[m].astype(F32) for m in range(4)]),
        weight_grad(act_all, out_all),
        d_up_grad,
    )

    core_index = core.reshape(1).astype(jnp.int32)
    up_parts = exchange(d_up_grad.reshape(by_chip))
    out_rows = lax.all_gather(out_part, ("z", "core"), axis=0, tiled=True)
    gate_up_grad = place_columns(core_index, gate_parts, swap(gate_parts, 4), None, chip_width, 0)
    down_grad = place_down(core_index, down_own, swap(down_own, 4), chip_width)
    d_flat_part, d_gain_one, d_bias_one = norm1_back(d_norm_in)
    d_inputs = d_middle + d_flat_part
    bias_sum = jnp.sum(d_mixed.astype(F32), axis=0)
    bias_own = jnp.zeros((3 * features,), F32)
    for part in range(3):
        bias_own = lax.dynamic_update_slice_in_dim(
            bias_own, bias_sum[part * HD : (part + 1) * HD], head_first + part * features, 0
        )
    sums = jnp.concatenate([d_gain_one, d_bias_one, bias_own, d_gain_two, d_bias_two])
    sums = sums + swap(sums, 4)
    sums = sums + sum(shift(sums, n) for n in (1, 2, 3))
    qkv_grad = place_qkv(jnp.stack([core, rank]).astype(jnp.int32), heads, swap(heads, 4))
    up_parts, sums, gate_up_grad, down_grad, qkv_grad = tie(
        up_parts, sums, gate_up_grad, down_grad, qkv_grad
    )
    sums = sums + sum(swap(sums, m) for m in (1, 2, 3))
    out_grad = out_rows.astype(F32)
    gate_up_grad = place_columns(
        core_index, up_parts, swap(up_parts, 4), gate_up_grad, chip_width, 1
    )
    return (
        result.reshape(row_count, local_len, features),
        d_inputs.reshape(row_count, local_len, features),
        sums[:features],
        sums[features : 2 * features],
        qkv_grad,
        sums[2 * features : 5 * features],
        out_grad,
        sums[5 * features : 6 * features],
        sums[6 * features :],
        gate_up_grad,
        down_grad,
    )


def solution(mesh):
    planes = (mesh.shape["seq"], mesh.shape["fsdp"]) == (8, 4)
    plan = plane_plan if planes else general_plan
    if planes:
        mesh = jax.sharding.Mesh(mesh.devices.reshape(4, 2, 4), ("z", "core", "fsdp"))
    spread = P(None, (*mesh.axis_names,), None)
    placed = (
        spread,
        P(),
        P(),
        P(),
        P("fsdp", None),
        P(),
        P("fsdp", None),
        P(),
        P(),
        P("fsdp", None),
        P("fsdp", None),
        spread,
    )
    return jax.shard_map(
        plan,
        mesh=mesh,
        in_specs=placed,
        out_specs=(
            spread,
            spread,
            P(),
            P(),
            P("fsdp", None),
            P(),
            P("fsdp", None),
            P(),
            P(),
            P("fsdp", None),
            P("fsdp", None),
        ),
        check_vma=False,
    )
```

```python
import functools

import jax
import jax.numpy as jnp
from jax import lax
from jax.experimental import pallas as pl
from jax.experimental.pallas import tpu as pltpu
from jax.sharding import PartitionSpec as P

HD = 64
ROT = 16


EPSILON = 1e-05
MASKED = -1e30


def layer_norm(values, norm_gain, offset):
    average = jnp.mean(values, axis=-1, keepdims=True)
    centred = values - average
    variance = jnp.mean(centred * centred, axis=-1, keepdims=True)
    return centred * lax.rsqrt(variance + EPSILON) * norm_gain + offset


def rotate(values, positions):
    half_rot = ROT // 2
    exponent = jnp.arange(half_rot, dtype=jnp.float32) * (2.0 / ROT)
    inverse = jnp.power(jnp.float32(10000.0), -exponent)
    angles = positions.astype(jnp.float32)[:, None] * inverse[None, :]
    cosine = jnp.cos(angles)[:, None, :]
    sine = jnp.sin(angles)[:, None, :]
    first = values[:, :, :half_rot]
    second = values[:, :, half_rot:ROT]
    return jnp.concatenate(
        [first * cosine - second * sine, second * cosine + first * sine, values[:, :, ROT:]], axis=2
    )


def fold_rows(left, shard):
    return jnp.dot(
        left, lax.all_gather(shard, "fsdp", axis=0, tiled=True), preferred_element_type=jnp.float32
    )


def map_back(grad_rows, shard):
    return lax.dot_general(
        grad_rows,
        lax.all_gather(shard, "fsdp", axis=0, tiled=True),
        (((1,), (1,)), ((), ())),
        preferred_element_type=jnp.float32,
    )


def grad_joint(left, right_side):
    seq_count = lax.axis_size("seq")
    fsdp_count = lax.axis_size("fsdp")
    token_count, total_rows = left.shape
    share = total_rows // (seq_count * fsdp_count)
    permuted = (
        left.reshape(token_count, fsdp_count, seq_count, share)
        .transpose(0, 2, 1, 3)
        .reshape(token_count, total_rows)
    )
    return lax.psum_scatter(
        lax.dot_general(
            permuted, right_side, (((0,), (0,)), ((), ())), preferred_element_type=jnp.float32
        ),
        ("seq", "fsdp"),
        scatter_dimension=0,
        tiled=True,
    )


def general_plan(
    inputs,
    segments,
    norm1_gain,
    norm1_bias,
    qkv_weight,
    qkv_bias,
    out_weight,
    norm2_gain,
    norm2_bias,
    gate_up_weight,
    down_weight,
    cotangent,
):
    row_count, local_len, features = inputs.shape
    fsdp_count = lax.axis_size("fsdp")
    fsdp_rank = lax.axis_index("fsdp")
    block_rank = lax.axis_index("seq") * fsdp_count + fsdp_rank
    token_count = row_count * local_len
    head_count = features // HD
    ff_width = gate_up_weight.shape[1] // 2
    scale_factor = HD ** (-0.5)
    flat = inputs.reshape(token_count, features).astype(jnp.float32)
    local_pos = block_rank * local_len + jnp.arange(local_len, dtype=jnp.int32)
    positions = jnp.tile(local_pos, row_count)
    weight_set = (qkv_weight, out_weight, gate_up_weight, down_weight)

    def forward_product(left, slot_index):
        return fold_rows(left, weight_set[slot_index])

    def backward_product(grad_rows, slot_index):
        return map_back(grad_rows, weight_set[slot_index])

    normed_in, norm1_back = jax.vjp(layer_norm, flat, norm1_gain, norm1_bias)
    in_low = normed_in.astype(jnp.bfloat16)
    mixed = forward_product(in_low, 0) + qkv_bias
    turn_input = mixed[:, : 2 * features].reshape(token_count, 2 * head_count, HD)
    turned, turn_back = jax.vjp(lambda values: rotate(values, positions), turn_input)
    turned_low = turned.astype(jnp.bfloat16)
    queries = turned_low[:, :head_count].reshape(row_count, local_len, features)
    keys_loc = turned_low[:, head_count:].reshape(row_count, local_len, features)
    values_loc = (
        mixed[:, 2 * features :].astype(jnp.bfloat16).reshape(row_count, local_len, features)
    )
    head_query, head_key, head_value = (
        lax.all_to_all(queries, "seq", split_axis=2, concat_axis=1, tiled=True),
        lax.all_to_all(keys_loc, "seq", split_axis=2, concat_axis=1, tiled=True),
        lax.all_to_all(values_loc, "seq", split_axis=2, concat_axis=1, tiled=True),
    )
    all_keys, all_values = (
        lax.all_gather(head_key, "fsdp", axis=1, tiled=True),
        lax.all_gather(head_value, "fsdp", axis=1, tiled=True),
    )
    query_len = head_query.shape[1]
    key_len = all_keys.shape[1]
    head_width = head_query.shape[2]
    local_heads = head_width // HD
    query_four = head_query.reshape(row_count, query_len, local_heads, HD)
    keys_four = all_keys.reshape(row_count, key_len, local_heads, HD)
    values_four = all_values.reshape(row_count, key_len, local_heads, HD)
    query_index = jnp.arange(query_len, dtype=jnp.int32)
    query_pos = (
        query_index // local_len * fsdp_count + fsdp_rank
    ) * local_len + query_index % local_len
    key_index = jnp.arange(key_len, dtype=jnp.int32)
    key_pos = (
        key_index % query_len // local_len * fsdp_count + key_index // query_len
    ) * local_len + key_index % local_len
    query_seg = jnp.take(segments, query_pos, axis=1)
    key_seg = jnp.take(segments, key_pos, axis=1)
    span = min(512, key_len)
    block_count = key_len // span

    def block_inputs(block_index):
        first_row = block_index * span
        block_keys = lax.dynamic_slice_in_dim(keys_four, first_row, span, 1)
        block_values = lax.dynamic_slice_in_dim(values_four, first_row, span, 1)
        block_pos = lax.dynamic_slice_in_dim(key_pos, first_row, span, 0)
        block_seg = lax.dynamic_slice_in_dim(key_seg, first_row, span, 1)
        allowed = (query_seg[:, :, None] == block_seg[:, None, :]) & (
            block_pos[None, None, :] <= query_pos[None, :, None]
        )
        scores = (
            jnp.einsum(
                "rqhd,rkhd->rhqk", query_four, block_keys, preferred_element_type=jnp.float32
            )
            * scale_factor
        )
        return (first_row, block_keys, block_values, allowed[:, None], scores)

    def forward_block(carry, block_index):
        row_top, running, weighted = carry
        first_row, block_keys, block_values, allowed, scores = block_inputs(block_index)
        new_top = jnp.maximum(row_top, jnp.max(jnp.where(allowed, scores, MASKED), axis=-1))
        probs = jnp.where(allowed, jnp.exp(scores - new_top[..., None]), 0.0)
        factor = jnp.exp(row_top - new_top)
        running = running * factor + jnp.sum(probs, axis=-1)
        weighted = weighted * factor[..., None] + jnp.einsum(
            "rhqk,rkhd->rhqd",
            probs.astype(jnp.bfloat16),
            block_values,
            preferred_element_type=jnp.float32,
        )
        return ((new_top, running, weighted), None)

    start_top = jnp.full((row_count, local_heads, query_len), MASKED, jnp.float32)
    start_total = jnp.zeros((row_count, local_heads, query_len), jnp.float32)
    start_weighted = jnp.zeros((row_count, local_heads, query_len, HD), jnp.float32)
    (row_top, running, weighted), _ = lax.scan(
        forward_block, (start_top, start_total, start_weighted), jnp.arange(block_count)
    )
    log_total = row_top + jnp.log(running)
    attended_heads = (
        (weighted / running[..., None])
        .transpose(0, 2, 1, 3)
        .reshape(row_count, query_len, head_width)
        .astype(jnp.bfloat16)
    )
    attended_loc = lax.all_to_all(attended_heads, "seq", split_axis=1, concat_axis=2, tiled=True)
    att_flat = attended_loc.reshape(token_count, features)
    middle = flat + forward_product(att_flat, 1)
    normed_mid, norm2_back = jax.vjp(layer_norm, middle, norm2_gain, norm2_bias)
    mid_low = normed_mid.astype(jnp.bfloat16)
    gate_up = forward_product(mid_low, 2)
    act_value, silu_back = jax.vjp(
        lambda gate_part, up_part: jax.nn.silu(gate_part) * up_part,
        gate_up[:, :ff_width],
        gate_up[:, ff_width:],
    )
    act_low = act_value.astype(jnp.bfloat16)
    result = middle + forward_product(act_low, 3)
    d_out = cotangent.reshape(token_count, features)
    d_act = backward_product(d_out, 3)
    d_gate, d_up = silu_back(d_act)
    d_gate_up = jnp.concatenate([d_gate, d_up], axis=1).astype(jnp.bfloat16)
    d_mid_norm = backward_product(d_gate_up, 2)
    d_middle_part, d_gain_two, d_bias_two = norm2_back(d_mid_norm)
    d_middle = d_out.astype(jnp.float32) + d_middle_part
    d_branch = d_middle.astype(jnp.bfloat16)
    d_attended = (
        backward_product(d_branch, 1).astype(jnp.bfloat16).reshape(row_count, local_len, features)
    )
    d_heads = lax.all_to_all(d_attended, "seq", split_axis=2, concat_axis=1, tiled=True)
    d_heads_four = d_heads.reshape(row_count, query_len, local_heads, HD)
    attended_four = attended_heads.reshape(row_count, query_len, local_heads, HD)
    delta = jnp.einsum(
        "rqhd,rqhd->rhq", d_heads_four.astype(jnp.float32), attended_four.astype(jnp.float32)
    )

    def backward_block(carry, block_index):
        d_query, d_keys_all, d_values_all = carry
        first_row, block_keys, block_values, allowed, scores = block_inputs(block_index)
        probs = jnp.where(allowed, jnp.exp(scores - log_total[..., None]), 0.0)
        d_block_values = jnp.einsum(
            "rhqk,rqhd->rkhd",
            probs.astype(jnp.bfloat16),
            d_heads_four,
            preferred_element_type=jnp.float32,
        )
        d_probs = jnp.einsum(
            "rqhd,rkhd->rhqk", d_heads_four, block_values, preferred_element_type=jnp.float32
        )
        d_scores = (probs * (d_probs - delta[..., None])).astype(jnp.bfloat16)
        d_query = (
            d_query
            + jnp.einsum(
                "rhqk,rkhd->rqhd", d_scores, block_keys, preferred_element_type=jnp.float32
            )
            * scale_factor
        )
        d_block_keys = (
            jnp.einsum("rhqk,rqhd->rkhd", d_scores, query_four, preferred_element_type=jnp.float32)
            * scale_factor
        )
        d_keys_all = lax.dynamic_update_slice_in_dim(d_keys_all, d_block_keys, first_row, 1)
        d_values_all = lax.dynamic_update_slice_in_dim(d_values_all, d_block_values, first_row, 1)
        return ((d_query, d_keys_all, d_values_all), None)

    zero_query = jnp.zeros((row_count, query_len, local_heads, HD), jnp.float32)
    zero_keys = jnp.zeros((row_count, key_len, local_heads, HD), jnp.float32)
    (d_query, d_keys_all, d_values_all), _ = lax.scan(
        backward_block, (zero_query, zero_keys, zero_keys), jnp.arange(block_count)
    )
    d_keys_sum, d_values_sum = (
        lax.psum_scatter(
            d_keys_all.reshape(row_count, key_len, head_width).astype(jnp.bfloat16),
            "fsdp",
            scatter_dimension=1,
            tiled=True,
        ).astype(jnp.float32),
        lax.psum_scatter(
            d_values_all.reshape(row_count, key_len, head_width).astype(jnp.bfloat16),
            "fsdp",
            scatter_dimension=1,
            tiled=True,
        ).astype(jnp.float32),
    )
    d_query_low = d_query.reshape(row_count, query_len, head_width).astype(jnp.bfloat16)
    dq_back, dk_back, dv_back = (
        lax.all_to_all(d_query_low, "seq", split_axis=1, concat_axis=2, tiled=True),
        lax.all_to_all(
            d_keys_sum.astype(jnp.bfloat16), "seq", split_axis=1, concat_axis=2, tiled=True
        ),
        lax.all_to_all(
            d_values_sum.astype(jnp.bfloat16), "seq", split_axis=1, concat_axis=2, tiled=True
        ),
    )
    d_turned = jnp.concatenate(
        [
            dq_back.reshape(token_count, head_count, HD),
            dk_back.reshape(token_count, head_count, HD),
        ],
        axis=1,
    ).astype(jnp.float32)
    (d_turn_input,) = turn_back(d_turned)
    d_mixed = jnp.concatenate(
        [
            d_turn_input.reshape(token_count, 2 * features),
            dv_back.reshape(token_count, features).astype(jnp.float32),
        ],
        axis=1,
    ).astype(jnp.bfloat16)
    d_qkv_bias = jnp.sum(d_mixed.astype(jnp.float32), axis=0)
    d_norm_in = backward_product(d_mixed, 0)
    d_flat_part, d_gain_one, d_bias_one = norm1_back(d_norm_in)
    d_inputs = d_middle + d_flat_part
    first_grad = grad_joint(in_low, d_mixed)
    second_grad = grad_joint(att_flat, d_branch)
    third_grad = grad_joint(mid_low, d_gate_up)
    fourth_grad = grad_joint(act_low, d_out)
    qkv_grad, out_grad, gate_up_grad, down_grad = (
        lax.all_gather(first_grad.astype(jnp.bfloat16), "seq", axis=0, tiled=True).astype(
            first_grad.dtype
        ),
        lax.all_gather(second_grad.astype(jnp.bfloat16), "seq", axis=0, tiled=True).astype(
            second_grad.dtype
        ),
        lax.all_gather(third_grad.astype(jnp.bfloat16), "seq", axis=0, tiled=True).astype(
            third_grad.dtype
        ),
        lax.all_gather(fourth_grad.astype(jnp.bfloat16), "seq", axis=0, tiled=True).astype(
            fourth_grad.dtype
        ),
    )
    gain_one, bias_one, bias_qkv, gain_two, bias_two = lax.psum(
        (d_gain_one, d_bias_one, d_qkv_bias, d_gain_two, d_bias_two), ("seq", "fsdp")
    )
    return (
        result.reshape(row_count, local_len, features),
        d_inputs.reshape(row_count, local_len, features),
        gain_one,
        bias_one,
        qkv_grad,
        bias_qkv,
        out_grad,
        gain_two,
        bias_two,
        gate_up_grad,
        down_grad,
    )


BLOCK = 512
BF = jnp.bfloat16
F32 = jnp.float32
SMALL = pl.CostEstimate(flops=1000, bytes_accessed=1000, transcendentals=0)


def swap(value, mask):
    return lax.ppermute(value, ("z", "core", "fsdp"), [(i, i ^ mask) for i in range(32)])


def shift(value, steps):
    return lax.ppermute(value, ("z", "core", "fsdp"), [(i, (i + 8 * steps) % 32) for i in range(32)])


def pick(stacked, index):
    return lax.dynamic_index_in_dim(stacked, index, 0, keepdims=False)


def exchange(value, axis="fsdp"):
    return lax.all_to_all(value, axis, split_axis=0, concat_axis=0, tiled=True)


def gather_near(value):
    half = value.shape[0] // 2
    by_x = swap(value, 1)
    by_y = swap(value, 2)
    return [value, by_x, by_y, swap(by_x[:half], 2), swap(by_y[half:], 1)]


def both_cores(near):
    return near + [swap(piece, 4) for piece in near]


def gather_pieces(value):
    return both_cores(gather_near(value))


def sum_quad(terms):
    return terms[0].astype(F32) + sum(swap(terms[m].astype(BF), m).astype(F32) for m in (1, 2, 3))


def sum_plane(near, far):
    arrived = swap(far.astype(BF), 4)
    return sum_quad([near[m].astype(F32) + arrived[m].astype(F32) for m in range(4)])


def dot(left, right):
    return jnp.dot(left, right, preferred_element_type=F32)


def dot_rows(left, right):
    return lax.dot_general(left, right, (((1,), (1,)), ((), ())), preferred_element_type=F32)


def dot_cols(left, right):
    return lax.dot_general(left, right, (((0,), (0,)), ((), ())), preferred_element_type=F32)


def turn_tables(row_len):
    half_rot = ROT // 2
    lane = jnp.arange(2 * HD, dtype=jnp.int32) % HD
    exponent = (lane % half_rot).astype(F32) * (2.0 / ROT)
    inverse = jnp.power(jnp.float32(10000.0), -exponent)
    angles = jnp.arange(row_len, dtype=jnp.int32).astype(F32)[:, None] * inverse[None, :]
    cosine = jnp.where(lane < ROT, jnp.cos(angles), 1.0)
    sine = jnp.sin(angles)
    ahead = jnp.where(lane < half_rot, -sine, 0.0)
    behind = jnp.where((lane >= half_rot) & (lane < ROT), sine, 0.0)
    return cosine, ahead, behind


def attend_kernel(
    split_ref, where_ref, mixed_ref, cos_ref, ahead_ref, behind_ref,
    q_ref, k_ref, v_ref, o_ref, log_ref, mine_ref, theirs_ref, kz, vz,
):
    local_len = mixed_ref.shape[2]
    row_len = q_ref.shape[0]
    low = lax.broadcasted_iota(jnp.int32, (local_len, 2 * HD), 1) < HD

    def prepare(i, carry):
        rows = pl.ds(pl.multiple_of(i * local_len, local_len), local_len)
        cosine, ahead, behind = cos_ref[rows], ahead_ref[rows], behind_ref[rows]

        def turn(x):
            return (
                x * cosine
                + pltpu.roll(x, 2 * HD - ROT // 2, 1) * ahead
                + pltpu.roll(x, ROT // 2, 1) * behind
            )

        first = mixed_ref[i, 0]
        second = mixed_ref[i, 1]
        turned0 = turn(first[:, : 2 * HD])
        turned1 = turn(second[:, : 2 * HD])
        q = jnp.where(low, turned0, pltpu.roll(turned1, HD, 1))
        k = jnp.where(low, pltpu.roll(turned0, HD, 1), turned1)
        v = jnp.where(low, first[:, 2 * HD :], second[:, 2 * HD :])
        q_ref[rows] = (q * HD**-0.5).astype(BF)
        k_ref[rows] = k.astype(BF)
        v_ref[rows] = v.astype(BF)
        kz[0, rows] = jnp.where(low, k, 0.0).astype(BF)
        kz[1, rows] = jnp.where(low, 0.0, k).astype(BF)
        vz[0, rows] = jnp.where(low, v, 0.0).astype(BF)
        vz[1, rows] = jnp.where(low, 0.0, v).astype(BF)
        return carry

    lax.fori_loop(0, row_len // local_len, prepare, 0)
    t_in = lax.broadcasted_iota(jnp.int32, (BLOCK, 1), 0)
    u_in = lax.broadcasted_iota(jnp.int32, (1, BLOCK), 1)
    low_q = lax.broadcasted_iota(jnp.int32, (BLOCK, 2 * HD), 1) < HD

    def query_block(qb, carry):
        rows = pl.ds(pl.multiple_of(qb * BLOCK, BLOCK), BLOCK)
        q = q_ref[rows]
        t = t_in + qb * BLOCK
        outs, logs = [], []
        for row in range(2):
            split = split_ref[row]
            start = jnp.where(t >= split, split, 0)

            def step(kb, state, diagonal, row=row, start=start):
                top, total, acc = state
                keys = pl.ds(pl.multiple_of(kb * BLOCK, BLOCK), BLOCK)
                u = u_in + kb * BLOCK
                scores = dot_rows(q, kz[row, keys])
                allowed = u >= start
                if diagonal:
                    allowed = allowed & (u <= t)
                scores = jnp.where(allowed, scores, MASKED)
                new_top = jnp.maximum(top, jnp.max(scores, axis=1, keepdims=True))
                probs = jnp.exp(scores - new_top)
                factor = jnp.exp(top - new_top)
                total = total * factor + jnp.sum(probs, axis=1, keepdims=True)
                acc = acc * factor + dot(probs.astype(BF), vz[row, keys])
                return new_top, total, acc

            state = (
                jnp.full((BLOCK, 1), MASKED, F32),
                jnp.zeros((BLOCK, 1), F32),
                jnp.zeros((BLOCK, 2 * HD), F32),
            )
            first_kb = jnp.where(qb * BLOCK >= split, split // BLOCK, 0)
            state = lax.fori_loop(
                first_kb, qb, lambda kb, state, step=step: step(kb, state, False), state
            )
            top, total, acc = step(qb, state, True)
            outs.append(acc / total)
            logs.append(top + jnp.log(total))
        o_ref[rows] = (outs[0] + outs[1]).astype(BF)
        turned = jnp.where(low_q, logs[0], logs[1]).T
        log_ref[0:1, rows] = turned[0:1]
        log_ref[1:2, rows] = turned[HD : HD + 1]
        step = lax.rem(qb - where_ref[0] + 4, 4)
        core = where_ref[1] // 4
        half = BLOCK // 2
        for ref, which in ((mine_ref, core), (theirs_ref, 1 - core)):
            ref[step] = o_ref[pl.ds(pl.multiple_of(qb * BLOCK + which * half, half), half)]
        return carry

    lax.fori_loop(0, row_len // BLOCK, query_block, 0)


def attend(split, where, mixed, tables):
    row_len = tables[0].shape[0]
    packed = jax.ShapeDtypeStruct((row_len, 2 * HD), BF)
    smem = pl.BlockSpec(memory_space=pltpu.SMEM)
    vmem = pl.BlockSpec(memory_space=pltpu.VMEM)
    pairs = 2 * row_len * row_len // 2
    return pl.pallas_call(
        attend_kernel,
        out_shape=(packed, packed, packed, packed, jax.ShapeDtypeStruct((2, row_len), F32))
        + (jax.ShapeDtypeStruct((4, row_len // 8, 2 * HD), BF),) * 2,
        in_specs=[smem, smem, vmem, vmem, vmem, vmem],
        out_specs=(vmem,) * 7,
        scratch_shapes=[pltpu.VMEM((2, row_len, 2 * HD), BF), pltpu.VMEM((2, row_len, 2 * HD), BF)],
        compiler_params=pltpu.CompilerParams(vmem_limit_bytes=48 * 2**20),
        cost_estimate=SMALL,
        name="attend",
    )(split, where, mixed, *tables)


def attend_back_kernel(
    split_ref, q_hbm, k_hbm, v_hbm, o_hbm, do_hbm, log_ref,
    cos_ref, ahead_ref, behind_ref,
    dmix_ref, dpos_ref, kz, vz, qz, dz, ktz, delta, dq_t, dk, dv,
    q_ref, k_ref, v_ref, o_ref, do_ref, sem,
):
    loads = [
        pltpu.make_async_copy(source, target, sem.at[n])
        for n, (source, target) in enumerate(
            ((k_hbm, k_ref), (v_hbm, v_ref), (q_hbm, q_ref), (do_hbm, do_ref), (o_hbm, o_ref))
        )
    ]
    for copy in loads:
        copy.start()
    for copy in loads:
        copy.wait()
    row_len = q_ref.shape[0]
    local_len = dmix_ref.shape[2]
    low = lax.broadcasted_iota(jnp.int32, (BLOCK, 2 * HD), 1) < HD
    low_t = lax.broadcasted_iota(jnp.int32, (2 * HD, BLOCK), 0) < HD
    lane = lax.broadcasted_iota(jnp.int32, (8, 2 * HD), 1)
    ones = [jnp.where(lane < HD, 1.0, 0.0).astype(BF), jnp.where(lane < HD, 0.0, 1.0).astype(BF)]

    def prepare(b, carry):
        rows = pl.ds(pl.multiple_of(b * BLOCK, BLOCK), BLOCK)
        zero = jnp.zeros((BLOCK, 2 * HD), F32)
        for ref, out in ((k_ref, kz), (v_ref, vz), (q_ref, qz), (do_ref, dz)):
            value = ref[rows].astype(F32)
            out[0, rows] = jnp.where(low, value, zero).astype(BF)
            out[1, rows] = jnp.where(low, zero, value).astype(BF)
        value = k_ref[rows].astype(F32).T
        ktz[0, :, rows] = jnp.where(low_t, value, 0.0).astype(BF)
        ktz[1, :, rows] = jnp.where(low_t, 0.0, value).astype(BF)
        product = do_ref[rows].astype(F32) * o_ref[rows].astype(F32)
        coarse = product.astype(BF)
        fine = (product - coarse.astype(F32)).astype(BF)
        for row in range(2):
            delta[row, :, rows] = dot_rows(ones[row], coarse) + dot_rows(ones[row], fine)
        dq_t[:, rows] = jnp.zeros((2 * HD, BLOCK), F32)
        return carry

    lax.fori_loop(0, row_len // BLOCK, prepare, 0)
    u_in = lax.broadcasted_iota(jnp.int32, (BLOCK, 1), 0)
    t_in = lax.broadcasted_iota(jnp.int32, (1, BLOCK), 1)

    def key_block(kb, carry):
        keys = pl.ds(pl.multiple_of(kb * BLOCK, BLOCK), BLOCK)
        u = u_in + kb * BLOCK
        sums_k, sums_v = [], []
        for row in range(2):
            split = split_ref[row]
            k_row = kz[row, keys]
            v_row = vz[row, keys]
            kt_row = ktz[row, :, keys]

            def step(qb, state, row=row, split=split, k_row=k_row, v_row=v_row, kt_row=kt_row):
                d_keys, d_values = state
                rows = pl.ds(pl.multiple_of(qb * BLOCK, BLOCK), BLOCK)
                t = t_in + qb * BLOCK
                start = jnp.where(t >= split, split, 0)
                allowed = (u >= start) & (u <= t)
                scores = dot_rows(k_row, q_ref[rows])
                probs = jnp.where(allowed, jnp.exp(scores - log_ref[pl.ds(row, 1), rows]), 0.0)
                d_probs = dot_rows(v_row, do_ref[rows])
                d_scores = (probs * (d_probs - delta[row, pl.ds(0, 1), rows])).astype(BF)
                d_values = d_values + dot(probs.astype(BF), dz[row, rows])
                d_keys = d_keys + dot(d_scores, qz[row, rows])
                dq_t[:, rows] += dot(kt_row, d_scores)
                return d_keys, d_values

            zero = jnp.zeros((BLOCK, 2 * HD), F32)
            last = jnp.where(
                (kb + 1) * BLOCK <= split, (split + BLOCK - 1) // BLOCK, row_len // BLOCK
            )
            d_keys, d_values = lax.fori_loop(kb, last, step, (zero, zero))
            sums_k.append(d_keys)
            sums_v.append(d_values)
        dk[keys] = sums_k[0] + sums_k[1]
        dv[keys] = sums_v[0] + sums_v[1]
        return carry

    lax.fori_loop(0, row_len // BLOCK, key_block, 0)
    low_l = lax.broadcasted_iota(jnp.int32, (local_len, 2 * HD), 1) < HD
    per = 2 * HD // local_len


    def finish(b, carry):
        start = pl.multiple_of(b * 2 * HD, 2 * HD)
        dq = dq_t[:, pl.ds(start, 2 * HD)].T * HD**-0.5
        for part in range(per):
            i = b * per + part
            rows = pl.ds(pl.multiple_of(i * local_len, local_len), local_len)
            cosine, ahead, behind = cos_ref[rows], ahead_ref[rows], behind_ref[rows]

            def turn(x, cosine=cosine, ahead=ahead, behind=behind):
                return (
                    x * cosine
                    - pltpu.roll(x, 2 * HD - ROT // 2, 1) * ahead
                    - pltpu.roll(x, ROT // 2, 1) * behind
                )

            q_part = turn(dq[part * local_len : (part + 1) * local_len])
            k_part = turn(dk[rows])
            v_part = dv[rows]
            first = jnp.where(low_l, q_part, pltpu.roll(k_part, HD, 1)).astype(BF)
            second = jnp.where(low_l, pltpu.roll(q_part, HD, 1), k_part).astype(BF)
            dpos_ref[rows, : 2 * HD] = first
            dpos_ref[rows, 2 * HD : 4 * HD] = second
            dpos_ref[rows, 4 * HD :] = v_part.astype(BF)
            dmix_ref[i, 0, :, : 2 * HD] = first
            dmix_ref[i, 1, :, : 2 * HD] = second
            dmix_ref[i, 0, :, 2 * HD :] = jnp.where(low_l, v_part, 0.0).astype(BF)
            dmix_ref[i, 1, :, 2 * HD :] = jnp.where(low_l, pltpu.roll(v_part, HD, 1), 0.0).astype(BF)
        return carry

    lax.fori_loop(0, row_len // (2 * HD), finish, 0)


def attend_back(split, q, k, v, out, d_out, logs, tables, local_len):
    row_len = q.shape[0]
    smem = pl.BlockSpec(memory_space=pltpu.SMEM)
    vmem = pl.BlockSpec(memory_space=pltpu.VMEM)
    masked = pltpu.VMEM((2, row_len, 2 * HD), BF)
    whole = pltpu.VMEM((row_len, 2 * HD), F32)
    pairs = 2 * row_len * row_len // 2
    return pl.pallas_call(
        attend_back_kernel,
        out_shape=(
            jax.ShapeDtypeStruct((row_len // local_len, 2, local_len, 4 * HD), BF),
        )
        + (jax.ShapeDtypeStruct((row_len, 6 * HD), BF),),
        in_specs=[smem] + [pl.BlockSpec(memory_space=pltpu.HBM)] * 5 + [vmem] * 4,
        out_specs=(vmem,) * 2,
        scratch_shapes=[
            masked, masked, masked, masked,
            pltpu.VMEM((2, 2 * HD, row_len), BF),
            pltpu.VMEM((2, 8, row_len), F32),
            pltpu.VMEM((2 * HD, row_len), F32),
            whole, whole,
        ]
        + [pltpu.VMEM((row_len, 2 * HD), BF)] * 5
        + [pltpu.SemaphoreType.DMA((5,))],
        compiler_params=pltpu.CompilerParams(vmem_limit_bytes=48 * 2**20),
        cost_estimate=SMALL,
        name="attend_back",
    )(split, q, k, v, out, d_out, logs, *tables)


def pick_heads_kernel(where_ref, q_ref, k_ref, v_ref, out_ref):
    wide = 2 * HD
    low = lax.broadcasted_iota(jnp.int32, (q_ref.shape[0], wide), 1) < HD
    for core in (0, 1):

        @pl.when(where_ref[1] // 4 == core)
        def _(core=core):
            def join(left, right):
                if core == 0:
                    return jnp.where(low, left, pltpu.roll(right, HD, 1)).astype(BF)
                return jnp.where(low, pltpu.roll(left, HD, 1), right).astype(BF)

            for z in range(4):
                cols = slice(z * wide, (z + 1) * wide)
                out_ref[:, cols] = join(q_ref[:, cols].astype(F32), k_ref[:, cols].astype(F32))
            for pair in range(2):
                left, right = (
                    v_ref[:, (2 * pair + n) * wide : (2 * pair + n + 1) * wide].astype(F32) for n in (0, 1)
                )
                out_ref[:, (4 + pair) * wide : (5 + pair) * wide] = join(left, right)


def pick_heads(where, weight):
    rows, columns = weight.shape
    wide = columns // 12
    blocks = [
        pl.BlockSpec((rows, wide), lambda chip, where, part=part: (0, part * 4 + chip)) for part in range(3)
    ]
    return pl.pallas_call(
        pick_heads_kernel,
        grid_spec=pltpu.PrefetchScalarGridSpec(
            num_scalar_prefetch=1,
            grid=(4,),
            in_specs=blocks,
            out_specs=pl.BlockSpec((None, rows, 12 * HD), lambda chip, where: (chip, 0, 0)),
        ),
        out_shape=jax.ShapeDtypeStruct((4, rows, 12 * HD), BF),
        compiler_params=pltpu.CompilerParams(vmem_limit_bytes=32 * 2**20),
        cost_estimate=SMALL,
        name="pick_heads",
    )(where, weight, weight, weight)


def small_call(kernel, name, out_shape, where, *arrays, flops=0, scratch=(), limit=32):
    size = sum(x.size * x.dtype.itemsize for x in arrays)
    vmem = pl.BlockSpec(memory_space=pltpu.VMEM)
    return pl.pallas_call(
        kernel,
        out_shape=out_shape,
        in_specs=[pl.BlockSpec(memory_space=pltpu.SMEM)] + [vmem] * len(arrays),
        out_specs=[vmem] * len(out_shape),
        scratch_shapes=scratch,
        compiler_params=pltpu.CompilerParams(vmem_limit_bytes=limit * 2**20),
        cost_estimate=SMALL,
        name=name,
    )(where, *arrays)


def pair_kernel(where_ref, mine_ref, theirs_ref, *outs):
    low = lax.broadcasted_iota(jnp.int32, mine_ref.shape[1:], 1) < HD
    for step, out in enumerate(outs):
        for core, (ref0, ref1) in enumerate(((mine_ref, theirs_ref), (theirs_ref, mine_ref))):

            @pl.when(where_ref[1] // 4 == core)
            def _(ref0=ref0, ref1=ref1):
                even, uneven = ref0[step].astype(F32), ref1[step].astype(F32)
                out[:, : 2 * HD] = jnp.where(low, even, pltpu.roll(uneven, HD, 1)).astype(BF)
                out[:, 2 * HD :] = jnp.where(low, pltpu.roll(even, HD, 1), uneven).astype(BF)


def out_project_kernel(where_ref, a0, a1, a2, a3, weight_ref, att_ref, o0, o1, o2, o3, sum_v):
    plane, rank = where_ref[0], where_ref[1] % 4
    span = a0.shape[0]
    for step, ref in enumerate((a0, a1, a2, a3)):
        lanes = pl.ds(pl.multiple_of(lax.rem(plane - step + 4, 4) * 2 * HD, 2 * HD), 2 * HD)
        for row in range(2):
            att_ref[row * span : (row + 1) * span, lanes] = ref[:, row * 2 * HD : (row + 1) * 2 * HD]
    sum_v[...] = dot(att_ref[...], weight_ref[...])
    part = span // 4
    for m, out in enumerate((o0, o1, o2, o3)):
        for row in range(2):
            rows = pl.ds(pl.multiple_of(row * span + (rank ^ m) * part, part), part)
            out[row * part : (row + 1) * part] = sum_v[rows].astype(out.dtype)


def d_att_kernel(where_ref, p0, p1, p2, p3_low, p3_high, weight_ref, branch_ref, heads_ref):
    rank = where_ref[1] % 4
    span = heads_ref.shape[1]
    part = span // 4
    for m, pieces in enumerate(((p0,), (p1,), (p2,), (p3_low, p3_high))):
        for row in range(2):
            rows = pl.ds(pl.multiple_of(row * span + (rank ^ m) * part, part), part)
            if len(pieces) == 2:
                branch_ref[rows] = pieces[row][...]
            else:
                branch_ref[rows] = pieces[0][row * part : (row + 1) * part]
    d_att = dot_rows(branch_ref[...], weight_ref[...])
    low = lax.broadcasted_iota(jnp.int32, heads_ref.shape[1:], 1) < HD
    for z in range(4):
        lanes = slice(z * 2 * HD, (z + 1) * 2 * HD)
        row0, row1 = d_att[:span, lanes], d_att[span:, lanes]
        heads_ref[2 * z] = jnp.where(low, row0, pltpu.roll(row1, HD, 1)).astype(BF)
        heads_ref[2 * z + 1] = jnp.where(low, pltpu.roll(row0, HD, 1), row1).astype(BF)


def d_in_kernel(where_ref, in_ref, weight_ref, near_ref, far_ref, x_v, d_v):
    core, rank = where_ref[1] // 4, where_ref[1] % 4
    reach, wide = in_ref.shape[1], 2 * HD
    features = weight_ref.shape[0]
    low = lax.broadcasted_iota(jnp.int32, (reach, wide), 1) < HD
    for z in range(4):
        for row in range(2):
            x_v[row * reach : (row + 1) * reach, z * wide : (z + 1) * wide] = in_ref[
                z, :, row * wide : (row + 1) * wide
            ]
    for pair in range(2):
        cols = slice((4 + pair) * wide, (5 + pair) * wide)
        one, two = (in_ref[2 * pair + n, :, 2 * wide :].astype(F32) for n in (0, 1))
        x_v[:reach, cols] = jnp.where(low, one, pltpu.roll(two, HD, 1)).astype(BF)
        x_v[reach:, cols] = jnp.where(low, pltpu.roll(one, HD, 1), two).astype(BF)
    part = reach // 8
    span = d_v.shape[1]

    def columns(n, carry):
        cols = pl.ds(pl.multiple_of(n * span, span), span)
        d_v[...] = dot_rows(x_v[...], weight_ref[cols])
        for ref, which in ((near_ref, core), (far_ref, 1 - core)):
            for m in range(4):
                for row in range(2):
                    first = row * reach + which * 4 * part + (rank ^ m) * part
                    rows = pl.ds(pl.multiple_of(first, part), part)
                    ref[m, row * part : (row + 1) * part, cols] = d_v[rows].astype(BF)
        return carry

    lax.fori_loop(0, features // span, columns, 0)


def hidden_kernel(where_ref, *refs, steps, own):
    n_mid, n_out = (10, 2) if own else (1, 4 * len(steps))
    mids, outs, refs = refs[:n_mid], refs[n_mid : n_mid + n_out], refs[n_mid + n_out :]
    gate_ref, up_ref, down_ref = refs[:3]
    refs = refs[3:] if own else refs[7:]
    alls, refs = refs[:4], refs[4:]
    d_mids, acts, refs = (refs[:2], refs[2:4], refs[4:]) if own else ((), (), refs)
    mid_v, out_v, gate_up_v, down_v, act_v, d_gate_v, d_up_v, sem_in, sem_w, sem_out = refs[:10]
    rows, features = mid_v.shape[1:]
    width, tile = down_v.shape[0], 256
    tiles = width // tile
    plane, mine = where_ref[0], where_ref[1]
    core = mine // 4
    shard = gate_ref.shape[1]
    step = rows // 4
    halves = 2 * len(steps)

    def blocks(h):
        base = lax.rem(plane + 4 - steps[h // 2], 4) * (2 * rows)
        return [
            pl.ds(pl.multiple_of(base + (mine ^ (4 * (h % 2) + m)) * step, step), step) for m in range(4)
        ]

    def loads(h):
        slot = h % 2
        if own:
            pieces, out_pieces = mids[5 * h : 5 * h + 5], outs[h : h + 1]
        else:
            pieces = [mids[0].at[block] for block in blocks(h)]
            out_pieces = outs[2 * h : 2 * h + 2]
        found = []
        for held, sources in ((mid_v, pieces), (out_v, out_pieces)):
            at = 0
            for source in sources:
                size = source.shape[0]
                found.append((source, held.at[slot, pl.ds(at, size)]))
                at += size
        return [pltpu.make_async_copy(x, y, sem_in.at[slot, n]) for n, (x, y) in enumerate(found)]

    def stores(h):
        slot = h % 2
        return [
            pltpu.make_async_copy(
                held.at[slot, pl.ds(m * step, step)], target.at[block], sem_out.at[slot, n, m]
            )
            for n, (held, target) in enumerate(zip((act_v, d_gate_v, d_up_v, out_v), alls))
            for m, block in enumerate(blocks(h))
        ]

    def tile_copies(j):
        cols = pl.ds(j * tile, tile)
        found = [
            (ref.at[m, :, cols], gate_up_v.at[g, pl.ds(m * shard, shard), cols])
            for g, ref in enumerate((gate_ref, up_ref))
            for m in range(4)
        ]
        first = pl.multiple_of(core * (down_ref.shape[0] - width) + j * tile, 128)
        found.append((down_ref.at[pl.ds(first, tile)], down_v.at[cols]))
        return [pltpu.make_async_copy(x, y, sem_w.at[j, n]) for n, (x, y) in enumerate(found)]

    def wait_tile(j):
        for copy in weight_copies[j]:
            copy.wait()
        if j == 0:

            @pl.when(core == 1)
            def _():
                gate_up_v[:, :, : 2 * width - down_ref.shape[0]] = jnp.zeros(
                    (2, features, 2 * width - down_ref.shape[0]), BF
                )

    def compute(slot, cols):
        gate = dot(mid_v[slot], gate_up_v[0, :, cols])
        up = dot(mid_v[slot], gate_up_v[1, :, cols])
        d_act = dot_rows(out_v[slot], down_v[cols])
        sig = 1.0 / (1.0 + jnp.exp(-gate))
        silu = gate * sig
        act_v[slot, :, cols] = (silu * up).astype(BF)
        d_gate_v[slot, :, cols] = (d_act * up * (sig + silu * (1.0 - sig))).astype(BF)
        d_up_v[slot, :, cols] = (d_act * silu).astype(BF)

    weight_copies = [tile_copies(j) for j in range(tiles)]
    for copies in [weight_copies[0], loads(0)] + weight_copies[1:] + [loads(1)]:
        for copy in copies:
            copy.start()
    for h in range(halves):
        slot = h % 2
        for copy in loads(h):
            copy.wait()
        if h == 0:
            for j in range(tiles):
                wait_tile(j)
                compute(0, pl.ds(j * tile, tile))
        else:
            compute(slot, pl.ds(0, tile))
            if h + 1 < halves:
                for copy in stores(h - 1):
                    copy.wait()
                for copy in loads(h + 1):
                    copy.start()

            def part(j, carry, slot=slot):
                compute(slot, pl.ds(pl.multiple_of(j * tile, tile), tile))
                return carry

            lax.fori_loop(1, tiles, part, 0)
        for copy in stores(h):
            copy.start()
    left = []
    if own:
        sum_v = refs[10]
        span = 512
        for i in (1, 0):
            for m in range(4):
                part = pl.ds(m * step, step)
                left.append(
                    pltpu.make_async_copy(act_v.at[i, part], acts[i].at[m], sem_out.at[i, 4, m])
                )
                left[-1].start()

            def term(n, carry, i=i):
                cols = pl.ds(pl.multiple_of(n * span, span), span)
                sum_v[i, :, cols] = (
                    dot_rows(d_gate_v[i], gate_up_v[0, cols]) + dot_rows(d_up_v[i], gate_up_v[1, cols])
                ).astype(BF)
                return carry

            lax.fori_loop(0, features // span, term, 0)
            for m in range(4):
                part = pl.ds(m * step, step)
                left.append(
                    pltpu.make_async_copy(sum_v.at[i, part], d_mids[i].at[m], sem_out.at[i, 5, m])
                )
                left[-1].start()
    for h in (halves - 2, halves - 1):
        left += stores(h)
    for copy in left:
        copy.wait()


def hidden_layer(where, mids, outs, weights, total, steps=(0,), before=None):
    own = before is None
    features = outs[0].shape[1]
    rows, width = total // 8, weights[0].shape[2]
    narrow = jax.ShapeDtypeStruct((total, width), BF)
    wide = jax.ShapeDtypeStruct((total, features), BF)
    term = jax.ShapeDtypeStruct((4, rows // 4, features), BF)
    act = jax.ShapeDtypeStruct((4, rows // 4, width), BF)
    held = pltpu.VMEM((2, rows, features), BF)
    small = pltpu.VMEM((2, rows, width), BF)
    dma = pltpu.SemaphoreType.DMA
    count = len(mids) + len(outs)
    kept = [] if own else list(before)
    hbm = pl.BlockSpec(memory_space=pltpu.HBM)
    found = pl.pallas_call(
        functools.partial(hidden_kernel, steps=steps, own=own),
        in_specs=[pl.BlockSpec(memory_space=pltpu.SMEM)] + [hbm] * (count + 3 + len(kept)),
        out_specs=[hbm] * (8 if own else 4),
        out_shape=[narrow, narrow, narrow, wide] + ([term, term, act, act] if own else []),
        input_output_aliases={count + 4 + n: n for n in range(len(kept))},
        scratch_shapes=[
            held, held,
            pltpu.VMEM((2, features, width), BF),
            pltpu.VMEM((width, features), BF),
            small, small, small,
            dma((2, 9)), dma((width // 256, 9)), dma((2, 6, 4)),
        ]
        + ([held] if own else []),
        compiler_params=pltpu.CompilerParams(vmem_limit_bytes=(38 if own else 32) * 2**20),
        cost_estimate=SMALL,
        name="hidden",
    )(where, *mids, *outs, *weights, *kept)
    return list(found[:4]), list(found[4:])


def weight_grad_kernel(left_ref, right_ref, out_ref):
    out_ref[...] = dot_cols(left_ref[...], right_ref[...]).astype(BF)


def weight_grad(left, right):
    tokens, features = left.shape
    width = right.shape[1]
    step = 256
    return pl.pallas_call(
        weight_grad_kernel,
        grid=(features // step,),
        in_specs=[
            pl.BlockSpec((tokens, step), lambda i: (0, i)),
            pl.BlockSpec((tokens, width), lambda i: (0, 0), pipeline_mode=pl.Buffered(1)),
        ],
        out_specs=pl.BlockSpec((step, width), lambda i: (i, 0)),
        out_shape=jax.ShapeDtypeStruct((features, width), BF),
        compiler_params=pltpu.CompilerParams(vmem_limit_bytes=48 * 2**20),
        cost_estimate=SMALL,
        name="weight_grad",
    )(left, right)


def place_columns_kernel(where_ref, own_ref, other_ref, *rest):
    out_ref = rest[-1]
    wide = own_ref.shape[-1]
    extra = out_ref.shape[-1] - wide

    @pl.when(where_ref[0] == 0)
    def _():
        out_ref[:, :wide] = own_ref[...].astype(F32)
        out_ref[:, wide:] = other_ref[:, wide - extra :].astype(F32)

    @pl.when(where_ref[0] == 1)
    def _():
        out_ref[:, :wide] = other_ref[...].astype(F32)
        out_ref[:, wide:] = own_ref[:, wide - extra :].astype(F32)


def place_columns(core, own, other, before, chip_width, kind):
    chips, rows, wide = own.shape
    cut = rows // 2
    half = pl.BlockSpec((None, cut, wide), lambda chip, b, core: (chip, b, 0))
    return pl.pallas_call(
        place_columns_kernel,
        grid_spec=pltpu.PrefetchScalarGridSpec(
            num_scalar_prefetch=1,
            grid=(chips, rows // cut),
            in_specs=[half, half] + ([] if before is None else [pl.BlockSpec(memory_space=pl.ANY)]),
            out_specs=pl.BlockSpec((cut, chip_width), lambda chip, b, core: (b, kind * chips + chip)),
        ),
        out_shape=jax.ShapeDtypeStruct((rows, 2 * chips * chip_width), F32),
        input_output_aliases={} if before is None else {3: 0},
        compiler_params=pltpu.CompilerParams(vmem_limit_bytes=32 * 2**20),
        cost_estimate=SMALL,
        name="place_columns",
    )(core, own, other, *([] if before is None else [before]))


def place_down_kernel(core_ref, own_ref, other_ref, out_ref, *, lead):
    first = pl.program_id(0) < lead
    mine = first == (core_ref[0] == 0)

    @pl.when(mine)
    def _():
        out_ref[...] = own_ref[...].astype(F32)

    @pl.when(jnp.logical_not(mine))
    def _():
        out_ref[...] = other_ref[...].astype(F32)


def place_down(core, own, other, total):
    width, features = own.shape
    step = 128
    count, lead = total // step, width // step
    skip = 2 * lead - count

    def block(of_core):
        def index(i, core):
            which = core[0] if of_core else 1 - core[0]
            return (jnp.where(which == 0, jnp.minimum(i, lead - 1), jnp.maximum(i - lead + skip, 0)), 0)

        return pl.BlockSpec((step, features), index)

    return pl.pallas_call(
        functools.partial(place_down_kernel, lead=lead),
        grid_spec=pltpu.PrefetchScalarGridSpec(
            num_scalar_prefetch=1,
            grid=(count,),
            in_specs=[block(True), block(False)],
            out_specs=pl.BlockSpec((step, features), lambda i, core: (i, 0)),
        ),
        out_shape=jax.ShapeDtypeStruct((total, features), F32),
        cost_estimate=SMALL,
        name="place_down",
    )(core, own, other)


def place_qkv_kernel(where_ref, own_ref, other_ref, out_ref):
    cut = own_ref.shape[2]
    core = where_ref[0]
    for ref, half in ((own_ref, core), (other_ref, 1 - core)):
        rows = pl.ds(pl.multiple_of(half * cut, cut), cut)
        for z in range(4):
            out_ref[rows, z * 2 * HD : (z + 1) * 2 * HD] = ref[z, 0].astype(F32)


def place_qkv(where, own, other):
    _, _, cut, wide = own.shape
    parts = wide // (2 * HD)
    piece = pl.BlockSpec((4, 1, cut, 2 * HD), lambda part, chip, where: (0, chip ^ where[1], 0, part))
    return pl.pallas_call(
        place_qkv_kernel,
        grid_spec=pltpu.PrefetchScalarGridSpec(
            num_scalar_prefetch=1,
            grid=(parts, 4),
            in_specs=[piece, piece],
            out_specs=pl.BlockSpec((2 * cut, 8 * HD), lambda part, chip, where: (0, part * 4 + chip)),
        ),
        out_shape=jax.ShapeDtypeStruct((2 * cut, parts * 32 * HD), F32),
        cost_estimate=SMALL,
        name="place_qkv",
    )(where, own, other)


def tie(*values):
    return lax.optimization_barrier(values)


def plane_plan(
    inputs,
    segments,
    norm1_gain,
    norm1_bias,
    qkv_weight,
    qkv_bias,
    out_weight,
    norm2_gain,
    norm2_bias,
    gate_up_weight,
    down_weight,
    cotangent,
):
    row_count, local_len, features = inputs.shape
    row_len = segments.shape[1]
    tokens = row_count * local_len
    plane, core, rank = lax.axis_index("z"), lax.axis_index("core"), lax.axis_index("fsdp")
    seq = plane * 2 + core
    own = core * 4 + rank
    shard = features // 4
    hidden = gate_up_weight.shape[1] // 2
    chip_width = hidden // 4
    width = -(-chip_width // 256) * 128
    tables = turn_tables(row_len)
    split = jnp.sum((segments == 0).astype(jnp.int32), axis=1)
    where = jnp.stack([plane, own]).astype(jnp.int32)

    def head_columns(chip):
        parts = [
            lax.dynamic_slice_in_dim(qkv_weight, (chip * 8 + seq) * HD + part * features, HD, 1)
            for part in (0, 1, 2)
        ]
        return jnp.concatenate(parts + parts[2:], axis=1)

    head_weight = exchange(jnp.stack([head_columns(chip) for chip in range(4)])).reshape(features, 4 * HD)
    picked = pick_heads(where, qkv_weight)
    head_first = (rank * 8 + seq) * HD
    bias_parts = [
        lax.dynamic_slice_in_dim(qkv_bias, head_first + part * features, HD, 0) for part in (0, 1, 2)
    ]
    head_bias = jnp.concatenate(bias_parts + bias_parts[2:])
    hidden_first = core * (chip_width - width)

    def hidden_columns(kind):
        firsts = [hidden_first + chip * chip_width + kind * hidden for chip in range(4)]
        return jnp.stack([lax.dynamic_slice_in_dim(gate_up_weight, first, width, 1) for first in firsts])

    gate_weight, up_weight = hidden_columns(0), hidden_columns(1)

    flat = inputs.reshape(tokens, features).astype(F32)
    normed_in, norm1_back = jax.vjp(layer_norm, flat, norm1_gain, norm1_bias)
    everywhere = ("z", "core", "fsdp")
    in_all = lax.all_gather(normed_in.astype(BF), everywhere, axis=0, tiled=True)
    d_out = cotangent.reshape(tokens, features)
    out_near = jnp.concatenate(gather_near(d_out), axis=0)
    out_far = swap(out_near, 4)
    in_all, out_near, out_far, gate_weight, up_weight, head_weight, picked, *tables = tie(
        in_all, out_near, out_far, gate_weight, up_weight, head_weight, picked, *tables
    )
    lows, highs = [out_near[: 2 * tokens]], [out_near[2 * tokens :]]

    mixed = (dot(in_all, head_weight) + head_bias).reshape(
        row_len // local_len, row_count, local_len, 4 * HD
    )
    q, k, v, out_heads, logs, mine, theirs, gate_weight, low, up_weight = tie(
        *attend(split, where, mixed, tables), exchange(gate_weight), shift(lows[0], 1), up_weight
    )
    lows.append(low)
    span = row_len // 8
    pair = jax.ShapeDtypeStruct((span, 4 * HD), BF)
    pairs = small_call(pair_kernel, "pair", [pair] * 4, where, mine, swap(theirs, 4))
    arrived = [pairs[0]] + [shift(pairs[n], n) for n in (1, 2, 3)]
    square = row_count * span
    block = jax.ShapeDtypeStruct((tokens, features), BF)
    blocks = jax.ShapeDtypeStruct((4, tokens, features), BF)
    att, *branch = small_call(
        out_project_kernel,
        "out_project",
        [jax.ShapeDtypeStruct((square, shard), BF), jax.ShapeDtypeStruct((tokens, features), F32)]
        + [block] * 3,
        where,
        *arrived,
        out_weight,
        scratch=[pltpu.VMEM((square, features), F32)],
    )
    branch_sum, up_weight, high = tie(sum_quad(branch), exchange(up_weight), shift(highs[0], 1))
    highs.append(high)
    hidden_weights = [gate_weight, up_weight, down_weight]
    middle = flat + branch_sum
    normed_mid, norm2_back = jax.vjp(layer_norm, middle, norm2_gain, norm2_bias)
    mid_low = normed_mid.astype(BF)

    mid_pieces = gather_pieces(mid_low)
    *mid_pieces, mid_own, low = tie(*mid_pieces, mid_low, shift(lows[1], 1))
    lows.append(low)
    mid_all = lax.all_gather(mid_own, everywhere, axis=0, tiled=True)
    total = row_count * row_len
    hidden_all, (d_near, d_far, act_near, act_far) = hidden_layer(
        where, mid_pieces, [out_near, out_far], hidden_weights, total
    )
    d_near, d_far, high = tie(d_near, d_far, shift(highs[1], 1))
    highs.append(high)
    d_norm_mid, low = tie(sum_plane(d_near, d_far), shift(lows[2], 1))
    lows.append(low)
    d_middle_part, d_gain_two, d_bias_two = norm2_back(d_norm_mid)
    d_middle = d_out.astype(F32) + d_middle_part

    d_pieces = gather_near(d_middle.astype(BF))
    d_branch, d_heads = small_call(
        d_att_kernel,
        "d_att",
        [
            jax.ShapeDtypeStruct((square, features), BF),
            jax.ShapeDtypeStruct((8, span, 2 * HD), BF),
        ],
        where,
        *d_pieces,
        out_weight,
    )
    d_heads = exchange(d_heads, ("z", "core")).reshape(row_len, 2 * HD)
    d_heads, high_own = tie(d_heads, highs[2])
    d_packed, d_mixed, mid_all, high = tie(
        *attend_back(split, q, k, v, out_heads, d_heads, logs, tables, local_len)[::-1],
        mid_all,
        shift(high_own, 1),
    )
    highs.append(high)

    arrived = exchange(d_packed.reshape(4, row_len // 4, 6 * HD), "z")
    d_mixed = d_mixed.reshape(row_len * row_count, 4 * HD)
    head_grad = dot_cols(in_all, d_mixed)[:, : 3 * HD].astype(BF)
    cut = shard // 2
    head_grad = head_grad.reshape(4, 2, cut, 3 * HD)
    mine = lax.dynamic_index_in_dim(head_grad, core, 1, keepdims=False)
    theirs = swap(lax.dynamic_index_in_dim(head_grad, 1 - core, 1, keepdims=False), 4)
    first, second = jnp.where(core == 0, mine, theirs), jnp.where(core == 0, theirs, mine)
    pairs = jnp.concatenate(
        [half[:, :, p * HD : (p + 1) * HD] for p in range(3) for half in (first, second)], axis=2
    )
    down = lax.dynamic_slice_in_dim(down_weight, hidden_first, width, 0)
    result_sum = sum_plane(
        dot(act_near.reshape(4 * tokens, width), down).reshape(4, tokens, features),
        dot(act_far.reshape(4 * tokens, width), down).astype(BF).reshape(4, tokens, features),
    )

    def rest(steps, before):
        outs = [
            piece for n in steps for piece in (lows[n], highs[n], swap(lows[n], 4), swap(highs[n], 4))
        ]
        return hidden_layer(where, [mid_all], outs, hidden_weights, total, steps, before)[0]

    hidden_all = rest((1, 2), hidden_all)
    arrived, result_sum, pairs, att, d_branch, picked, *hidden_all = tie(
        arrived, result_sum, pairs, att, d_branch, picked, *hidden_all
    )
    result = middle + result_sum

    pairs = [pick(pairs, rank ^ m) for m in range(4)]
    pairs = [pairs[0]] + [swap(pairs[m], m) for m in (1, 2, 3)]
    head_all = exchange(picked).reshape(features, 12 * HD)
    out_part = dot_cols(att, d_branch).astype(BF)
    out_part = lax.psum_scatter(out_part, ("z", "core"), scatter_dimension=0, tiled=True)
    act_all, d_gate_all, d_up_all, out_all = rest((3,), hidden_all)
    head_all, d_gate_grad, d_up_all, act_all, arrived, out_part, *pairs = tie(
        head_all, weight_grad(mid_all, d_gate_all), d_up_all, act_all, arrived, out_part, *pairs
    )

    by_chip = (4, shard, width)
    near, far = small_call(
        d_in_kernel,
        "d_in",
        [blocks] * 2,
        where,
        arrived,
        head_all,
        scratch=[
            pltpu.VMEM((8 * tokens, 12 * HD), BF),
            pltpu.VMEM((8 * tokens, 512), F32),
        ],
        limit=48,
    )
    heads = lax.all_gather(jnp.stack(pairs), "z", axis=0)
    gate_parts, d_up_grad, near, far, act_all = tie(
        exchange(d_gate_grad.reshape(by_chip)),
        weight_grad(mid_all, d_up_all),
        near,
        swap(far, 4),
        act_all,
    )
    d_norm_in, down_own, d_up_grad = tie(
        sum_quad([near[m].astype(F32) + far[m].astype(F32) for m in range(4)]),
        weight_grad(act_all, out_all),
        d_up_grad,
    )

    core_index = core.reshape(1).astype(jnp.int32)
    up_parts = exchange(d_up_grad.reshape(by_chip))
    out_rows = lax.all_gather(out_part, ("z", "core"), axis=0, tiled=True)
    gate_up_grad = place_columns(core_index, gate_parts, swap(gate_parts, 4), None, chip_width, 0)
    down_grad = place_down(core_index, down_own, swap(down_own, 4), chip_width)
    d_flat_part, d_gain_one, d_bias_one = norm1_back(d_norm_in)
    d_inputs = d_middle + d_flat_part
    bias_sum = jnp.sum(d_mixed.astype(F32), axis=0)
    bias_own = jnp.zeros((3 * features,), F32)
    for part in range(3):
        bias_own = lax.dynamic_update_slice_in_dim(
            bias_own, bias_sum[part * HD : (part + 1) * HD], head_first + part * features, 0
        )
    sums = jnp.concatenate([d_gain_one, d_bias_one, bias_own, d_gain_two, d_bias_two])
    sums = sums + swap(sums, 4)
    sums = sums + sum(shift(sums, n) for n in (1, 2, 3))
    qkv_grad = place_qkv(jnp.stack([core, rank]).astype(jnp.int32), heads, swap(heads, 4))
    up_parts, sums, gate_up_grad, down_grad, qkv_grad = tie(
        up_parts, sums, gate_up_grad, down_grad, qkv_grad
    )
    sums = sums + sum(swap(sums, m) for m in (1, 2, 3))
    out_grad = out_rows.astype(F32)
    gate_up_grad = place_columns(
        core_index, up_parts, swap(up_parts, 4), gate_up_grad, chip_width, 1
    )
    return (
        result.reshape(row_count, local_len, features),
        d_inputs.reshape(row_count, local_len, features),
        sums[:features],
        sums[features : 2 * features],
        qkv_grad,
        sums[2 * features : 5 * features],
        out_grad,
        sums[5 * features : 6 * features],
        sums[6 * features :],
        gate_up_grad,
        down_grad,
    )


def solution(mesh):
    planes = (mesh.shape["seq"], mesh.shape["fsdp"]) == (8, 4)
    plan = plane_plan if planes else general_plan
    if planes:
        mesh = jax.sharding.Mesh(mesh.devices.reshape(4, 2, 4), ("z", "core", "fsdp"))
    spread = P(None, (*mesh.axis_names,), None)
    placed = (
        spread,
        P(),
        P(),
        P(),
        P("fsdp", None),
        P(),
        P("fsdp", None),
        P(),
        P(),
        P("fsdp", None),
        P("fsdp", None),
        spread,
    )
    return jax.shard_map(
        plan,
        mesh=mesh,
        in_specs=placed,
        out_specs=(
            spread,
            spread,
            P(),
            P(),
            P("fsdp", None),
            P(),
            P("fsdp", None),
            P(),
            P(),
            P("fsdp", None),
            P("fsdp", None),
        ),
        check_vma=False,
    )
```
